512 devices in a mesh: bin: 32 (over y, x, core), pen: 16 (over z).
Axes of the slice: x: 4, y: 4, z: 16, core: 2. Of those that a mesh axis runs over, the one named last changes fastest.
Arguments:
- features: bfloat16 [1048576, 64], P(('bin', 'pen')), may hold values from -6 to 6
- positions: float32 [3, 1048576], P(None, ('bin', 'pen')), may hold values from 0 to 192, as said below
- home_cells: int32 [3, 1048576], P(None, ('bin', 'pen')), may hold values from 0 to 191, as said below
- neighbours: int32 [1048576, 16], P(('bin', 'pen')), may hold values from 0 to 26, as said below
- degrees: int32 [1048576], P(('bin', 'pen')), may hold values from 1 to 16
- lift_input: bfloat16 [64, 64], replicated, may hold values from -0.75 to 0.75
- kernel_first: float32 [3, 64], replicated, may hold values from -4 to 4
- kernel_bias: float32 [64], replicated, may hold values from -1 to 1
- kernel_second: bfloat16 [64, 64], replicated, may hold values from -0.75 to 0.75
- spectral_weights: bfloat16 [32, 32, 32, 64, 128], P(None, 'bin', 'pen'), may hold values from -6 to 6
- skip_weights: float32 [64, 64], replicated, may hold values from -0.75 to 0.75
- skip_bias: float32 [64], replicated, may hold values from -0.5 to 0.5
Outputs:
- latent_out: bfloat16 [128, 128, 192, 64], P('bin', 'pen')
The draws below stay inside these ranges and needn't reach their ends.
Inputs may be any that keep to these rules, and one draw needn't show every extreme that they name: `neighbours`: each code k names the step (k // 9 - 1, (k // 3) % 3 - 1, k % 3 - 1) of the 3 x 3 x 3 cells around a point's home cell; slot 0 is 13, the home cell itself, and the other slots hold distinct codes other than 13. `home_cells`: row 0 is below 4, row 1 below 8, row 2 below 192. `positions`: each point lies in its home cell: the integer parts of its coordinates are that cell's global coordinates.
All inputs are finite; a program needn't handle non-finite values.
Results may differ from the reference program's by a relative error of at most 0.0037.
Values sent between devices are 32-bit elements; how exact they have to be, the bound alone decides.
No kernel may reach another device: no remote copies, remote signals or barrier semaphores. Data moves between devices by JAX's collectives and lax.ppermute only.
A program may use at most 128 MiB of HBM per device.

```python
import math
import jax
import jax.numpy as jnp
import numpy as np
from jax import lax

FEAT = 64
CH = 64
HID = 64
MODES = 32
NZ = 192
DEG = 16
PTS = 2048
CX = 4
CY = 8
NX = 128
NY = 128
POINTS = 1048576
N_BIN = 32
N_PEN = 16


def point_cells(key):
    pens = NY // CY
    owner = jnp.arange(POINTS, dtype=jnp.int32) // PTS
    bin_of = owner // pens
    pen_of = owner % pens
    key_x, key_y, key_z = jax.random.split(key, 3)
    local_x = jax.random.randint(key_x, (POINTS,), 0, CX)
    local_y = jax.random.randint(key_y, (POINTS,), 0, CY)
    local_z = jax.random.randint(key_z, (POINTS,), 0, NZ)
    local_x = local_x.at[0].set(0).at[POINTS - 1].set(CX - 1)
    local_y = local_y.at[0].set(0).at[POINTS - 1].set(CY - 1)
    local_z = local_z.at[0].set(0).at[POINTS - 1].set(NZ - 1)
    return (bin_of * CX + local_x, pen_of * CY + local_y, local_z, local_x, local_y)


def draw_positions(key, part):
    cell_x, cell_y, cell_z, local_x, local_y = point_cells(key)
    key = jax.random.fold_in(key, 11)
    fraction = jax.random.uniform(key, (3, POINTS), jnp.float32, 0.0, 0.999)
    cells = jnp.stack([cell_x, cell_y, cell_z]).astype(jnp.float32)
    return cells + fraction


def draw_home_cells(key, part):
    cell_x, cell_y, cell_z, local_x, local_y = point_cells(key)
    return jnp.stack([local_x, local_y, cell_z]).astype(jnp.int32)


def draw_neighbours(key, part):
    key = jax.random.fold_in(key, 12)
    scores = jax.random.randint(key, (POINTS, 26), 0, 1 << 20) * 32 + jnp.arange(26, dtype=jnp.int32)[None, :]
    order = jnp.argsort(scores, axis=1)[:, :DEG - 1]
    codes_table = jnp.asarray(np.array([k for k in range(27) if k != 13], dtype=np.int32))
    codes = codes_table[order]
    codes = jnp.concatenate([jnp.full((POINTS, 1), 13, jnp.int32), codes], axis=1)
    return codes.astype(jnp.int32)


def draw_degrees(key, part):
    key = jax.random.fold_in(key, 13)
    values = jax.random.randint(key, (POINTS,), 1, DEG + 1)
    values = values.at[1::PTS].set(1)
    return values.at[::PTS].set(DEG).astype(jnp.int32)


def block_scale(key, extent, shards, least, largest):
    factor_of = 1.0
    for position, blocks in shards:
        steps = jax.random.uniform(jax.random.fold_in(jax.random.fold_in(key, 6), position), (blocks,), jnp.float32, least / len(shards), largest / len(shards))
        factor_of = factor_of * jnp.repeat(jnp.exp(steps), extent[position] // blocks).reshape((-1,) + (1,) * (len(extent) - 1 - position))
    return factor_of


def centred(rng, extent, spread, limit, cuts=(), kind=jnp.bfloat16):
    values = jax.random.normal(rng, extent, jnp.float32) * spread
    if len(cuts) > 0:
        values = block_scale(rng, extent, cuts, -0.22, 0.18) * values
    return jnp.clip(values, min=-limit, max=limit).astype(kind)


def setup_inputs(seed: int = 0) -> dict:
    streams_of = jax.random.split(jax.random.key(seed), 13)
    return {
        "features": centred(streams_of[0], (POINTS, FEAT), 1.0, 6.0, ((0, 512),)),
        "positions": draw_positions(jax.random.fold_in(streams_of[12], 71), 0),
        "home_cells": draw_home_cells(jax.random.fold_in(streams_of[12], 71), 0),
        "neighbours": draw_neighbours(jax.random.fold_in(streams_of[12], 71), 0),
        "degrees": draw_degrees(jax.random.fold_in(streams_of[12], 71), 0),
        "lift_input": centred(streams_of[5], (FEAT, CH), FEAT ** -0.5, 0.75),
        "kernel_first": centred(streams_of[6], (3, HID), 1.0, 4.0, (), jnp.float32),
        "kernel_bias": jnp.clip(jax.random.uniform(streams_of[7], (HID,), jnp.float32, -1.0, 1.0), -1.0, 1.0),
        "kernel_second": centred(streams_of[8], (HID, CH), HID ** -0.5, 0.75),
        "spectral_weights": centred(streams_of[9], (MODES, MODES, MODES, CH, 2 * CH), (max(1, 2 * CH * MODES ** 3 // (NX * NY * NZ))) ** -0.5, 6.0, ((1, 32), (2, 16))),
        "skip_weights": centred(streams_of[10], (CH, CH), CH ** -0.5, 0.75, (), jnp.float32),
        "skip_bias": jnp.clip(jax.random.uniform(streams_of[11], (CH,), jnp.float32, -0.5, 0.5), -0.5, 0.5),
    }


def dft_table(rows, length, count, signed):
    mode = jnp.arange(count, dtype=jnp.int32)
    if signed:
        mode = jnp.where(mode < count // 2, mode, mode - count)
    phase = rows.astype(jnp.int32)[:, None] * mode[None, :] % length
    angle = phase.astype(jnp.float32) * (2.0 * math.pi / length)
    scale = 1.0 / math.sqrt(length)
    return (jnp.cos(angle) * scale, jnp.sin(angle) * scale)

def pair_messages(off_x, off_y, off_z, feat_rows, valid, kernel_first, kernel_bias, kernel_second, lift_input):
    pre = off_x[..., None] * kernel_first[0] + off_y[..., None] * kernel_first[1] + off_z[..., None] * kernel_first[2] + kernel_bias
    hidden = jax.nn.gelu(pre).astype(jnp.bfloat16)
    count, slots_n, width = hidden.shape
    kernel = jnp.dot(hidden.reshape(count * slots_n, width), kernel_second, preferred_element_type=jnp.float32)
    kernel = kernel.reshape(count, slots_n, -1)
    values = jnp.dot(feat_rows, lift_input, preferred_element_type=jnp.float32)
    return kernel * values[:, None, :] * valid[..., None]

def reference(features, positions, home_cells, neighbours, degrees, lift_input, kernel_first, kernel_bias, kernel_second, spectral_weights, skip_weights, skip_bias):
    high = lax.Precision.HIGHEST
    slots = jnp.arange(DEG, dtype=jnp.int32)[None, :]

    def one_device(index, grid):
        index = index.astype(jnp.int32)
        start = (index * PTS).astype(jnp.int32)
        codes = lax.dynamic_slice_in_dim(neighbours, start, PTS, 0)
        feat_rows = lax.dynamic_slice_in_dim(features, start, PTS, 0)
        where = lax.dynamic_slice_in_dim(positions, start, PTS, 1)
        home = lax.dynamic_slice_in_dim(home_cells, start, PTS, 1)
        live = lax.dynamic_slice_in_dim(degrees, start, PTS, 0)
        bin_of = index // N_PEN
        pen_of = index % N_PEN
        cell_x = jnp.clip(bin_of * CX + home[0][:, None] + codes // 9 - 1, 0, NX - 1)
        cell_y = jnp.clip(pen_of * CY + home[1][:, None] + codes // 3 % 3 - 1, 0, NY - 1)
        cell_z = jnp.clip(home[2][:, None] + codes % 3 - 1, 0, NZ - 1)
        off_x = cell_x.astype(jnp.float32) + 0.5 - where[0][:, None]
        off_y = cell_y.astype(jnp.float32) + 0.5 - where[1][:, None]
        off_z = cell_z.astype(jnp.float32) + 0.5 - where[2][:, None]
        valid = (slots < live[:, None]).astype(jnp.float32)
        message = pair_messages(off_x, off_y, off_z, feat_rows, valid, kernel_first, kernel_bias, kernel_second, lift_input)
        ids = ((cell_x * NY + cell_y) * NZ + cell_z).astype(jnp.int32)
        return grid.at[ids.reshape(-1)].add(message.reshape(-1, CH))
    grid = lax.fori_loop(0, N_BIN * N_PEN, one_device, jnp.zeros((NX * NY * NZ, CH), jnp.float32))
    latent = grid.reshape(NX, NY, NZ, CH)
    cos_z, sin_z = dft_table(jnp.arange(NZ, dtype=jnp.int32), NZ, MODES, False)
    cos_y, sin_y = dft_table(jnp.arange(NY, dtype=jnp.int32), NY, MODES, True)
    cos_x, sin_x = dft_table(jnp.arange(NX, dtype=jnp.int32), NX, MODES, True)

    def forward_z(slab):
        real = jnp.einsum('yzc,zk->ykc', slab, cos_z, precision=high)
        imag = -jnp.einsum('yzc,zk->ykc', slab, sin_z, precision=high)
        return (real, imag)
    z_re, z_im = lax.map(forward_z, latent)
    y_re = jnp.einsum('xykc,yj->xjkc', z_re, cos_y, precision=high) + jnp.einsum('xykc,yj->xjkc', z_im, sin_y, precision=high)
    y_im = jnp.einsum('xykc,yj->xjkc', z_im, cos_y, precision=high) - jnp.einsum('xykc,yj->xjkc', z_re, sin_y, precision=high)
    x_re = jnp.einsum('xykc,xj->jykc', y_re, cos_x, precision=high) + jnp.einsum('xykc,xj->jykc', y_im, sin_x, precision=high)
    x_im = jnp.einsum('xykc,xj->jykc', y_im, cos_x, precision=high) - jnp.einsum('xykc,xj->jykc', y_re, sin_x, precision=high)
    weights = spectral_weights.astype(jnp.float32)
    real_w = jnp.einsum('abki,abkio->abko', x_re, weights, precision=high)
    imag_w = jnp.einsum('abki,abkio->abko', x_im, weights, precision=high)
    mix_re = real_w[..., :CH] - imag_w[..., CH:]
    mix_im = real_w[..., CH:] + imag_w[..., :CH]
    bx_re = jnp.einsum('jykc,xj->xykc', mix_re, cos_x, precision=high) - jnp.einsum('jykc,xj->xykc', mix_im, sin_x, precision=high)
    bx_im = jnp.einsum('jykc,xj->xykc', mix_im, cos_x, precision=high) + jnp.einsum('jykc,xj->xykc', mix_re, sin_x, precision=high)
    by_re = jnp.einsum('xjkc,yj->xykc', bx_re, cos_y, precision=high) - jnp.einsum('xjkc,yj->xykc', bx_im, sin_y, precision=high)
    by_im = jnp.einsum('xjkc,yj->xykc', bx_im, cos_y, precision=high) + jnp.einsum('xjkc,yj->xykc', bx_re, sin_y, precision=high)
    doubling = jnp.where(jnp.arange(MODES) == 0, 1.0, 2.0).astype(jnp.float32)[:, None]

    def finish(pieces):
        slab, part_re, part_im = pieces
        spectral_part = jnp.einsum('ykc,zk->yzc', part_re * doubling, cos_z, precision=high) - jnp.einsum('ykc,zk->yzc', part_im * doubling, sin_z, precision=high)
        skip = jnp.einsum('yzc,cd->yzd', slab, skip_weights, precision=high)
        return jax.nn.gelu(spectral_part + skip + skip_bias).astype(jnp.bfloat16)
    return lax.map(finish, (latent, by_re, by_im))
```

```python
import functools
import math

import jax
import jax.numpy as jnp
import numpy as np
from jax import lax
from jax.experimental import pallas as pl
from jax.experimental.pallas import tpu as pltpu
from jax.sharding import PartitionSpec as P

NZ = 192
CX = 4
CY = 8
PTS = 2048
CH = 64
MODES = 32
CHUNK = 256
SUB = 128
HALVES = 2 * CH

F32 = jnp.float32
BF16 = jnp.bfloat16
HIGH = lax.Precision.HIGHEST
LIMIT = pltpu.CompilerParams(vmem_limit_bytes=48 * 1024 * 1024)

NN = (((1,), (0,)), ((), ()))
NT = (((1,), (1,)), ((), ()))
TN = (((0,), (0,)), ((), ()))


def mm(a, b, dims=NN, precision=None):
    return lax.dot_general(a, b, dims, precision=precision, preferred_element_type=F32)


def gelu(x):
    inner = x * (0.7978845608028654 + 0.035677408136300125 * (x * x))
    half = 0.5 * x
    return half + half * jnp.tanh(inner)


def swap(x):
    return pltpu.roll(x, CH, 1)


def sign_row(shape):
    lane = lax.broadcasted_iota(jnp.int32, shape, 1)
    return jnp.where(lane < CH, 1.0, -1.0).astype(F32)


def tables(length, signed):
    mode = np.arange(MODES)
    if signed:
        mode = np.where(mode < MODES // 2, mode, mode - MODES)
    return mode


def angles(rows, length, signed):
    mode = tables(length, signed)
    phase = (np.asarray(rows)[:, None] * mode[None, :]) % length
    angle = phase * (2.0 * math.pi / length)
    scale = 1.0 / math.sqrt(length)
    return np.cos(angle) * scale, np.sin(angle) * scale


def z_forward_table():
    c, s = angles(np.arange(NZ), NZ, False)
    return np.concatenate([c.T, -s.T], axis=0).astype(np.float32)


def z_inverse_table():
    c, s = angles(np.arange(NZ), NZ, False)
    w = np.where(np.arange(MODES) == 0, 1.0, 2.0)[:, None]
    return np.concatenate([c.T * w, -s.T * w], axis=0).astype(np.float32)


def y_forward_tables(pens):
    length = CY * pens
    c, s = angles(np.arange(length), length, True)
    main = np.concatenate([c.T, s.T], axis=0)
    side = np.zeros((CX, 2, MODES, pens, CX, 2))
    for q in range(pens):
        for h in range(2):
            y = min(max(q * CY - 1 + h * (CY + 1), 0), length - 1)
            for x in range(CX):
                side[x, 0, :, q, x, h] = c[y]
                side[x, 1, :, q, x, h] = s[y]
    side = side.reshape(CX * 2 * MODES, pens * CX * 2)
    return main.astype(np.float32), side.astype(np.float32)


def y_inverse_table(pens):
    length = CY * pens
    c, s = angles(np.arange(length), length, True)
    return np.concatenate([c, s], axis=0).astype(np.float32)


def x_tables(bins):
    length = CX * bins
    c, s = angles(np.arange(length), length, True)
    fwd = np.zeros((2, 2, MODES, bins, 2, CX))
    inv = np.zeros((2, bins, 2, CX, 2, MODES))
    for k in range(2):
        fwd[0, k, :, :, k, :] = c.T.reshape(MODES, bins, CX)
        fwd[1, k, :, :, k, :] = s.T.reshape(MODES, bins, CX)
        inv[0, :, k, :, k, :] = c.reshape(bins, CX, MODES)
        inv[1, :, k, :, k, :] = s.reshape(bins, CX, MODES)
    fwd = fwd.reshape(4 * MODES, bins * 2 * CX)
    inv = inv.reshape(2 * bins * 2 * CX, 2 * MODES)
    return fwd.astype(np.float32), inv.astype(np.float32)


def pieces(x):
    hi = x.astype(BF16).astype(F32)
    rest = x - hi
    mid = rest.astype(BF16).astype(F32)
    return hi, mid, rest - mid


def lift_kernel(last, at, feat, pos, home, nbr, deg, lift, first, bias, second, tabz,
                own, ysides, xsides, spec, edge, grid, rank, data, mess):
    bin_index = at[0]
    pen_index = at[1]
    last_bin, last_pen = last
    hx = home[0:1, :]
    hy = home[1:2, :]
    hz = home[2:3, :]
    col = hx * CY + hy

    ids = lax.broadcasted_iota(jnp.int32, (CX * CY, PTS), 0)
    carry = jnp.sum(jnp.where(col < ids, 1.0, 0.0), axis=1, keepdims=True)
    tri = jnp.where(
        lax.broadcasted_iota(jnp.int32, (CHUNK, CHUNK), 0)
        < lax.broadcasted_iota(jnp.int32, (CHUNK, CHUNK), 1), 1.0, 0.0).astype(BF16)
    for blk in range(PTS // CHUNK):
        part = slice(blk * CHUNK, (blk + 1) * CHUNK)
        hot = jnp.where(col[:, part] == ids[:, part], 1.0, 0.0)
        ahead = mm(hot.astype(BF16), tri) + carry
        rank[0:1, part] = jnp.sum(hot * ahead, axis=0, keepdims=True).astype(jnp.int32)
        carry = carry + jnp.sum(hot, axis=1, keepdims=True)

    slot = lax.broadcasted_iota(jnp.int32, (16, PTS), 0)
    bits = jnp.sum(
        jnp.where(slot < deg[...], jnp.left_shift(1, nbr[...]), 0), axis=0, keepdims=True)
    code = lax.broadcasted_iota(jnp.int32, (32, PTS), 0)
    live = jnp.bitwise_and(jnp.right_shift(bits, code), 1).astype(F32)
    off_x = (hx + bin_index * CX).astype(F32) + 0.5 - pos[0:1, :]
    off_y = (hy + pen_index * CY).astype(F32) + 0.5 - pos[1:2, :]
    off_z = hz.astype(F32) + 0.5 - pos[2:3, :]
    rows = [*pieces(off_x), *pieces(off_y), *pieces(off_z), hz.astype(F32), col.astype(F32),
            jnp.zeros((5, PTS), F32)]
    data[0:64, :] = feat[...]
    data[64:80, :] = jnp.concatenate(rows, axis=0).astype(BF16)
    data[80:112, :] = live.astype(BF16)

    grid[...] = jnp.zeros_like(grid)

    taps = jnp.concatenate([first[...], bias[...], jnp.zeros((4, CH), F32)], axis=0)
    taps = jnp.concatenate([taps, jnp.zeros((8, 128 - CH), F32)], axis=1)
    taps = jnp.transpose(taps)
    k_x, k_y, k_z, k_b = (
        jnp.broadcast_to(taps[0:CH, j:j + 1], (CH, CHUNK)) for j in range(4))
    zero = jnp.zeros((CH, CH), F32)
    sec_t = jnp.transpose(second[...].astype(F32))
    quad = jnp.concatenate(
        [jnp.concatenate([sec_t if i == j else zero for j in range(4)], axis=1)
         for i in range(4)], axis=0).astype(BF16)
    lift_t = jnp.transpose(lift[...].astype(F32)).astype(BF16)
    z_ids = lax.broadcasted_iota(jnp.int32, (NZ, SUB), 0)

    def chunk(step, _):
        base = step * CHUNK
        want = lax.broadcasted_iota(jnp.int32, (CHUNK, PTS), 0) + base
        perm = jnp.where(rank[0:1, :] == want, 1.0, 0.0).astype(BF16)
        t = mm(data[...], perm, NT)
        values = mm(lift_t, t[0:64].astype(BF16))
        ox = t[64:65] + t[65:66] + t[66:67]
        oy = t[67:68] + t[68:69] + t[69:70]
        oz = t[70:71] + t[71:72] + t[72:73]
        hzs = t[73:74].astype(jnp.int32)
        cols = t[74:75].astype(jnp.int32)
        hxs = lax.shift_right_logical(cols, 3) + bin_index * CX
        hys = jnp.bitwise_and(cols, 7) + pen_index * CY

        def ends(g, last):
            return (jnp.where(g > 0, -1.0, 0.0), None, jnp.where(g < last, 1.0, 0.0))

        base_pre = k_x * ox + k_y * oy + k_z * oz + k_b
        ex = ends(hxs, last_bin)
        ey = ends(hys, last_pen)
        ez = ends(hzs, NZ - 1)
        pend = []

        def flush():
            while len(pend) < 4:
                pend.append((None, jnp.zeros((CH, CHUNK), BF16)))
            hid4 = jnp.concatenate([h for _, h in pend], axis=0)
            kern = mm(quad, hid4)
            for j, (where, _) in enumerate(pend):
                if where is None:
                    continue
                dx, dy, dz = where
                k = dx * 9 + dy * 3 + dz
                m = kern[j * CH:(j + 1) * CH] * (values * t[80 + k:81 + k])
                hi = m.astype(BF16)
                lo = (m - hi.astype(F32)).astype(BF16)
                r = (dx * 3 + dy) * CH
                for s in range(CHUNK // SUB):
                    cut = slice(s * SUB, (s + 1) * SUB)
                    mess[s, r:r + CH, dz * SUB:(dz + 1) * SUB] = hi[:, cut]
                    mess[s, r:r + CH, (3 + dz) * SUB:(4 + dz) * SUB] = lo[:, cut]
            pend.clear()

        for dx in range(3):
            pre_x = base_pre if ex[dx] is None else base_pre + ex[dx] * k_x
            for dy in range(3):
                pre_y = pre_x if ey[dy] is None else pre_x + ey[dy] * k_y
                for dz in range(3):
                    pre = pre_y if ez[dz] is None else pre_y + ez[dz] * k_z
                    pend.append(((dx, dy, dz), gelu(pre).astype(BF16)))
                    if len(pend) == 4:
                        flush()
        flush()

        for s in range(CHUNK // SUB):
            cut = slice(s * SUB, (s + 1) * SUB)
            c_row = cols[:, cut]
            h_row = hzs[:, cut]
            zs = (jnp.maximum(h_row - 1, 0), h_row, jnp.minimum(h_row + 1, NZ - 1))

            def column(c, _):
                mine = c_row == c
                hot = jnp.concatenate(
                    [jnp.where(z_ids == jnp.where(mine, z, -1), 1.0, 0.0).astype(BF16)
                     for z in zs], axis=1)
                hot = jnp.concatenate([hot, hot], axis=1)
                acc = mm(mess[s], hot, NT)
                cx = lax.shift_right_logical(c, 3)
                cy = jnp.bitwise_and(c, 7)
                for dx in range(3):
                    for dy in range(3):
                        r = (dx * 3 + dy) * CH
                        grid[cx + dx, cy + dy] += acc[r:r + CH]
                return 0

            lax.fori_loop(jnp.min(c_row), jnp.max(c_row) + 1, column, 0)
        return 0

    lax.fori_loop(0, PTS // CHUNK, chunk, 0)

    lane = lax.broadcasted_iota(jnp.int32, (MODES, HALVES), 1)
    table = tabz[...]
    for xi in range(CX + 2):
        for yp in range((CY + 2) // 2):
            pair = grid[xi, 2 * yp:2 * yp + 2].reshape(2 * CH, NZ)
            d = mm(table, pair, NT, HIGH)
            re, im = d[0:MODES], d[MODES:]
            out = (jnp.where(lane < CH, re, swap(im)), jnp.where(lane < CH, swap(re), im))
            for j in range(2):
                yi = 2 * yp + j
                row = CY if yi == 0 else (CY + 1 if yi == CY + 1 else yi - 1)
                if xi in (0, CX + 1):
                    e = 0 if xi == 0 else 1
                    edge[e, :, row, :] = out[j]
                    xsides[e, row] = grid[xi, yi]
                else:
                    x = xi - 1
                    if row < CY:
                        spec[:, x * CY + row, :] = out[j]
                        own[x * CY + row] = grid[xi, yi]
                    else:
                        spec[:, CX * CY + x * 2 + row - CY, :] = out[j]
                        ysides[row - CY, x] = grid[xi, yi]


def lift_points(at, last, feat, pos, home, nbr, deg, lift, first, bias, second):
    shapes = [
        jax.ShapeDtypeStruct((CX * CY, CH, NZ), F32),
        jax.ShapeDtypeStruct((2, CX, CH, NZ), F32),
        jax.ShapeDtypeStruct((2, CY + 2, CH, NZ), F32),
        jax.ShapeDtypeStruct((MODES, CX * (CY + 2), HALVES), F32),
        jax.ShapeDtypeStruct((2, MODES, CY + 2, HALVES), F32),
    ]
    return pl.pallas_call(
        functools.partial(lift_kernel, last),
        out_shape=shapes,
        in_specs=[pl.BlockSpec(memory_space=pltpu.SMEM)]
        + [pl.BlockSpec(memory_space=pltpu.VMEM)] * 10,
        out_specs=[pl.BlockSpec(memory_space=pltpu.VMEM)] * 5,
        scratch_shapes=[
            pltpu.VMEM((CX + 2, CY + 2, CH, NZ), F32),
            pltpu.VMEM((8, PTS), jnp.int32),
            pltpu.VMEM((112, PTS), BF16),
            pltpu.VMEM((CHUNK // SUB, 9 * CH, 6 * SUB), BF16),
        ],
        compiler_params=LIMIT,
        name="lift",
    )(at, feat, pos, home, nbr, deg, lift, first, bias, second, jnp.asarray(z_forward_table()))


def join_kernel(last, at, spec, edge, below, above, out):
    low = at[0] == 0
    top = at[0] == last
    n = CX * CY
    b = jnp.where(low, edge[0], below[...])
    a = jnp.where(top, edge[1], above[...])
    out[...] = spec[...]
    out[:, 0:CY] += b[:, 0:CY]
    out[:, n - CY:n] += a[:, 0:CY]
    out[:, n:n + 2] += b[:, CY:]
    out[:, n + 2 * CX - 2:n + 2 * CX] += a[:, CY:]


def y_kernel(last, at, r, main, side, ysides, xsides, below, above, out, yedge):
    sgn = sign_row((MODES, HALVES))
    n = CX * CY
    pens = r.shape[0]
    for kz in range(2):
        o = kz * (n + 2 * CX)
        halo = mm(side[...], r[:, o + n:o + n + 2 * CX, :].reshape(pens * 2 * CX, HALVES), NN, HIGH)
        for x in range(CX):
            rows = r[:, o + x * CY:o + (x + 1) * CY, :].reshape(pens * CY, HALVES)
            ab = mm(main[...], rows, NN, HIGH) + halo[x * 2 * MODES:(x + 1) * 2 * MODES]
            out[:, kz * CX + x, :] = ab[:MODES] + swap(ab[MODES:]) * sgn
    low = at[0] == 0
    top = at[0] == last
    yedge[...] = ysides[...]
    for h in range(2):
        yedge[h, 0] += jnp.where(low, xsides[0, CY + h], below[CY + h])
        yedge[h, CX - 1] += jnp.where(top, xsides[1, CY + h], above[CY + h])


def x_kernel(r, fwd, inv, w, out, lhs, res):
    rows = r.shape[0] * r.shape[1]
    modes = 2 * MODES
    sgn = sign_row((modes, HALVES))
    ab = mm(fwd[...], r[...].reshape(rows, HALVES), NN, HIGH)
    x = ab[:modes] + swap(ab[modes:]) * sgn
    parts = [*pieces(x), *pieces(swap(x))]
    lhs[...] = jnp.zeros_like(lhs)
    for j, p in enumerate(parts):
        lhs[:, j, :] = p
    for k in range(2):
        for j in range(MODES):
            m = k * MODES + j
            res[m] = mm(lhs[m][:, 0:CH].astype(BF16), w[j, 0, k])
    re = res[:, 0, :] + res[:, 1, :] + res[:, 2, :]
    im = res[:, 3, :] + res[:, 4, :] + res[:, 5, :]
    mixed = re - swap(im) * sgn
    ab = mm(inv[...], mixed, NN, HIGH)
    a, b = ab[:rows], ab[rows:]
    y = a - swap(b) * sign_row((rows, HALVES))
    out[...] = y.reshape(out.shape)


def y_back_kernel(r, inv, out):
    rows = inv.shape[0] // 2
    sgn = sign_row((rows, HALVES))
    for i in range(2 * CX):
        ab = mm(inv[...], r[:, i, :], NN, HIGH)
        y = ab[:rows] - swap(ab[rows:]) * sgn
        out[:, i * CY:(i + 1) * CY, :] = y.reshape(rows // CY, CY, HALVES)


def final_kernel(last, at, zb, tab, own, xsides, below, above, yedge, left, right, skip, bias, out):
    low = at[0] == 0
    top = at[0] == last[0]
    first_pen = at[1] == 0
    last_pen = at[1] == last[1]
    lane = lax.broadcasted_iota(jnp.int32, (MODES, HALVES), 1)
    zero = jnp.zeros((CH, CH), F32)
    skip_t = jnp.transpose(skip[...])
    pair = jnp.concatenate(
        [jnp.concatenate([skip_t, zero], axis=1), jnp.concatenate([zero, skip_t], axis=1)], axis=0)
    col = jnp.concatenate([bias[...], bias[...]], axis=1)
    col = jnp.transpose(jnp.broadcast_to(col, (8, HALVES)))
    col = jnp.broadcast_to(col[:, 0:1], (HALVES, NZ))
    for x in range(CX):
        for yp in range(CY // 2):
            i = x * CY + 2 * yp
            u = zb[:, i, :]
            v = zb[:, i + 1, :]
            s = jnp.concatenate(
                [jnp.where(lane < CH, u, swap(v)), jnp.where(lane < CH, swap(u), v)], axis=0)
            spectral = mm(s, tab[...], TN, HIGH)
            lat = []
            for j in range(2):
                y = 2 * yp + j
                l = own[i + j]
                if x == 0:
                    l = l + jnp.where(low, xsides[0, y], below[y])
                if x == CX - 1:
                    l = l + jnp.where(top, xsides[1, y], above[y])
                if y == 0:
                    l = l + jnp.where(first_pen, yedge[0, x], left[x])
                if y == CY - 1:
                    l = l + jnp.where(last_pen, yedge[1, x], right[x])
                lat.append(l)
            total = spectral + mm(pair, jnp.concatenate(lat, axis=0), NN, HIGH) + col
            out[x, 2 * yp:2 * yp + 2] = gelu(total).astype(BF16).reshape(2, CH, NZ)


def call(kernel, shapes, args, scratch=(), smem=False, name=None):
    specs = [pl.BlockSpec(memory_space=pltpu.VMEM)] * len(args)
    if smem:
        specs[0] = pl.BlockSpec(memory_space=pltpu.SMEM)
    return pl.pallas_call(
        kernel,
        out_shape=shapes,
        in_specs=specs,
        scratch_shapes=list(scratch),
        compiler_params=LIMIT,
        name=name,
    )(*args)


def shape(*dims):
    return jax.ShapeDtypeStruct(dims, F32)


def exchange(x, axis):
    return lax.all_to_all(x, axis, split_axis=0, concat_axis=0, tiled=True)


def moved(x, axis, step):
    devices = range(lax.axis_size(axis))
    return lax.ppermute(x, axis, [(i - step, i) for i in devices if i - step in devices])


def per_device(features, positions, home_cells, neighbours, degrees, lift_input, kernel_first,
               kernel_bias, kernel_second, spectral_weights, skip_weights, skip_bias):
    bins = lax.axis_size("bin")
    pens = lax.axis_size("pen")
    at = jnp.stack([lax.axis_index("bin"), lax.axis_index("pen")]).astype(jnp.int32)
    own, ysides, xsides, spec, edge = lift_points(
        at, (bins * CX - 1, pens * CY - 1), features.T, positions, home_cells, neighbours.T,
        degrees[None, :], lift_input, kernel_first, kernel_bias[None, :], kernel_second)
    edge_below = moved(edge[1], "bin", 1)
    edge_above = moved(edge[0], "bin", -1)
    below = moved(xsides[1], "bin", 1)
    above = moved(xsides[0], "bin", -1)
    spec = call(functools.partial(join_kernel, bins - 1), shape(*spec.shape),
                (at, spec, edge, edge_below, edge_above), smem=True, name="join")
    rows = 2 * CX * (CY + 2)
    r = exchange(spec.reshape(pens, rows, HALVES), "pen")
    main, side = y_forward_tables(pens)
    r, yedge = call(
        functools.partial(y_kernel, bins - 1),
        [shape(MODES, 2 * CX, HALVES), shape(*ysides.shape)],
        (at, r, jnp.asarray(main), jnp.asarray(side), ysides, xsides, below, above),
        smem=True, name="forward_y")
    left = moved(yedge[1], "pen", 1)
    right = moved(yedge[0], "pen", -1)
    r = exchange(r, "bin")
    fwd, inv = x_tables(bins)
    r = call(x_kernel, shape(MODES, 2 * CX, HALVES),
             (r, jnp.asarray(fwd), jnp.asarray(inv), spectral_weights),
             scratch=[pltpu.VMEM((2 * MODES, 8, HALVES), F32)] * 2, name="mix_x")
    r = exchange(r, "bin")
    r = call(y_back_kernel, shape(pens, 2 * CX * CY, HALVES),
             (r, jnp.asarray(y_inverse_table(pens))), name="inverse_y")
    r = exchange(r, "pen")
    out = call(
        functools.partial(final_kernel, (bins - 1, pens - 1)),
        jax.ShapeDtypeStruct((CX, CY, CH, NZ), BF16),
        (at, r.reshape(MODES, CX * CY, HALVES), jnp.asarray(z_inverse_table()), own, xsides,
         below, above, yedge, left, right, skip_weights, skip_bias[None, :]),
        smem=True, name="finish")
    return out.transpose(0, 1, 3, 2)


def solution(mesh):
    in_specs = (
        P(("bin", "pen"), None),
        P(None, ("bin", "pen")),
        P(None, ("bin", "pen")),
        P(("bin", "pen"), None),
        P(("bin", "pen")),
        P(),
        P(),
        P(),
        P(),
        P(None, "bin", "pen", None, None),
        P(),
        P(),
    )
    out_specs = P("bin", "pen", None, None)
    return jax.shard_map(
        per_device, mesh=mesh, in_specs=in_specs, out_specs=out_specs, check_vma=False
    )
```

```python
import functools
import math

import jax
import jax.numpy as jnp
import numpy as np
from jax import lax
from jax.experimental import pallas as pl
from jax.experimental.pallas import tpu as pltpu
from jax.sharding import PartitionSpec as P

NZ = 192
CX = 4
CY = 8
PTS = 2048
CH = 64
MODES = 32
CHUNK = 256
SUB = 128
HALVES = 2 * CH

F32 = jnp.float32
BF16 = jnp.bfloat16
HIGH = lax.Precision.HIGH
LIMIT = pltpu.CompilerParams(vmem_limit_bytes=32 * 1024 * 1024)

NN = (((1,), (0,)), ((), ()))
NT = (((1,), (1,)), ((), ()))
TN = (((0,), (0,)), ((), ()))


def mm(a, b, dims=NN, precision=None):
    return lax.dot_general(a, b, dims, precision=precision, preferred_element_type=F32)


def gelu(x):
    inner = x * (0.7978845608028654 + 0.035677408136300125 * (x * x))
    half = 0.5 * x
    return half + half * jnp.tanh(inner)


def swap(x):
    return pltpu.roll(x, CH, 1)


def sign_row(shape):
    lane = lax.broadcasted_iota(jnp.int32, shape, 1)
    return jnp.where(lane < CH, 1.0, -1.0).astype(F32)


def tables(length, signed):
    mode = np.arange(MODES)
    if signed:
        mode = np.where(mode < MODES // 2, mode, mode - MODES)
    return mode


def angles(rows, length, signed):
    mode = tables(length, signed)
    phase = (np.asarray(rows)[:, None] * mode[None, :]) % length
    angle = phase * (2.0 * math.pi / length)
    scale = 1.0 / math.sqrt(length)
    return np.cos(angle) * scale, np.sin(angle) * scale


def z_forward_table():
    c, s = angles(np.arange(NZ), NZ, False)
    return np.concatenate([c.T, -s.T], axis=0).astype(np.float32)


def z_inverse_table():
    c, s = angles(np.arange(NZ), NZ, False)
    w = np.where(np.arange(MODES) == 0, 1.0, 2.0)[:, None]
    return np.concatenate([c.T * w, -s.T * w], axis=0).astype(np.float32)


def y_forward_tables(pens):
    length = CY * pens
    c, s = angles(np.arange(length), length, True)
    main = np.concatenate([c.T, s.T], axis=0)
    side = np.zeros((CX, 2, MODES, pens, CX, 2))
    for q in range(pens):
        for h in range(2):
            y = min(max(q * CY - 1 + h * (CY + 1), 0), length - 1)
            for x in range(CX):
                side[x, 0, :, q, x, h] = c[y]
                side[x, 1, :, q, x, h] = s[y]
    side = side.reshape(CX * 2 * MODES, pens * CX * 2)
    return main.astype(np.float32), side.astype(np.float32)


def y_inverse_table(pens):
    length = CY * pens
    c, s = angles(np.arange(length), length, True)
    return np.concatenate([c, s], axis=0).astype(np.float32)


def x_tables(bins):
    length = CX * bins
    c, s = angles(np.arange(length), length, True)
    fwd = np.zeros((2, 2, MODES, bins, 2, CX))
    inv = np.zeros((2, bins, 2, CX, 2, MODES))
    for k in range(2):
        fwd[0, k, :, :, k, :] = c.T.reshape(MODES, bins, CX)
        fwd[1, k, :, :, k, :] = s.T.reshape(MODES, bins, CX)
        inv[0, :, k, :, k, :] = c.reshape(bins, CX, MODES)
        inv[1, :, k, :, k, :] = s.reshape(bins, CX, MODES)
    fwd = fwd.reshape(4 * MODES, bins * 2 * CX)
    inv = inv.reshape(2 * bins * 2 * CX, 2 * MODES)
    return fwd.astype(np.float32), inv.astype(np.float32)


def pieces(x):
    hi = x.astype(BF16).astype(F32)
    rest = x - hi
    mid = rest.astype(BF16).astype(F32)
    return hi, mid, rest - mid


def home_plane(order):
    return jnp.where(order == 0, 0, jnp.where(order == 1, CX - 1, order - 1))


def add_chunk(last, at, step, plane0, data, rankb, taps, quad, lift_t, mess, keys, grid):
    base = step * CHUNK
    lanes = lax.broadcasted_iota(jnp.int32, (PTS, 128), 1) + base
    perm = jnp.concatenate(
        [jnp.where(rankb[...] == lanes + j * 128, 1.0, 0.0).astype(BF16)
         for j in range(CHUNK // 128)], axis=1)
    t = mm(data[...], perm)
    hzs = t[73:74]
    cols = t[74:75]
    spans = [(jnp.min(cols[:, j * SUB:(j + 1) * SUB]).astype(jnp.int32),
              jnp.max(cols[:, j * SUB:(j + 1) * SUB]).astype(jnp.int32) + 1)
             for j in range(CHUNK // SUB)]
    key = 256.0 * cols
    key = jnp.concatenate(
        [key + jnp.maximum(hzs - 1.0, 0.0), key + hzs, key + jnp.minimum(hzs + 1.0, NZ - 1.0),
         jnp.zeros((5, CHUNK), F32)], axis=0)
    key = jnp.transpose(key)
    for dz in range(3):
        keys[dz] = jnp.broadcast_to(key[:, dz:dz + 1], (CHUNK, NZ))

    values = mm(lift_t[...], t[0:64].astype(BF16))
    ox = t[64:65] + t[65:66] + t[66:67]
    oy = t[67:68] + t[68:69] + t[69:70]
    oz = t[70:71] + t[71:72] + t[72:73]
    coli = cols.astype(jnp.int32)
    gx = home_plane(lax.shift_right_logical(coli, 3)) + at[0] * CX
    gy = jnp.bitwise_and(coli, 7) + at[1] * CY
    k_x, k_y, k_z, k_b = taps[0], taps[1], taps[2], taps[3]

    def ends(g, end):
        return (jnp.where(g > 0, -1.0, 0.0), None, jnp.where(g < end, 1.0, 0.0))

    base_pre = k_x * ox + k_y * oy + k_z * oz + k_b
    ex = ends(gx, last[0])
    ey = ends(gy, last[1])
    ez = ends(hzs, NZ - 1.0)
    pend = []

    def flush():
        while len(pend) < 4:
            pend.append((None, jnp.zeros((CH, CHUNK), BF16)))
        kern = mm(quad[...], jnp.concatenate([h for _, h in pend], axis=0))
        for j, (where, _) in enumerate(pend):
            if where is None:
                continue
            dx, dy, dz = where
            k = dx * 9 + dy * 3 + dz
            m = kern[j * CH:(j + 1) * CH] * (values * t[80 + k:81 + k])
            hi = m.astype(BF16)
            lo = (m - hi.astype(F32)).astype(BF16)
            r = (dx * 3 + dy) * CH
            for s in range(CHUNK // SUB):
                cut = slice(s * SUB, (s + 1) * SUB)
                mess[s, r:r + CH, dz * SUB:(dz + 1) * SUB] = hi[:, cut]
                mess[s, r:r + CH, (3 + dz) * SUB:(4 + dz) * SUB] = lo[:, cut]
        pend.clear()

    for dx in range(3):
        pre_x = base_pre if ex[dx] is None else base_pre + ex[dx] * k_x
        for dy in range(3):
            pre_y = pre_x if ey[dy] is None else pre_x + ey[dy] * k_y
            for dz in range(3):
                pre = pre_y if ez[dz] is None else pre_y + ez[dz] * k_z
                pend.append(((dx, dy, dz), gelu(pre).astype(BF16)))
                if len(pend) == 4:
                    flush()
    flush()

    lane = lax.broadcasted_iota(jnp.int32, (SUB, NZ), 1).astype(F32)
    for s in range(CHUNK // SUB):
        def column(c, _):
            goal = lane + 256.0 * c.astype(F32)
            hot = jnp.concatenate(
                [jnp.where(keys[dz, s * SUB:(s + 1) * SUB] == goal, 1.0, 0.0).astype(BF16)
                 for dz in range(3)], axis=0)
            acc = mm(mess[s], jnp.concatenate([hot, hot], axis=0))
            cx = home_plane(lax.shift_right_logical(c, 3)) - plane0
            cy = jnp.bitwise_and(c, 7)
            for dx in range(3):
                for dy in range(3):
                    r = (dx * 3 + dy) * CH
                    grid[cx + dx, cy + dy] += acc[r:r + CH]
            return 0

        lax.fori_loop(spans[s][0], spans[s][1], column, 0)


def sides_kernel(last, at, feat_h, pos_h, home_h, nbr_h, deg_h, lift_h, first_h, bias_h, second_h,
                 grid, low, high, data, rankb, taps, quad, lift_t, count,
                 pos, home, nbr, deg, lift, first, bias, second, mess, keys, sems):
    pairs = [(home_h, home), (pos_h, pos), (nbr_h, nbr), (deg_h, deg),
             (feat_h, data.at[0:64]), (lift_h, lift), (first_h, first), (bias_h, bias),
             (second_h, second)]
    copies = [pltpu.make_async_copy(a, b, sems.at[i]) for i, (a, b) in enumerate(pairs)]
    for c in copies:
        c.start()
    grid[...] = jnp.zeros_like(grid)
    tri = jnp.where(
        lax.broadcasted_iota(jnp.int32, (CHUNK, CHUNK), 0)
        < lax.broadcasted_iota(jnp.int32, (CHUNK, CHUNK), 1), 1.0, 0.0).astype(BF16)
    for c in copies:
        c.wait()
    hx = home[0:1, :]
    hy = home[1:2, :]
    hz = home[2:3, :]
    order = jnp.where(hx == 0, 0, jnp.where(hx == CX - 1, 1, hx + 1))
    col = order * CY + hy
    count[0] = jnp.sum(jnp.where(order < 2, 1.0, 0.0)).astype(jnp.int32)

    ids = lax.broadcasted_iota(jnp.int32, (CX * CY, PTS), 0)
    carry = jnp.sum(jnp.where(col < ids, 1.0, 0.0), axis=1, keepdims=True)
    for blk in range(PTS // CHUNK):
        part = slice(blk * CHUNK, (blk + 1) * CHUNK)
        hot = jnp.where(col[:, part] == ids[:, part], 1.0, 0.0)
        ahead = mm(hot.astype(BF16), tri) + carry
        rank = jnp.sum(hot * ahead, axis=0, keepdims=True)
        rank = jnp.transpose(jnp.broadcast_to(rank, (8, CHUNK)))
        rankb[part, :] = jnp.broadcast_to(rank[:, 0:1], (CHUNK, 128)).astype(jnp.int32)
        carry = carry + jnp.sum(hot, axis=1, keepdims=True)

    slot = lax.broadcasted_iota(jnp.int32, (16, PTS), 0)
    bits = jnp.sum(
        jnp.where(slot < deg[...], jnp.left_shift(1, nbr[...]), 0), axis=0, keepdims=True)
    code = lax.broadcasted_iota(jnp.int32, (32, PTS), 0)
    live = jnp.bitwise_and(jnp.right_shift(bits, code), 1).astype(F32)
    off_x = (hx + at[0] * CX).astype(F32) + 0.5 - pos[0:1, :]
    off_y = (hy + at[1] * CY).astype(F32) + 0.5 - pos[1:2, :]
    off_z = hz.astype(F32) + 0.5 - pos[2:3, :]
    rows = [*pieces(off_x), *pieces(off_y), *pieces(off_z), hz.astype(F32), col.astype(F32),
            jnp.zeros((5, PTS), F32)]
    data[64:80, :] = jnp.concatenate(rows, axis=0).astype(BF16)
    data[80:112, :] = live.astype(BF16)

    flat = jnp.concatenate([first[...], bias[...], jnp.zeros((4, CH), F32)], axis=0)
    flat = jnp.concatenate([flat, jnp.zeros((8, 128 - CH), F32)], axis=1)
    flat = jnp.transpose(flat)
    for j in range(4):
        taps[j] = jnp.broadcast_to(flat[0:CH, j:j + 1], (CH, CHUNK))
    zero = jnp.zeros((CH, CH), F32)
    sec_t = jnp.transpose(second[...].astype(F32))
    quad[...] = jnp.concatenate(
        [jnp.concatenate([sec_t if i == j else zero for j in range(4)], axis=1)
         for i in range(4)], axis=0).astype(BF16)
    lift_t[...] = jnp.transpose(lift[...].astype(F32)).astype(BF16)

    def chunk(step, _):
        add_chunk(last, at, step, 0, data, rankb, taps, quad, lift_t, mess, keys, grid)
        return 0

    lax.fori_loop(0, (count[0] + CHUNK - 1) // CHUNK, chunk, 0)
    low[...] = grid[0]
    high[...] = grid[CX + 1]


def middle_kernel(last, at, count, data, rankb, taps, quad, lift_t, grid, mess, keys):
    grid[...] = jnp.zeros_like(grid)

    def chunk(step, _):
        add_chunk(last, at, step, 1, data, rankb, taps, quad, lift_t, mess, keys, grid)
        return 0

    lax.fori_loop((count[0] + CHUNK - 1) // CHUNK, PTS // CHUNK, chunk, 0)


def lift_points(at, last, feat, pos, home, nbr, deg, lift, first, bias, second):
    vmem = pl.BlockSpec(memory_space=pltpu.VMEM)
    smem = pl.BlockSpec(memory_space=pltpu.SMEM)
    work = [
        pltpu.VMEM((CHUNK // SUB, 9 * CH, 6 * SUB), BF16),
        pltpu.VMEM((3, CHUNK, NZ), F32),
    ]
    inputs = (feat, pos, home, nbr, deg, lift, first, bias, second)
    grid, low, high, *prepared, count = pl.pallas_call(
        functools.partial(sides_kernel, last),
        out_shape=[
            shape(CX + 2, CY + 2, CH, NZ),
            shape(CY + 2, CH, NZ),
            shape(CY + 2, CH, NZ),
            jax.ShapeDtypeStruct((112, PTS), BF16),
            jax.ShapeDtypeStruct((PTS, 128), jnp.int32),
            shape(4, CH, CHUNK),
            jax.ShapeDtypeStruct((4 * CH, 4 * CH), BF16),
            jax.ShapeDtypeStruct((CH, CH), BF16),
            jax.ShapeDtypeStruct((1,), jnp.int32),
        ],
        in_specs=[smem] + [pl.BlockSpec(memory_space=pltpu.HBM)] * len(inputs),
        out_specs=[vmem] * 8 + [smem],
        scratch_shapes=[pltpu.VMEM(x.shape, x.dtype) for x in inputs[1:]] + work
        + [pltpu.SemaphoreType.DMA((len(inputs),))],
        compiler_params=LIMIT,
        name="lift_sides",
    )(at, *inputs)
    middle = pl.pallas_call(
        functools.partial(middle_kernel, last),
        out_shape=shape(CX, CY + 2, CH, NZ),
        in_specs=[smem, smem] + [vmem] * 5,
        scratch_shapes=work,
        compiler_params=LIMIT,
        name="lift_middle",
    )(at, count, *prepared)
    return grid, low, high, middle


def latent_kernel(last, at, tabz, sides, middle, below, above, spec, own, yedge):
    low = at[0] == 0
    top = at[0] == last
    lane = lax.broadcasted_iota(jnp.int32, (MODES, HALVES), 1)
    table = tabz[...]
    for x in range(CX):
        for yp in range((CY + 2) // 2):
            cells = []
            for y in (2 * yp, 2 * yp + 1):
                l = sides[x + 1, y] + middle[x, y]
                if x == 0:
                    l = l + jnp.where(low, sides[0, y], below[y])
                if x == CX - 1:
                    l = l + jnp.where(top, sides[CX + 1, y], above[y])
                cells.append(l)
            d = mm(table, jnp.concatenate(cells, axis=0), NT, HIGH)
            re, im = d[0:MODES], d[MODES:]
            out = (jnp.where(lane < CH, re, swap(im)), jnp.where(lane < CH, swap(re), im))
            for j in range(2):
                y = 2 * yp + j
                if y in (0, CY + 1):
                    h = 0 if y == 0 else 1
                    spec[:, CX * CY + x * 2 + h, :] = out[j]
                    yedge[h, x] = cells[j]
                else:
                    spec[:, x * CY + y - 1, :] = out[j]
                    own[x * CY + y - 1] = cells[j]


def y_kernel(r, main, side, yedge, out, yedge_out):
    sgn = sign_row((MODES, HALVES))
    n = CX * CY
    pens = r.shape[0]
    for kz in range(2):
        o = kz * (n + 2 * CX)
        halo = mm(side[...], r[:, o + n:o + n + 2 * CX, :].reshape(pens * 2 * CX, HALVES), NN, HIGH)
        for x in range(CX):
            rows = r[:, o + x * CY:o + (x + 1) * CY, :].reshape(pens * CY, HALVES)
            ab = mm(main[...], rows, NN, HIGH) + halo[x * 2 * MODES:(x + 1) * 2 * MODES]
            out[:, kz * CX + x, :] = ab[:MODES] + swap(ab[MODES:]) * sgn
    yedge_out[...] = yedge[...]


def x_kernel(r, fwd, inv, w, out, lhs, res):
    rows = r.shape[0] * r.shape[1]
    modes = 2 * MODES
    sgn = sign_row((modes, HALVES))
    ab = mm(fwd[...], r[...].reshape(rows, HALVES), NN, HIGH)
    x = ab[:modes] + swap(ab[modes:]) * sgn
    parts = [*pieces(x), *pieces(swap(x))]
    lhs[...] = jnp.zeros_like(lhs)
    for j, p in enumerate(parts):
        lhs[:, j, :] = p
    for k in range(2):
        for j in range(MODES):
            m = k * MODES + j
            res[m] = mm(lhs[m][:, 0:CH].astype(BF16), w[j, 0, k])
    re = res[:, 0, :] + res[:, 1, :] + res[:, 2, :]
    im = res[:, 3, :] + res[:, 4, :] + res[:, 5, :]
    mixed = re - swap(im) * sgn
    ab = mm(inv[...], mixed, NN, HIGH)
    a, b = ab[:rows], ab[rows:]
    y = a - swap(b) * sign_row((rows, HALVES))
    out[...] = y.reshape(out.shape)


def y_back_kernel(r, inv, left, right, out):
    rows = inv.shape[0] // 2
    sgn = sign_row((rows, HALVES))
    for i in range(2 * CX):
        ab = mm(inv[...], r[:, i, :], NN, HIGH)
        y = ab[:rows] - swap(ab[rows:]) * sgn
        out[:, i * CY:(i + 1) * CY, :] = y.reshape(rows // CY, CY, HALVES)


def final_kernel(last, at, zb, tab, own, yedge, left, right, skip, bias, out):
    first_pen = at[1] == 0
    last_pen = at[1] == last
    lane = lax.broadcasted_iota(jnp.int32, (MODES, HALVES), 1)
    zero = jnp.zeros((CH, CH), F32)
    skip_t = jnp.transpose(skip[...])
    pair = jnp.concatenate(
        [jnp.concatenate([skip_t, zero], axis=1), jnp.concatenate([zero, skip_t], axis=1)], axis=0)
    col = jnp.concatenate([bias[...], bias[...]], axis=1)
    col = jnp.transpose(jnp.broadcast_to(col, (8, HALVES)))
    col = jnp.broadcast_to(col[:, 0:1], (HALVES, NZ))
    for x in range(CX):
        for yp in range(CY // 2):
            i = x * CY + 2 * yp
            u = zb[:, i, :]
            v = zb[:, i + 1, :]
            s = jnp.concatenate(
                [jnp.where(lane < CH, u, swap(v)), jnp.where(lane < CH, swap(u), v)], axis=0)
            spectral = mm(s, tab[...], TN, HIGH)
            lat = []
            for j in range(2):
                y = 2 * yp + j
                l = own[i + j]
                if y == 0:
                    l = l + jnp.where(first_pen, yedge[0, x], left[x])
                if y == CY - 1:
                    l = l + jnp.where(last_pen, yedge[1, x], right[x])
                lat.append(l)
            total = spectral + mm(pair, jnp.concatenate(lat, axis=0), NN, HIGH) + col
            out[x, 2 * yp:2 * yp + 2] = gelu(total).astype(BF16).reshape(2, CH, NZ)


def call(kernel, shapes, args, scratch=(), smem=False, name=None, unread=0):
    specs = [pl.BlockSpec(memory_space=pltpu.VMEM)] * len(args)
    if smem:
        specs[0] = pl.BlockSpec(memory_space=pltpu.SMEM)
    for j in range(unread):
        specs[-1 - j] = pl.BlockSpec(memory_space=pl.ANY)
    return pl.pallas_call(
        kernel,
        out_shape=shapes,
        in_specs=specs,
        scratch_shapes=list(scratch),
        compiler_params=LIMIT,
        name=name,
    )(*args)


def shape(*dims):
    return jax.ShapeDtypeStruct(dims, F32)


def exchange(x, axis):
    return lax.all_to_all(x, axis, split_axis=0, concat_axis=0, tiled=True)


def moved(x, axis, step):
    devices = range(lax.axis_size(axis))
    return lax.ppermute(x, axis, [(i - step, i) for i in devices if i - step in devices])


def per_device(features, positions, home_cells, neighbours, degrees, lift_input, kernel_first,
               kernel_bias, kernel_second, spectral_weights, skip_weights, skip_bias):
    bins = lax.axis_size("bin")
    pens = lax.axis_size("pen")
    at = jnp.stack([lax.axis_index("bin"), lax.axis_index("pen")]).astype(jnp.int32)
    sides, low, high, middle = lift_points(
        at, (bins * CX - 1, pens * CY - 1), features.T, positions, home_cells, neighbours.T,
        degrees[None, :], lift_input, kernel_first, kernel_bias[None, :], kernel_second)
    below = moved(high, "bin", 1)
    above = moved(low, "bin", -1)
    spec, own, yedge = call(
        functools.partial(latent_kernel, bins - 1),
        [shape(MODES, CX * (CY + 2), HALVES), shape(CX * CY, CH, NZ), shape(2, CX, CH, NZ)],
        (at, jnp.asarray(z_forward_table()), sides, middle, below, above),
        smem=True, name="latent_z")
    rows = 2 * CX * (CY + 2)
    r = exchange(spec.reshape(pens, rows, HALVES), "pen")
    main, side = y_forward_tables(pens)
    r, yedge = call(y_kernel, [shape(MODES, 2 * CX, HALVES), shape(2, CX, CH, NZ)],
                    (r, jnp.asarray(main), jnp.asarray(side), yedge), name="forward_y")
    left = moved(yedge[1], "pen", 1)
    right = moved(yedge[0], "pen", -1)
    r = exchange(r, "bin")
    fwd, inv = x_tables(bins)
    r = call(x_kernel, shape(MODES, 2 * CX, HALVES),
             (r, jnp.asarray(fwd), jnp.asarray(inv), spectral_weights),
             scratch=[pltpu.VMEM((2 * MODES, 8, HALVES), F32)] * 2, name="mix_x")
    r = exchange(r, "bin")
    r = call(y_back_kernel, shape(pens, 2 * CX * CY, HALVES),
             (r, jnp.asarray(y_inverse_table(pens)), left, right), unread=2, name="inverse_y")
    r = exchange(r, "pen")
    out = call(
        functools.partial(final_kernel, pens - 1),
        jax.ShapeDtypeStruct((CX, CY, CH, NZ), BF16),
        (at, r.reshape(MODES, CX * CY, HALVES), jnp.asarray(z_inverse_table()), own,
         yedge, left, right, skip_weights, skip_bias[None, :]),
        smem=True, name="finish")
    return out.transpose(0, 1, 3, 2)


def solution(mesh):
    in_specs = (
        P(("bin", "pen"), None),
        P(None, ("bin", "pen")),
        P(None, ("bin", "pen")),
        P(("bin", "pen"), None),
        P(("bin", "pen")),
        P(),
        P(),
        P(),
        P(),
        P(None, "bin", "pen", None, None),
        P(),
        P(),
    )
    out_specs = P("bin", "pen", None, None)
    return jax.shard_map(
        per_device, mesh=mesh, in_specs=in_specs, out_specs=out_specs, check_vma=False
    )
```

```python
import functools
import math

import jax
import jax.numpy as jnp
import numpy as np
from jax import lax
from jax.experimental import pallas as pl
from jax.experimental.pallas import tpu as pltpu
from jax.sharding import PartitionSpec as P

NZ = 192
CX = 4
CY = 8
PTS = 2048
CH = 64
MODES = 32
CHUNK = 256
SUB = 128
FIRST = 5
HALVES = 2 * CH

F32 = jnp.float32
BF16 = jnp.bfloat16
HIGH = lax.Precision.HIGH
LIMIT = pltpu.CompilerParams(vmem_limit_bytes=24 * 1024 * 1024)

NN = (((1,), (0,)), ((), ()))
NT = (((1,), (1,)), ((), ()))
TN = (((0,), (0,)), ((), ()))


def mm(a, b, dims=NN, precision=None):
    return lax.dot_general(a, b, dims, precision=precision, preferred_element_type=F32)


def gelu(x):
    inner = x * (0.7978845608028654 + 0.035677408136300125 * (x * x))
    half = 0.5 * x
    return half + half * jnp.tanh(inner)


def swap(x):
    return pltpu.roll(x, CH, 1)


def sign_row(shape):
    lane = lax.broadcasted_iota(jnp.int32, shape, 1)
    return jnp.where(lane < CH, 1.0, -1.0).astype(F32)


def tables(length, signed):
    mode = np.arange(MODES)
    if signed:
        mode = np.where(mode < MODES // 2, mode, mode - MODES)
    return mode


def angles(rows, length, signed):
    mode = tables(length, signed)
    phase = (np.asarray(rows)[:, None] * mode[None, :]) % length
    angle = phase * (2.0 * math.pi / length)
    scale = 1.0 / math.sqrt(length)
    return np.cos(angle) * scale, np.sin(angle) * scale


def z_forward_table():
    c, s = angles(np.arange(NZ), NZ, False)
    return np.concatenate([c.T, -s.T], axis=0).astype(np.float32)


def z_inverse_table():
    c, s = angles(np.arange(NZ), NZ, False)
    w = np.where(np.arange(MODES) == 0, 1.0, 2.0)[:, None]
    return np.concatenate([c.T * w, -s.T * w], axis=0).astype(np.float32)


def y_forward_table(pens):
    length = CY * pens
    c, s = angles(np.arange(length), length, True)
    return np.concatenate([c.T, s.T], axis=0).astype(np.float32)


def y_inverse_table(pens):
    length = CY * pens
    c, s = angles(np.arange(length), length, True)
    return np.concatenate([c, s], axis=0).astype(np.float32)


def x_tables(bins):
    length = CX * bins
    c, s = angles(np.arange(length), length, True)
    fwd = np.zeros((2, 2, MODES, bins, 2, CX))
    inv = np.zeros((2, bins, 2, CX, 2, MODES))
    for k in range(2):
        fwd[0, k, :, :, k, :] = c.T.reshape(MODES, bins, CX)
        fwd[1, k, :, :, k, :] = s.T.reshape(MODES, bins, CX)
        inv[0, :, k, :, k, :] = c.reshape(bins, CX, MODES)
        inv[1, :, k, :, k, :] = s.reshape(bins, CX, MODES)
    fwd = fwd.reshape(4 * MODES, bins * 2 * CX)
    inv = inv.reshape(2 * bins * 2 * CX, 2 * MODES)
    return fwd.astype(np.float32), inv.astype(np.float32)


def pieces(x):
    hi = x.astype(BF16).astype(F32)
    rest = x - hi
    mid = rest.astype(BF16).astype(F32)
    return hi, mid, rest - mid


def home_plane(order):
    return jnp.where(order == 0, 0, jnp.where(order == 1, CX - 1, order - 1))


def add_chunk(last, at, step, plane0, data, rankb, taps, quad, lift_t, mess, keys, grid):
    base = step * CHUNK
    lanes = lax.broadcasted_iota(jnp.int32, (PTS, 128), 1) + base
    perm = jnp.concatenate(
        [jnp.where(rankb[...] == lanes + j * 128, 1.0, 0.0).astype(BF16)
         for j in range(CHUNK // 128)], axis=1)
    t = mm(data[...], perm)
    hzs = t[73:74]
    cols = t[74:75]
    spans = [(jnp.min(cols[:, j * SUB:(j + 1) * SUB]).astype(jnp.int32),
              jnp.max(cols[:, j * SUB:(j + 1) * SUB]).astype(jnp.int32) + 1)
             for j in range(CHUNK // SUB)]
    key = 256.0 * cols
    key = jnp.concatenate(
        [key + jnp.maximum(hzs - 1.0, 0.0), key + hzs, key + jnp.minimum(hzs + 1.0, NZ - 1.0),
         jnp.zeros((5, CHUNK), F32)], axis=0)
    key = jnp.transpose(key)
    for dz in range(3):
        keys[dz] = jnp.broadcast_to(key[:, dz:dz + 1], (CHUNK, NZ))

    values = mm(lift_t[...], t[0:64].astype(BF16))
    ox = t[64:65] + t[65:66] + t[66:67]
    oy = t[67:68] + t[68:69] + t[69:70]
    oz = t[70:71] + t[71:72] + t[72:73]
    coli = cols.astype(jnp.int32)
    gx = home_plane(lax.shift_right_logical(coli, 3)) + at[0] * CX
    gy = jnp.bitwise_and(coli, 7) + at[1] * CY
    k_x, k_y, k_z, k_b = taps[0], taps[1], taps[2], taps[3]

    def ends(g, end):
        return (jnp.where(g > 0, -1.0, 0.0), None, jnp.where(g < end, 1.0, 0.0))

    base_pre = k_x * ox + k_y * oy + k_z * oz + k_b
    ex = ends(gx, last[0])
    ey = ends(gy, last[1])
    ez = ends(hzs, NZ - 1.0)
    pend = []

    def flush():
        while len(pend) < 4:
            pend.append((None, jnp.zeros((CH, CHUNK), BF16)))
        kern = mm(quad[...], jnp.concatenate([h for _, h in pend], axis=0))
        for j, (where, _) in enumerate(pend):
            if where is None:
                continue
            dx, dy, dz = where
            k = dx * 9 + dy * 3 + dz
            m = kern[j * CH:(j + 1) * CH] * (values * t[80 + k:81 + k])
            hi = m.astype(BF16)
            r = (dx * 3 + dy) * CH
            for s in range(CHUNK // SUB):
                cut = slice(s * SUB, (s + 1) * SUB)
                mess[s, r:r + CH, dz * SUB:(dz + 1) * SUB] = hi[:, cut]
        pend.clear()

    for dx in range(3):
        pre_x = base_pre if ex[dx] is None else base_pre + ex[dx] * k_x
        for dy in range(3):
            pre_y = pre_x if ey[dy] is None else pre_x + ey[dy] * k_y
            for dz in range(3):
                pre = pre_y if ez[dz] is None else pre_y + ez[dz] * k_z
                pend.append(((dx, dy, dz), gelu(pre).astype(BF16)))
                if len(pend) == 4:
                    flush()
    flush()

    lane = lax.broadcasted_iota(jnp.int32, (SUB, NZ), 1).astype(F32)
    longest = spans[0][1] - spans[0][0]
    for begin, end in spans[1:]:
        longest = jnp.maximum(longest, end - begin)

    def column(j, _):
        results = []
        for s, (begin, end) in enumerate(spans):
            c = jnp.minimum(begin + j, end - 1)
            goal = lane + jnp.where(begin + j < end, 256.0 * c.astype(F32), -1.0e6)
            hot = jnp.concatenate(
                [jnp.where(keys[dz, s * SUB:(s + 1) * SUB] == goal, 1.0, 0.0).astype(BF16)
                 for dz in range(3)], axis=0)
            results.append((c, mm(mess[s], hot)))
        for c, acc in results:
            cx = home_plane(lax.shift_right_logical(c, 3)) - plane0
            cy = jnp.bitwise_and(c, 7)
            for dx in range(3):
                for dy in range(3):
                    r = (dx * 3 + dy) * CH
                    grid[cx + dx, cy + dy] += acc[r:r + CH]
        return 0

    lax.fori_loop(0, longest, column, 0)


def sides_kernel(last, at, feat_h, pos_h, home_h, nbr_h, deg_h, lift_h, first_h, bias_h, second_h,
                 grid, low, high, data, rankb, taps, quad, lift_t, count,
                 pos, home, nbr, deg, lift, first, bias, second, mess, keys, sems):
    pairs = [(home_h, home), (pos_h, pos), (nbr_h, nbr), (deg_h, deg),
             (feat_h, data.at[0:64]), (lift_h, lift), (first_h, first), (bias_h, bias),
             (second_h, second)]
    copies = [pltpu.make_async_copy(a, b, sems.at[i]) for i, (a, b) in enumerate(pairs)]
    for c in copies:
        c.start()
    grid[...] = jnp.zeros_like(grid)
    tri = jnp.where(
        lax.broadcasted_iota(jnp.int32, (CHUNK, CHUNK), 0)
        < lax.broadcasted_iota(jnp.int32, (CHUNK, CHUNK), 1), 1.0, 0.0).astype(BF16)
    for c in copies:
        c.wait()
    hx = home[0:1, :]
    hy = home[1:2, :]
    hz = home[2:3, :]
    order = jnp.where(hx == 0, 0, jnp.where(hx == CX - 1, 1, hx + 1))
    col = order * CY + hy
    outer = jnp.sum(jnp.where(order < 2, 1.0, 0.0)).astype(jnp.int32)
    split = jnp.maximum((outer + CHUNK - 1) // CHUNK, FIRST)
    count[0] = split

    ids = lax.broadcasted_iota(jnp.int32, (CX * CY, PTS), 0)
    carry = jnp.sum(jnp.where(col < ids, 1.0, 0.0), axis=1, keepdims=True)
    for blk in range(PTS // CHUNK):
        part = slice(blk * CHUNK, (blk + 1) * CHUNK)
        hot = jnp.where(col[:, part] == ids[:, part], 1.0, 0.0)
        ahead = mm(hot.astype(BF16), tri) + carry
        rank = jnp.sum(hot * ahead, axis=0, keepdims=True)
        rank = jnp.transpose(jnp.broadcast_to(rank, (8, CHUNK)))
        rankb[part, :] = jnp.broadcast_to(rank[:, 0:1], (CHUNK, 128)).astype(jnp.int32)
        carry = carry + jnp.sum(hot, axis=1, keepdims=True)

    slot = lax.broadcasted_iota(jnp.int32, (16, PTS), 0)
    bits = jnp.sum(
        jnp.where(slot < deg[...], jnp.left_shift(1, nbr[...]), 0), axis=0, keepdims=True)
    code = lax.broadcasted_iota(jnp.int32, (32, PTS), 0)
    live = jnp.bitwise_and(jnp.right_shift(bits, code), 1).astype(F32)
    off_x = (hx + at[0] * CX).astype(F32) + 0.5 - pos[0:1, :]
    off_y = (hy + at[1] * CY).astype(F32) + 0.5 - pos[1:2, :]
    off_z = hz.astype(F32) + 0.5 - pos[2:3, :]
    rows = [*pieces(off_x), *pieces(off_y), *pieces(off_z), hz.astype(F32), col.astype(F32),
            jnp.zeros((5, PTS), F32)]
    data[64:80, :] = jnp.concatenate(rows, axis=0).astype(BF16)
    data[80:112, :] = live.astype(BF16)

    flat = jnp.concatenate([first[...], bias[...], jnp.zeros((4, CH), F32)], axis=0)
    flat = jnp.concatenate([flat, jnp.zeros((8, 128 - CH), F32)], axis=1)
    flat = jnp.transpose(flat)
    for j in range(4):
        taps[j] = jnp.broadcast_to(flat[0:CH, j:j + 1], (CH, CHUNK))
    zero = jnp.zeros((CH, CH), F32)
    sec_t = jnp.transpose(second[...].astype(F32))
    quad[...] = jnp.concatenate(
        [jnp.concatenate([sec_t if i == j else zero for j in range(4)], axis=1)
         for i in range(4)], axis=0).astype(BF16)
    lift_t[...] = jnp.transpose(lift[...].astype(F32)).astype(BF16)

    def chunk(step, _):
        add_chunk(last, at, step, 0, data, rankb, taps, quad, lift_t, mess, keys, grid)
        return 0

    lax.fori_loop(0, split, chunk, 0)
    low[...] = grid[0]
    high[...] = grid[CX + 1]


def middle_kernel(last, at, count, data, rankb, taps, quad, lift_t, grid, mess, keys):
    grid[...] = jnp.zeros_like(grid)

    def chunk(step, _):
        add_chunk(last, at, step, 1, data, rankb, taps, quad, lift_t, mess, keys, grid)
        return 0

    lax.fori_loop(count[0], PTS // CHUNK, chunk, 0)


def lift_points(at, last, feat, pos, home, nbr, deg, lift, first, bias, second):
    vmem = pl.BlockSpec(memory_space=pltpu.VMEM)
    smem = pl.BlockSpec(memory_space=pltpu.SMEM)
    work = [
        pltpu.VMEM((CHUNK // SUB, 9 * CH, 3 * SUB), BF16),
        pltpu.VMEM((3, CHUNK, NZ), F32),
    ]
    inputs = (feat, pos, home, nbr, deg, lift, first, bias, second)
    grid, low, high, *prepared, count = pl.pallas_call(
        functools.partial(sides_kernel, last),
        out_shape=[
            shape(CX + 2, CY + 2, CH, NZ),
            shape(CY + 2, CH, NZ),
            shape(CY + 2, CH, NZ),
            jax.ShapeDtypeStruct((112, PTS), BF16),
            jax.ShapeDtypeStruct((PTS, 128), jnp.int32),
            shape(4, CH, CHUNK),
            jax.ShapeDtypeStruct((4 * CH, 4 * CH), BF16),
            jax.ShapeDtypeStruct((CH, CH), BF16),
            jax.ShapeDtypeStruct((1,), jnp.int32),
        ],
        in_specs=[smem] + [pl.BlockSpec(memory_space=pltpu.HBM)] * len(inputs),
        out_specs=[vmem] * 8 + [smem],
        scratch_shapes=[pltpu.VMEM(x.shape, x.dtype) for x in inputs[1:]] + work
        + [pltpu.SemaphoreType.DMA((len(inputs),))],
        compiler_params=LIMIT,
        name="lift_sides",
    )(at, *inputs)
    middle = pl.pallas_call(
        functools.partial(middle_kernel, last),
        out_shape=shape(CX, CY + 2, CH, NZ),
        in_specs=[smem, smem] + [vmem] * 5,
        scratch_shapes=work,
        compiler_params=LIMIT,
        name="lift_middle",
    )(at, count, *prepared)
    return grid, low, high, middle


def latent_kernel(last, at, sides, middle, below, above, own, low_y, high_y):
    low = at[0] == 0
    top = at[0] == last
    for x in range(CX):
        for y in range(CY + 2):
            l = sides[x + 1, y] + middle[x, y]
            if x == 0:
                l = l + jnp.where(low, sides[0, y], below[y])
            if x == CX - 1:
                l = l + jnp.where(top, sides[CX + 1, y], above[y])
            if y == 0:
                low_y[x] = l
            elif y == CY + 1:
                high_y[x] = l
            else:
                own[x * CY + y - 1] = l


def z_modes(table, pair):
    lane = lax.broadcasted_iota(jnp.int32, (MODES, HALVES), 1)
    d = mm(table, pair, NT, HIGH)
    re, im = d[0:MODES], d[MODES:]
    return jnp.where(lane < CH, re, swap(im)), jnp.where(lane < CH, swap(re), im)


def inner_kernel(tabz, own, spec):
    table = tabz[...]
    for x in range(CX):
        for y in range(1, CY - 1, 2):
            i = x * CY + y
            u, v = z_modes(table, own[i:i + 2].reshape(2 * CH, NZ))
            spec[:, i, :] = u
            spec[:, i + 1, :] = v
        spec[:, x * CY, :] = jnp.zeros((MODES, HALVES), F32)
        spec[:, x * CY + CY - 1, :] = jnp.zeros((MODES, HALVES), F32)


def outer_kernel(last, at, tabz, own, part, low_y, high_y, left, right, spec, ends):
    first_pen = at[1] == 0
    last_pen = at[1] == last
    table = tabz[...]
    spec[...] = part[...]
    for x in range(CX):
        a = own[x * CY] + jnp.where(first_pen, low_y[x], left[x])
        b = own[x * CY + CY - 1] + jnp.where(last_pen, high_y[x], right[x])
        u, v = z_modes(table, jnp.concatenate([a, b], axis=0))
        spec[:, x * CY, :] = u
        spec[:, x * CY + CY - 1, :] = v
        ends[0, x] = a
        ends[1, x] = b


def y_kernel(r, main, out):
    sgn = sign_row((MODES, HALVES))
    pens = r.shape[0]
    for i in range(2 * CX):
        rows = r[:, i * CY:(i + 1) * CY, :].reshape(pens * CY, HALVES)
        ab = mm(main[...], rows, NN, HIGH)
        out[:, i, :] = ab[:MODES] + swap(ab[MODES:]) * sgn


def x_kernel(r, fwd, inv, w, out, lhs, res):
    rows = r.shape[0] * r.shape[1]
    modes = 2 * MODES
    sgn = sign_row((modes, HALVES))
    ab = mm(fwd[...], r[...].reshape(rows, HALVES), NN, HIGH)
    x = ab[:modes] + swap(ab[modes:]) * sgn
    parts = [*pieces(x), *pieces(swap(x))]
    lhs[...] = jnp.zeros_like(lhs)
    for j, p in enumerate(parts):
        lhs[:, j, :] = p
    for k in range(2):
        for j in range(MODES):
            m = k * MODES + j
            res[m] = mm(lhs[m][:, 0:CH].astype(BF16), w[j, 0, k])
    re = res[:, 0, :] + res[:, 1, :] + res[:, 2, :]
    im = res[:, 3, :] + res[:, 4, :] + res[:, 5, :]
    mixed = re - swap(im) * sgn
    ab = mm(inv[...], mixed, NN, HIGH)
    a, b = ab[:rows], ab[rows:]
    y = a - swap(b) * sign_row((rows, HALVES))
    out[...] = y.reshape(out.shape)


def y_back_kernel(r, inv, out):
    rows = inv.shape[0] // 2
    sgn = sign_row((rows, HALVES))
    for i in range(2 * CX):
        ab = mm(inv[...], r[:, i, :], NN, HIGH)
        y = ab[:rows] - swap(ab[rows:]) * sgn
        out[:, i * CY:(i + 1) * CY, :] = y.reshape(rows // CY, CY, HALVES)


def final_kernel(zb, tab, own, ends, skip, bias, out):
    lane = lax.broadcasted_iota(jnp.int32, (MODES, HALVES), 1)
    zero = jnp.zeros((CH, CH), F32)
    skip_t = jnp.transpose(skip[...])
    pair = jnp.concatenate(
        [jnp.concatenate([skip_t, zero], axis=1), jnp.concatenate([zero, skip_t], axis=1)], axis=0)
    col = jnp.concatenate([bias[...], bias[...]], axis=1)
    col = jnp.transpose(jnp.broadcast_to(col, (8, HALVES)))
    col = jnp.broadcast_to(col[:, 0:1], (HALVES, NZ))
    for x in range(CX):
        for yp in range(CY // 2):
            i = x * CY + 2 * yp
            u = zb[:, i, :]
            v = zb[:, i + 1, :]
            s = jnp.concatenate(
                [jnp.where(lane < CH, u, swap(v)), jnp.where(lane < CH, swap(u), v)], axis=0)
            spectral = mm(s, tab[...], TN, HIGH)
            lat = []
            for j in range(2):
                y = 2 * yp + j
                lat.append(ends[0, x] if y == 0 else ends[1, x] if y == CY - 1 else own[i + j])
            total = spectral + mm(pair, jnp.concatenate(lat, axis=0), NN, HIGH) + col
            out[x, 2 * yp:2 * yp + 2] = gelu(total).astype(BF16).reshape(2, CH, NZ)


def call(kernel, shapes, args, scratch=(), smem=False, name=None):
    specs = [pl.BlockSpec(memory_space=pltpu.VMEM)] * len(args)
    if smem:
        specs[0] = pl.BlockSpec(memory_space=pltpu.SMEM)
    return pl.pallas_call(
        kernel,
        out_shape=shapes,
        in_specs=specs,
        scratch_shapes=list(scratch),
        compiler_params=LIMIT,
        name=name,
    )(*args)


def shape(*dims):
    return jax.ShapeDtypeStruct(dims, F32)


def exchange(x, axis):
    return lax.all_to_all(x, axis, split_axis=0, concat_axis=0, tiled=True)


def moved(x, axis, step):
    devices = range(lax.axis_size(axis))
    return lax.ppermute(x, axis, [(i - step, i) for i in devices if i - step in devices])


def per_device(features, positions, home_cells, neighbours, degrees, lift_input, kernel_first,
               kernel_bias, kernel_second, spectral_weights, skip_weights, skip_bias):
    bins = lax.axis_size("bin")
    pens = lax.axis_size("pen")
    at = jnp.stack([lax.axis_index("bin"), lax.axis_index("pen")]).astype(jnp.int32)
    sides, low, high, middle = lift_points(
        at, (bins * CX - 1, pens * CY - 1), features.T, positions, home_cells, neighbours.T,
        degrees[None, :], lift_input, kernel_first, kernel_bias[None, :], kernel_second)
    below = moved(high, "bin", 1)
    above = moved(low, "bin", -1)
    half = shape(CX, CH, NZ)
    own, low_y, high_y = call(
        functools.partial(latent_kernel, bins - 1), [shape(CX * CY, CH, NZ), half, half],
        (at, sides, middle, below, above), smem=True, name="latent")
    left = moved(high_y, "pen", 1)
    right = moved(low_y, "pen", -1)
    table = jnp.asarray(z_forward_table())
    spec = call(inner_kernel, shape(MODES, CX * CY, HALVES), (table, own), name="forward_z")
    spec, ends = call(
        functools.partial(outer_kernel, pens - 1), [shape(*spec.shape), shape(2, CX, CH, NZ)],
        (at, table, own, spec, low_y, high_y, left, right), smem=True, name="forward_z_ends")
    r = exchange(spec.reshape(pens, 2 * CX * CY, HALVES), "pen")
    r = call(y_kernel, shape(MODES, 2 * CX, HALVES), (r, jnp.asarray(y_forward_table(pens))),
             name="forward_y")
    r = exchange(r, "bin")
    fwd, inv = x_tables(bins)
    r = call(x_kernel, shape(MODES, 2 * CX, HALVES),
             (r, jnp.asarray(fwd), jnp.asarray(inv), spectral_weights),
             scratch=[pltpu.VMEM((2 * MODES, 8, HALVES), F32)] * 2, name="mix_x")
    r = exchange(r, "bin")
    r = call(y_back_kernel, shape(pens, 2 * CX * CY, HALVES),
             (r, jnp.asarray(y_inverse_table(pens))), name="inverse_y")
    r = exchange(r, "pen")
    out = call(
        final_kernel, jax.ShapeDtypeStruct((CX, CY, CH, NZ), BF16),
        (r.reshape(MODES, CX * CY, HALVES), jnp.asarray(z_inverse_table()), own, ends,
         skip_weights, skip_bias[None, :]), name="finish")
    return out.transpose(0, 1, 3, 2)


def solution(mesh):
    in_specs = (
        P(("bin", "pen"), None),
        P(None, ("bin", "pen")),
        P(None, ("bin", "pen")),
        P(("bin", "pen"), None),
        P(("bin", "pen")),
        P(),
        P(),
        P(),
        P(),
        P(None, "bin", "pen", None, None),
        P(),
        P(),
    )
    out_specs = P("bin", "pen", None, None)
    return jax.shard_map(
        per_device, mesh=mesh, in_specs=in_specs, out_specs=out_specs, check_vma=False
    )
```

```python
import functools
import math

import jax
import jax.numpy as jnp
import numpy as np
from jax import lax
from jax.experimental import pallas as pl
from jax.experimental.pallas import tpu as pltpu
from jax.sharding import PartitionSpec as P

NZ = 192
CX = 4
CY = 8
PTS = 2048
CH = 64
MODES = 32
CHUNK = 256
SUB = 128
LARGE = 512
FIRST = 5
HALVES = 2 * CH

F32 = jnp.float32
BF16 = jnp.bfloat16
HIGH = lax.Precision.HIGH
LIMIT = pltpu.CompilerParams(vmem_limit_bytes=24 * 1024 * 1024)

NN = (((1,), (0,)), ((), ()))
NT = (((1,), (1,)), ((), ()))
TN = (((0,), (0,)), ((), ()))


def mm(a, b, dims=NN, precision=None):
    return lax.dot_general(a, b, dims, precision=precision, preferred_element_type=F32)


def gelu(x):
    inner = x * (0.7978845608028654 + 0.035677408136300125 * (x * x))
    half = 0.5 * x
    return half + half * jnp.tanh(inner)


def swap(x):
    return pltpu.roll(x, CH, 1)


def sign_row(shape):
    lane = lax.broadcasted_iota(jnp.int32, shape, 1)
    return jnp.where(lane < CH, 1.0, -1.0).astype(F32)


def tables(length, signed):
    mode = np.arange(MODES)
    if signed:
        mode = np.where(mode < MODES // 2, mode, mode - MODES)
    return mode


def angles(rows, length, signed):
    mode = tables(length, signed)
    phase = (np.asarray(rows)[:, None] * mode[None, :]) % length
    angle = phase * (2.0 * math.pi / length)
    scale = 1.0 / math.sqrt(length)
    return np.cos(angle) * scale, np.sin(angle) * scale


def z_forward_table():
    c, s = angles(np.arange(NZ), NZ, False)
    return np.concatenate([c.T, -s.T], axis=0).astype(np.float32)


def z_inverse_table():
    c, s = angles(np.arange(NZ), NZ, False)
    w = np.where(np.arange(MODES) == 0, 1.0, 2.0)[:, None]
    return np.concatenate([c.T * w, -s.T * w], axis=0).astype(np.float32)


def y_forward_table(pens):
    length = CY * pens
    c, s = angles(np.arange(length), length, True)
    return np.concatenate([c.T, s.T], axis=0).astype(np.float32)


def y_inverse_table(pens):
    length = CY * pens
    c, s = angles(np.arange(length), length, True)
    return np.concatenate([c, s], axis=0).astype(np.float32)


def x_tables(bins):
    length = CX * bins
    c, s = angles(np.arange(length), length, True)
    fwd = np.zeros((2, 2, MODES, bins, 2, CX))
    inv = np.zeros((2, bins, 2, CX, 2, MODES))
    for k in range(2):
        fwd[0, k, :, :, k, :] = c.T.reshape(MODES, bins, CX)
        fwd[1, k, :, :, k, :] = s.T.reshape(MODES, bins, CX)
        inv[0, :, k, :, k, :] = c.reshape(bins, CX, MODES)
        inv[1, :, k, :, k, :] = s.reshape(bins, CX, MODES)
    fwd = fwd.reshape(4 * MODES, bins * 2 * CX)
    inv = inv.reshape(2 * bins * 2 * CX, 2 * MODES)
    return fwd.astype(np.float32), inv.astype(np.float32)


def pieces(x):
    hi = x.astype(BF16).astype(F32)
    rest = x - hi
    mid = rest.astype(BF16).astype(F32)
    return hi, mid, rest - mid


def home_plane(order):
    return jnp.where(order == 0, 0, jnp.where(order == 1, CX - 1, order - 1))


def add_chunk(last, at, base, size, plane0, data, rankb, taps, quad, lift_t, mess, keys, grid):
    lanes = lax.broadcasted_iota(jnp.int32, (PTS, 128), 1) + base
    perm = jnp.concatenate(
        [jnp.where(rankb[...] == lanes + j * 128, 1.0, 0.0).astype(BF16)
         for j in range(size // 128)], axis=1)
    t = mm(data[...], perm)
    hzs = t[73:74]
    cols = t[74:75]
    spans = [(jnp.min(cols[:, j * SUB:(j + 1) * SUB]).astype(jnp.int32),
              jnp.max(cols[:, j * SUB:(j + 1) * SUB]).astype(jnp.int32) + 1)
             for j in range(size // SUB)]
    key = 256.0 * cols
    key = jnp.concatenate(
        [key + jnp.maximum(hzs - 1.0, 0.0), key + hzs, key + jnp.minimum(hzs + 1.0, NZ - 1.0),
         jnp.zeros((5, size), F32)], axis=0)
    key = jnp.transpose(key)
    for dz in range(3):
        keys[dz, 0:size] = jnp.broadcast_to(key[:, dz:dz + 1], (size, NZ))

    values = mm(lift_t[...], t[0:64].astype(BF16))
    ox = t[64:65] + t[65:66] + t[66:67]
    oy = t[67:68] + t[68:69] + t[69:70]
    oz = t[70:71] + t[71:72] + t[72:73]
    coli = cols.astype(jnp.int32)
    gx = home_plane(lax.shift_right_logical(coli, 3)) + at[0] * CX
    gy = jnp.bitwise_and(coli, 7) + at[1] * CY
    k_x, k_y, k_z, k_b = (taps[j, :, 0:size] for j in range(4))

    def ends(g, end):
        return (jnp.where(g > 0, -1.0, 0.0), None, jnp.where(g < end, 1.0, 0.0))

    base_pre = k_x * ox + k_y * oy + k_z * oz + k_b
    ex = ends(gx, last[0])
    ey = ends(gy, last[1])
    ez = ends(hzs, NZ - 1.0)
    pend = []

    def flush():
        while len(pend) < 4:
            pend.append((None, jnp.zeros((CH, size), BF16)))
        kern = mm(quad[...], jnp.concatenate([h for _, h in pend], axis=0))
        for j, (where, _) in enumerate(pend):
            if where is None:
                continue
            dx, dy, dz = where
            k = dx * 9 + dy * 3 + dz
            m = kern[j * CH:(j + 1) * CH] * (values * t[80 + k:81 + k])
            hi = m.astype(BF16)
            r = (dx * 3 + dy) * CH
            for s in range(size // SUB):
                cut = slice(s * SUB, (s + 1) * SUB)
                mess[s, r:r + CH, dz * SUB:(dz + 1) * SUB] = hi[:, cut]
        pend.clear()

    for dx in range(3):
        pre_x = base_pre if ex[dx] is None else base_pre + ex[dx] * k_x
        for dy in range(3):
            pre_y = pre_x if ey[dy] is None else pre_x + ey[dy] * k_y
            for dz in range(3):
                pre = pre_y if ez[dz] is None else pre_y + ez[dz] * k_z
                pend.append(((dx, dy, dz), gelu(pre).astype(BF16)))
                if len(pend) == 4:
                    flush()
    flush()

    lane = lax.broadcasted_iota(jnp.int32, (SUB, NZ), 1).astype(F32)
    longest = spans[0][1] - spans[0][0]
    for begin, end in spans[1:]:
        longest = jnp.maximum(longest, end - begin)

    def column(j, _):
        results = []
        for s, (begin, end) in enumerate(spans):
            c = jnp.minimum(begin + j, end - 1)
            goal = lane + jnp.where(begin + j < end, 256.0 * c.astype(F32), -1.0e6)
            hot = jnp.concatenate(
                [jnp.where(keys[dz, s * SUB:(s + 1) * SUB] == goal, 1.0, 0.0).astype(BF16)
                 for dz in range(3)], axis=0)
            results.append((c, [mm(mess[s, q * 3 * CH:(q + 1) * 3 * CH], hot) for q in range(3)]))
        for c, acc in results:
            cx = home_plane(lax.shift_right_logical(c, 3)) - plane0
            cy = jnp.bitwise_and(c, 7)
            for dx in range(3):
                for dy in range(3):
                    grid[cx + dx, cy + dy] += acc[dx][dy * CH:(dy + 1) * CH]
        return 0

    lax.fori_loop(0, longest, column, 0)


def sides_kernel(last, at, feat_h, pos_h, home_h, nbr_h, deg_h, lift_h, first_h, bias_h, second_h,
                 grid, low, high, data, rankb, taps, quad, lift_t, count,
                 pos, home, nbr, deg, lift, first, bias, second, mess, keys, sems):
    pairs = [(home_h, home), (pos_h, pos), (nbr_h, nbr), (deg_h, deg),
             (feat_h, data.at[0:64]), (lift_h, lift), (first_h, first), (bias_h, bias),
             (second_h, second)]
    copies = [pltpu.make_async_copy(a, b, sems.at[i]) for i, (a, b) in enumerate(pairs)]
    for c in copies:
        c.start()
    grid[...] = jnp.zeros_like(grid)
    tri = jnp.where(
        lax.broadcasted_iota(jnp.int32, (CHUNK, CHUNK), 0)
        < lax.broadcasted_iota(jnp.int32, (CHUNK, CHUNK), 1), 1.0, 0.0).astype(BF16)
    for c in copies:
        c.wait()
    hx = home[0:1, :]
    hy = home[1:2, :]
    hz = home[2:3, :]
    order = jnp.where(hx == 0, 0, jnp.where(hx == CX - 1, 1, hx + 1))
    col = order * CY + hy
    outer = jnp.sum(jnp.where(order < 2, 1.0, 0.0)).astype(jnp.int32)
    split = jnp.maximum((outer + CHUNK - 1) // CHUNK, FIRST)
    count[0] = split

    ids = lax.broadcasted_iota(jnp.int32, (CX * CY, PTS), 0)
    carry = jnp.sum(jnp.where(col < ids, 1.0, 0.0), axis=1, keepdims=True)
    for blk in range(PTS // CHUNK):
        part = slice(blk * CHUNK, (blk + 1) * CHUNK)
        hot = jnp.where(col[:, part] == ids[:, part], 1.0, 0.0)
        ahead = mm(hot.astype(BF16), tri) + carry
        rank = jnp.sum(hot * ahead, axis=0, keepdims=True)
        rank = jnp.transpose(jnp.broadcast_to(rank, (8, CHUNK)))
        rankb[part, :] = jnp.broadcast_to(rank[:, 0:1], (CHUNK, 128)).astype(jnp.int32)
        carry = carry + jnp.sum(hot, axis=1, keepdims=True)

    slot = lax.broadcasted_iota(jnp.int32, (16, PTS), 0)
    bits = jnp.sum(
        jnp.where(slot < deg[...], jnp.left_shift(1, nbr[...]), 0), axis=0, keepdims=True)
    code = lax.broadcasted_iota(jnp.int32, (32, PTS), 0)
    live = jnp.bitwise_and(jnp.right_shift(bits, code), 1).astype(F32)
    off_x = (hx + at[0] * CX).astype(F32) + 0.5 - pos[0:1, :]
    off_y = (hy + at[1] * CY).astype(F32) + 0.5 - pos[1:2, :]
    off_z = hz.astype(F32) + 0.5 - pos[2:3, :]
    rows = [*pieces(off_x), *pieces(off_y), *pieces(off_z), hz.astype(F32), col.astype(F32),
            jnp.zeros((5, PTS), F32)]
    data[64:80, :] = jnp.concatenate(rows, axis=0).astype(BF16)
    data[80:112, :] = live.astype(BF16)

    flat = jnp.concatenate([first[...], bias[...], jnp.zeros((4, CH), F32)], axis=0)
    flat = jnp.concatenate([flat, jnp.zeros((8, 128 - CH), F32)], axis=1)
    flat = jnp.transpose(flat)
    for j in range(4):
        taps[j] = jnp.broadcast_to(flat[0:CH, j:j + 1], (CH, LARGE))
    zero = jnp.zeros((CH, CH), F32)
    sec_t = jnp.transpose(second[...].astype(F32))
    quad[...] = jnp.concatenate(
        [jnp.concatenate([sec_t if i == j else zero for j in range(4)], axis=1)
         for i in range(4)], axis=0).astype(BF16)
    lift_t[...] = jnp.transpose(lift[...].astype(F32)).astype(BF16)

    def chunk(size, first, step, _):
        add_chunk(last, at, first + step * size, size, 0, data, rankb, taps, quad, lift_t, mess,
                  keys, grid)
        return 0

    large = split // 2
    lax.fori_loop(0, large, functools.partial(chunk, LARGE, 0), 0)
    lax.fori_loop(0, split - 2 * large, functools.partial(chunk, CHUNK, large * LARGE), 0)
    low[...] = grid[0]
    high[...] = grid[CX + 1]


def middle_kernel(last, at, count, data, rankb, taps, quad, lift_t, grid, mess, keys):
    grid[...] = jnp.zeros_like(grid)

    def chunk(size, first, step, _):
        add_chunk(last, at, first + step * size, size, 1, data, rankb, taps, quad, lift_t, mess,
                  keys, grid)
        return 0

    split = count[0]
    odd = jnp.bitwise_and(split, 1)
    large = (PTS // CHUNK - split) // 2
    lax.fori_loop(0, odd, functools.partial(chunk, CHUNK, split * CHUNK), 0)
    lax.fori_loop(0, large, functools.partial(chunk, LARGE, (split + odd) * CHUNK), 0)


def lift_points(at, last, feat, pos, home, nbr, deg, lift, first, bias, second):
    vmem = pl.BlockSpec(memory_space=pltpu.VMEM)
    smem = pl.BlockSpec(memory_space=pltpu.SMEM)
    work = [
        pltpu.VMEM((LARGE // SUB, 9 * CH, 3 * SUB), BF16),
        pltpu.VMEM((3, LARGE, NZ), F32),
    ]
    inputs = tuple(
        pltpu.with_memory_space_constraint(x, pltpu.HBM)
        for x in (feat, pos, home, nbr, deg, lift, first, bias, second))
    grid, low, high, *prepared, count = pl.pallas_call(
        functools.partial(sides_kernel, last),
        out_shape=[
            shape(CX + 2, CY + 2, CH, NZ),
            shape(CY + 2, CH, NZ),
            shape(CY + 2, CH, NZ),
            jax.ShapeDtypeStruct((112, PTS), BF16),
            jax.ShapeDtypeStruct((PTS, 128), jnp.int32),
            shape(4, CH, LARGE),
            jax.ShapeDtypeStruct((4 * CH, 4 * CH), BF16),
            jax.ShapeDtypeStruct((CH, CH), BF16),
            jax.ShapeDtypeStruct((1,), jnp.int32),
        ],
        in_specs=[smem] + [pl.BlockSpec(memory_space=pltpu.HBM)] * len(inputs),
        out_specs=[vmem] * 8 + [smem],
        scratch_shapes=[pltpu.VMEM(x.shape, x.dtype) for x in inputs[1:]] + work
        + [pltpu.SemaphoreType.DMA((len(inputs),))],
        compiler_params=LIMIT,
        name="lift_sides",
    )(at, *inputs)
    middle = pl.pallas_call(
        functools.partial(middle_kernel, last),
        out_shape=shape(CX, CY + 2, CH, NZ),
        in_specs=[smem, smem] + [vmem] * 5,
        scratch_shapes=work,
        compiler_params=LIMIT,
        name="lift_middle",
    )(at, count, *prepared)
    return grid, low, high, middle


def latent_kernel(last, at, sides, middle, below, above, own, low_y, high_y):
    low = at[0] == 0
    top = at[0] == last
    for x in range(CX):
        for y in range(CY + 2):
            l = sides[x + 1, y] + middle[x, y]
            if x == 0:
                l = l + jnp.where(low, sides[0, y], below[y])
            if x == CX - 1:
                l = l + jnp.where(top, sides[CX + 1, y], above[y])
            if y == 0:
                low_y[x] = l
            elif y == CY + 1:
                high_y[x] = l
            else:
                own[x * CY + y - 1] = l


def z_modes(table, pair):
    lane = lax.broadcasted_iota(jnp.int32, (MODES, HALVES), 1)
    d = mm(table, pair, NT, HIGH)
    re, im = d[0:MODES], d[MODES:]
    return jnp.where(lane < CH, re, swap(im)), jnp.where(lane < CH, swap(re), im)


def inner_kernel(tabz, own, spec):
    table = tabz[...]
    for x in range(CX):
        for y in range(1, CY - 1, 2):
            i = x * CY + y
            u, v = z_modes(table, own[i:i + 2].reshape(2 * CH, NZ))
            spec[:, i, :] = u
            spec[:, i + 1, :] = v
        spec[:, x * CY, :] = jnp.zeros((MODES, HALVES), F32)
        spec[:, x * CY + CY - 1, :] = jnp.zeros((MODES, HALVES), F32)


def outer_kernel(last, at, tabz, own, part, low_y, high_y, left, right, spec, ends):
    first_pen = at[1] == 0
    last_pen = at[1] == last
    table = tabz[...]
    spec[...] = part[...]
    for x in range(CX):
        a = own[x * CY] + jnp.where(first_pen, low_y[x], left[x])
        b = own[x * CY + CY - 1] + jnp.where(last_pen, high_y[x], right[x])
        u, v = z_modes(table, jnp.concatenate([a, b], axis=0))
        spec[:, x * CY, :] = u
        spec[:, x * CY + CY - 1, :] = v
        ends[0, x] = a
        ends[1, x] = b


def y_kernel(r, main, out):
    sgn = sign_row((MODES, HALVES))
    pens = r.shape[0]
    for i in range(2 * CX):
        rows = r[:, i * CY:(i + 1) * CY, :].reshape(pens * CY, HALVES)
        ab = mm(main[...], rows, NN, HIGH)
        out[:, i, :] = ab[:MODES] + swap(ab[MODES:]) * sgn


def x_kernel(r, fwd, inv, w, out, lhs, res):
    rows = r.shape[0] * r.shape[1]
    modes = 2 * MODES
    sgn = sign_row((modes, HALVES))
    ab = mm(fwd[...], r[...].reshape(rows, HALVES), NN, HIGH)
    x = ab[:modes] + swap(ab[modes:]) * sgn
    parts = [*pieces(x), *pieces(swap(x))]
    lhs[...] = jnp.zeros_like(lhs)
    for j, p in enumerate(parts):
        lhs[:, j, :] = p
    for k in range(2):
        for j in range(MODES):
            m = k * MODES + j
            res[m] = mm(lhs[m][:, 0:CH].astype(BF16), w[j, 0, k])
    re = res[:, 0, :] + res[:, 1, :] + res[:, 2, :]
    im = res[:, 3, :] + res[:, 4, :] + res[:, 5, :]
    mixed = re - swap(im) * sgn
    ab = mm(inv[...], mixed, NN, HIGH)
    a, b = ab[:rows], ab[rows:]
    y = a - swap(b) * sign_row((rows, HALVES))
    out[...] = y.reshape(out.shape)


def y_back_kernel(r, inv, out):
    rows = inv.shape[0] // 2
    sgn = sign_row((rows, HALVES))
    for i in range(2 * CX):
        ab = mm(inv[...], r[:, i, :], NN, HIGH)
        y = ab[:rows] - swap(ab[rows:]) * sgn
        out[:, i * CY:(i + 1) * CY, :] = y.reshape(rows // CY, CY, HALVES)


def final_kernel(zb, tab, own, ends, skip, bias, out):
    lane = lax.broadcasted_iota(jnp.int32, (MODES, HALVES), 1)
    zero = jnp.zeros((CH, CH), F32)
    skip_t = jnp.transpose(skip[...])
    pair = jnp.concatenate(
        [jnp.concatenate([skip_t, zero], axis=1), jnp.concatenate([zero, skip_t], axis=1)], axis=0)
    col = jnp.concatenate([bias[...], bias[...]], axis=1)
    col = jnp.transpose(jnp.broadcast_to(col, (8, HALVES)))
    col = jnp.broadcast_to(col[:, 0:1], (HALVES, NZ))
    for x in range(CX):
        for yp in range(CY // 2):
            i = x * CY + 2 * yp
            u = zb[:, i, :]
            v = zb[:, i + 1, :]
            s = jnp.concatenate(
                [jnp.where(lane < CH, u, swap(v)), jnp.where(lane < CH, swap(u), v)], axis=0)
            spectral = mm(s, tab[...], TN, HIGH)
            lat = []
            for j in range(2):
                y = 2 * yp + j
                lat.append(ends[0, x] if y == 0 else ends[1, x] if y == CY - 1 else own[i + j])
            total = spectral + mm(pair, jnp.concatenate(lat, axis=0), NN, HIGH) + col
            out[x, 2 * yp:2 * yp + 2] = gelu(total).astype(BF16).reshape(2, CH, NZ)


def call(kernel, shapes, args, scratch=(), smem=False, name=None):
    specs = [pl.BlockSpec(memory_space=pltpu.VMEM)] * len(args)
    if smem:
        specs[0] = pl.BlockSpec(memory_space=pltpu.SMEM)
    return pl.pallas_call(
        kernel,
        out_shape=shapes,
        in_specs=specs,
        scratch_shapes=list(scratch),
        compiler_params=LIMIT,
        name=name,
    )(*args)


def shape(*dims):
    return jax.ShapeDtypeStruct(dims, F32)


def exchange(x, axis):
    return lax.all_to_all(x, axis, split_axis=0, concat_axis=0, tiled=True)


def moved(x, axis, step):
    devices = range(lax.axis_size(axis))
    return lax.ppermute(x, axis, [(i - step, i) for i in devices if i - step in devices])


def per_device(features, positions, home_cells, neighbours, degrees, lift_input, kernel_first,
               kernel_bias, kernel_second, spectral_weights, skip_weights, skip_bias):
    bins = lax.axis_size("bin")
    pens = lax.axis_size("pen")
    at = jnp.stack([lax.axis_index("bin"), lax.axis_index("pen")]).astype(jnp.int32)
    sides, low, high, middle = lift_points(
        at, (bins * CX - 1, pens * CY - 1), features.T, positions, home_cells, neighbours.T,
        degrees[None, :], lift_input, kernel_first, kernel_bias[None, :], kernel_second)
    below = moved(high, "bin", 1)
    above = moved(low, "bin", -1)
    half = shape(CX, CH, NZ)
    own, low_y, high_y = call(
        functools.partial(latent_kernel, bins - 1), [shape(CX * CY, CH, NZ), half, half],
        (at, sides, middle, below, above), smem=True, name="latent")
    left = moved(high_y, "pen", 1)
    right = moved(low_y, "pen", -1)
    table = jnp.asarray(z_forward_table())
    spec = call(inner_kernel, shape(MODES, CX * CY, HALVES), (table, own), name="forward_z")
    spec, ends = call(
        functools.partial(outer_kernel, pens - 1), [shape(*spec.shape), shape(2, CX, CH, NZ)],
        (at, table, own, spec, low_y, high_y, left, right), smem=True, name="forward_z_ends")
    r = exchange(spec.reshape(pens, 2 * CX * CY, HALVES), "pen")
    r = call(y_kernel, shape(MODES, 2 * CX, HALVES), (r, jnp.asarray(y_forward_table(pens))),
             name="forward_y")
    r = exchange(r, "bin")
    fwd, inv = x_tables(bins)
    r = call(x_kernel, shape(MODES, 2 * CX, HALVES),
             (r, jnp.asarray(fwd), jnp.asarray(inv), spectral_weights),
             scratch=[pltpu.VMEM((2 * MODES, 8, HALVES), F32)] * 2, name="mix_x")
    r = exchange(r, "bin")
    r = call(y_back_kernel, shape(pens, 2 * CX * CY, HALVES),
             (r, jnp.asarray(y_inverse_table(pens))), name="inverse_y")
    r = exchange(r, "pen")
    out = call(
        final_kernel, jax.ShapeDtypeStruct((CX, CY, CH, NZ), BF16),
        (r.reshape(MODES, CX * CY, HALVES), jnp.asarray(z_inverse_table()), own, ends,
         skip_weights, skip_bias[None, :]), name="finish")
    return out.transpose(0, 1, 3, 2)


def solution(mesh):
    in_specs = (
        P(("bin", "pen"), None),
        P(None, ("bin", "pen")),
        P(None, ("bin", "pen")),
        P(("bin", "pen"), None),
        P(("bin", "pen")),
        P(),
        P(),
        P(),
        P(),
        P(None, "bin", "pen", None, None),
        P(),
        P(),
    )
    out_specs = P("bin", "pen", None, None)
    return jax.shard_map(
        per_device, mesh=mesh, in_specs=in_specs, out_specs=out_specs, check_vma=False
    )
```

```python
import functools
import math

import jax
import jax.numpy as jnp
import numpy as np
from jax import lax
from jax.experimental import pallas as pl
from jax.experimental.pallas import tpu as pltpu
from jax.sharding import PartitionSpec as P

NZ = 192
CX = 4
CY = 8
PTS = 2048
CH = 64
MODES = 32
CHUNK = 256
SUB = 128
LARGE = 512
FIRST = 5
SECOND = 6
HALVES = 2 * CH

F32 = jnp.float32
BF16 = jnp.bfloat16
HIGH = lax.Precision.HIGH
LIMIT = pltpu.CompilerParams(vmem_limit_bytes=24 * 1024 * 1024)

NN = (((1,), (0,)), ((), ()))
NT = (((1,), (1,)), ((), ()))
TN = (((0,), (0,)), ((), ()))


def mm(a, b, dims=NN, precision=None):
    return lax.dot_general(a, b, dims, precision=precision, preferred_element_type=F32)


def gelu(x):
    inner = x * (0.7978845608028654 + 0.035677408136300125 * (x * x))
    half = 0.5 * x
    return half + half * jnp.tanh(inner)


def swap(x):
    return pltpu.roll(x, CH, 1)


def sign_row(shape):
    lane = lax.broadcasted_iota(jnp.int32, shape, 1)
    return jnp.where(lane < CH, 1.0, -1.0).astype(F32)


def tables(length, signed):
    mode = np.arange(MODES)
    if signed:
        mode = np.where(mode < MODES // 2, mode, mode - MODES)
    return mode


def angles(rows, length, signed):
    mode = tables(length, signed)
    phase = (np.asarray(rows)[:, None] * mode[None, :]) % length
    angle = phase * (2.0 * math.pi / length)
    scale = 1.0 / math.sqrt(length)
    return np.cos(angle) * scale, np.sin(angle) * scale


def z_forward_table():
    c, s = angles(np.arange(NZ), NZ, False)
    return np.concatenate([c.T, -s.T], axis=0).astype(np.float32)


def z_inverse_table():
    c, s = angles(np.arange(NZ), NZ, False)
    w = np.where(np.arange(MODES) == 0, 1.0, 2.0)[:, None]
    return np.concatenate([c.T * w, -s.T * w], axis=0).astype(np.float32)


def y_forward_table(pens):
    length = CY * pens
    c, s = angles(np.arange(length), length, True)
    return np.concatenate([c.T, s.T], axis=0).astype(np.float32)


def y_inverse_table(pens):
    length = CY * pens
    c, s = angles(np.arange(length), length, True)
    return np.concatenate([c, s], axis=0).astype(np.float32)


def x_tables(bins):
    length = CX * bins
    c, s = angles(np.arange(length), length, True)
    fwd = np.zeros((2, 2, MODES, bins, 2, CX))
    inv = np.zeros((2, bins, 2, CX, 2, MODES))
    for k in range(2):
        fwd[0, k, :, :, k, :] = c.T.reshape(MODES, bins, CX)
        fwd[1, k, :, :, k, :] = s.T.reshape(MODES, bins, CX)
        inv[0, :, k, :, k, :] = c.reshape(bins, CX, MODES)
        inv[1, :, k, :, k, :] = s.reshape(bins, CX, MODES)
    fwd = fwd.reshape(4 * MODES, bins * 2 * CX)
    inv = inv.reshape(2 * bins * 2 * CX, 2 * MODES)
    return fwd.astype(np.float32), inv.astype(np.float32)


def pieces(x):
    hi = x.astype(BF16).astype(F32)
    rest = x - hi
    mid = rest.astype(BF16).astype(F32)
    return hi, mid, rest - mid


SIDE = 2 * CY
BOTH = SIDE + 4


def column_rank(hx, hy):
    side = jnp.where(hx == 0, 0, CY) + hy
    end = SIDE + (hx - 1) * 2 + jnp.where(hy == 0, 0, 1)
    core = BOTH + (hx - 1) * (CY - 2) + hy - 1
    inner = jnp.where((hy == 0) | (hy == CY - 1), end, core)
    return jnp.where((hx == 0) | (hx == CX - 1), side, inner)


def column_x(o):
    inner = jnp.where(o < BOTH, jnp.where(o < SIDE + 2, 1, 2), jnp.where(o < BOTH + CY - 2, 1, 2))
    return jnp.where(o < CY, 0, jnp.where(o < SIDE, CX - 1, inner))


def column_y(o):
    side = jnp.where(o < CY, o, o - CY)
    end = jnp.where((o == SIDE) | (o == SIDE + 2), 0, CY - 1)
    core = jnp.where(o < BOTH + CY - 2, o - BOTH, o - (BOTH + CY - 2)) + 1
    return jnp.where(o < SIDE, side, jnp.where(o < BOTH, end, core))


def add_chunk(last, at, base, size, plane0, data, rankb, taps, quad, lift_t, mess, keys, grid):
    lanes = lax.broadcasted_iota(jnp.int32, (PTS, 128), 1) + base
    perm = jnp.concatenate(
        [jnp.where(rankb[...] == lanes + j * 128, 1.0, 0.0).astype(BF16)
         for j in range(size // 128)], axis=1)
    t = mm(data[...], perm)
    hzs = t[73:74]
    cols = t[74:75]
    spans = [(jnp.min(cols[:, j * SUB:(j + 1) * SUB]).astype(jnp.int32),
              jnp.max(cols[:, j * SUB:(j + 1) * SUB]).astype(jnp.int32) + 1)
             for j in range(size // SUB)]
    key = 256.0 * cols
    key = jnp.concatenate(
        [key + jnp.maximum(hzs - 1.0, 0.0), key + hzs, key + jnp.minimum(hzs + 1.0, NZ - 1.0),
         jnp.zeros((5, size), F32)], axis=0)
    key = jnp.transpose(key)
    for dz in range(3):
        keys[dz, 0:size] = jnp.broadcast_to(key[:, dz:dz + 1], (size, NZ))

    values = mm(lift_t[...], t[0:64].astype(BF16))
    ox = t[64:65] + t[65:66] + t[66:67]
    oy = t[67:68] + t[68:69] + t[69:70]
    oz = t[70:71] + t[71:72] + t[72:73]
    coli = cols.astype(jnp.int32)
    gx = column_x(coli) + at[0] * CX
    gy = column_y(coli) + at[1] * CY
    k_x, k_y, k_z, k_b = (taps[j, :, 0:size] for j in range(4))

    def ends(g, end):
        return (jnp.where(g > 0, -1.0, 0.0), None, jnp.where(g < end, 1.0, 0.0))

    base_pre = k_x * ox + k_y * oy + k_z * oz + k_b
    ex = ends(gx, last[0])
    ey = ends(gy, last[1])
    ez = ends(hzs, NZ - 1.0)
    pend = []

    def flush():
        while len(pend) < 4:
            pend.append((None, jnp.zeros((CH, size), BF16)))
        kern = mm(quad[...], jnp.concatenate([h for _, h in pend], axis=0))
        for j, (where, _) in enumerate(pend):
            if where is None:
                continue
            dx, dy, dz = where
            k = dx * 9 + dy * 3 + dz
            m = kern[j * CH:(j + 1) * CH] * (values * t[80 + k:81 + k])
            hi = m.astype(BF16)
            r = (dx * 3 + dy) * CH
            for s in range(size // SUB):
                cut = slice(s * SUB, (s + 1) * SUB)
                mess[s, r:r + CH, dz * SUB:(dz + 1) * SUB] = hi[:, cut]
        pend.clear()

    for dx in range(3):
        pre_x = base_pre if ex[dx] is None else base_pre + ex[dx] * k_x
        for dy in range(3):
            pre_y = pre_x if ey[dy] is None else pre_x + ey[dy] * k_y
            for dz in range(3):
                pre = pre_y if ez[dz] is None else pre_y + ez[dz] * k_z
                pend.append(((dx, dy, dz), gelu(pre).astype(BF16)))
                if len(pend) == 4:
                    flush()
    flush()

    lane = lax.broadcasted_iota(jnp.int32, (SUB, NZ), 1).astype(F32)
    longest = spans[0][1] - spans[0][0]
    for begin, end in spans[1:]:
        longest = jnp.maximum(longest, end - begin)

    def column(j, _):
        results = []
        for s, (begin, end) in enumerate(spans):
            c = jnp.minimum(begin + j, end - 1)
            goal = lane + jnp.where(begin + j < end, 256.0 * c.astype(F32), -1.0e6)
            hot = jnp.concatenate(
                [jnp.where(keys[dz, s * SUB:(s + 1) * SUB] == goal, 1.0, 0.0).astype(BF16)
                 for dz in range(3)], axis=0)
            results.append((c, [mm(mess[s, q * 3 * CH:(q + 1) * 3 * CH], hot) for q in range(3)]))
        for c, acc in results:
            cx = column_x(c) - plane0
            cy = column_y(c)
            for dx in range(3):
                for dy in range(3):
                    grid[cx + dx, cy + dy] += acc[dx][dy * CH:(dy + 1) * CH]
        return 0

    lax.fori_loop(0, longest, column, 0)


def sides_kernel(last, at, feat_h, pos_h, home_h, nbr_h, deg_h, lift_h, first_h, bias_h, second_h,
                 grid, low, high, data, rankb, taps, quad, lift_t, span_a, span_b,
                 pos, home, nbr, deg, lift, first, bias, second, mess, keys, sems):
    pairs = [(home_h, home), (pos_h, pos), (nbr_h, nbr), (deg_h, deg),
             (feat_h, data.at[0:64]), (lift_h, lift), (first_h, first), (bias_h, bias),
             (second_h, second)]
    copies = [pltpu.make_async_copy(a, b, sems.at[i]) for i, (a, b) in enumerate(pairs)]
    for c in copies:
        c.start()
    grid[...] = jnp.zeros_like(grid)
    tri = jnp.where(
        lax.broadcasted_iota(jnp.int32, (CHUNK, CHUNK), 0)
        < lax.broadcasted_iota(jnp.int32, (CHUNK, CHUNK), 1), 1.0, 0.0).astype(BF16)
    for c in copies:
        c.wait()
    hx = home[0:1, :]
    hy = home[1:2, :]
    hz = home[2:3, :]
    col = column_rank(hx, hy)

    def blocks(limit, least):
        n = jnp.sum(jnp.where(col < limit, 1.0, 0.0)).astype(jnp.int32)
        return jnp.maximum((n + CHUNK - 1) // CHUNK, least)

    split = blocks(SIDE, FIRST)
    later = jnp.maximum(blocks(BOTH, SECOND), split)
    span_a[0] = split
    span_a[1] = later
    span_b[0] = later
    span_b[1] = PTS // CHUNK

    ids = lax.broadcasted_iota(jnp.int32, (CX * CY, PTS), 0)
    carry = jnp.sum(jnp.where(col < ids, 1.0, 0.0), axis=1, keepdims=True)
    for blk in range(PTS // CHUNK):
        part = slice(blk * CHUNK, (blk + 1) * CHUNK)
        hot = jnp.where(col[:, part] == ids[:, part], 1.0, 0.0)
        ahead = mm(hot.astype(BF16), tri) + carry
        rank = jnp.sum(hot * ahead, axis=0, keepdims=True)
        rank = jnp.transpose(jnp.broadcast_to(rank, (8, CHUNK)))
        rankb[part, :] = jnp.broadcast_to(rank[:, 0:1], (CHUNK, 128)).astype(jnp.int32)
        carry = carry + jnp.sum(hot, axis=1, keepdims=True)

    slot = lax.broadcasted_iota(jnp.int32, (16, PTS), 0)
    bits = jnp.sum(
        jnp.where(slot < deg[...], jnp.left_shift(1, nbr[...]), 0), axis=0, keepdims=True)
    code = lax.broadcasted_iota(jnp.int32, (32, PTS), 0)
    live = jnp.bitwise_and(jnp.right_shift(bits, code), 1).astype(F32)
    off_x = (hx + at[0] * CX).astype(F32) + 0.5 - pos[0:1, :]
    off_y = (hy + at[1] * CY).astype(F32) + 0.5 - pos[1:2, :]
    off_z = hz.astype(F32) + 0.5 - pos[2:3, :]
    rows = [*pieces(off_x), *pieces(off_y), *pieces(off_z), hz.astype(F32), col.astype(F32),
            jnp.zeros((5, PTS), F32)]
    data[64:80, :] = jnp.concatenate(rows, axis=0).astype(BF16)
    data[80:112, :] = live.astype(BF16)

    flat = jnp.concatenate([first[...], bias[...], jnp.zeros((4, CH), F32)], axis=0)
    flat = jnp.concatenate([flat, jnp.zeros((8, 128 - CH), F32)], axis=1)
    flat = jnp.transpose(flat)
    for j in range(4):
        taps[j] = jnp.broadcast_to(flat[0:CH, j:j + 1], (CH, LARGE))
    zero = jnp.zeros((CH, CH), F32)
    sec_t = jnp.transpose(second[...].astype(F32))
    quad[...] = jnp.concatenate(
        [jnp.concatenate([sec_t if i == j else zero for j in range(4)], axis=1)
         for i in range(4)], axis=0).astype(BF16)
    lift_t[...] = jnp.transpose(lift[...].astype(F32)).astype(BF16)

    def chunk(size, first, step, _):
        add_chunk(last, at, first + step * size, size, 0, data, rankb, taps, quad, lift_t, mess,
                  keys, grid)
        return 0

    large = split // 2
    lax.fori_loop(0, large, functools.partial(chunk, LARGE, 0), 0)
    lax.fori_loop(0, split - 2 * large, functools.partial(chunk, CHUNK, large * LARGE), 0)
    low[...] = grid[0]
    high[...] = grid[CX + 1]


def middle_kernel(last, at, span, data, rankb, taps, quad, lift_t, grid, mess, keys):
    grid[...] = jnp.zeros_like(grid)

    def chunk(size, first, step, _):
        add_chunk(last, at, first + step * size, size, 1, data, rankb, taps, quad, lift_t, mess,
                  keys, grid)
        return 0

    split = span[0]
    odd = jnp.bitwise_and(span[1] - split, 1)
    large = (span[1] - split) // 2
    lax.fori_loop(0, odd, functools.partial(chunk, CHUNK, split * CHUNK), 0)
    lax.fori_loop(0, large, functools.partial(chunk, LARGE, (split + odd) * CHUNK), 0)


def lift_points(at, last, feat, pos, home, nbr, deg, lift, first, bias, second):
    vmem = pl.BlockSpec(memory_space=pltpu.VMEM)
    smem = pl.BlockSpec(memory_space=pltpu.SMEM)
    work = [
        pltpu.VMEM((LARGE // SUB, 9 * CH, 3 * SUB), BF16),
        pltpu.VMEM((3, LARGE, NZ), F32),
    ]
    inputs = tuple(
        pltpu.with_memory_space_constraint(x, pltpu.HBM)
        for x in (feat, pos, home, nbr, deg, lift, first, bias, second))
    grid, low, high, *prepared, span_a, span_b = pl.pallas_call(
        functools.partial(sides_kernel, last),
        out_shape=[
            shape(CX + 2, CY + 2, CH, NZ),
            shape(CY + 2, CH, NZ),
            shape(CY + 2, CH, NZ),
            jax.ShapeDtypeStruct((112, PTS), BF16),
            jax.ShapeDtypeStruct((PTS, 128), jnp.int32),
            shape(4, CH, LARGE),
            jax.ShapeDtypeStruct((4 * CH, 4 * CH), BF16),
            jax.ShapeDtypeStruct((CH, CH), BF16),
            jax.ShapeDtypeStruct((2,), jnp.int32),
            jax.ShapeDtypeStruct((2,), jnp.int32),
        ],
        in_specs=[smem] + [pl.BlockSpec(memory_space=pltpu.HBM)] * len(inputs),
        out_specs=[vmem] * 8 + [smem, smem],
        scratch_shapes=[pltpu.VMEM(x.shape, x.dtype) for x in inputs[1:]] + work
        + [pltpu.SemaphoreType.DMA((len(inputs),))],
        compiler_params=LIMIT,
        name="lift_sides",
    )(at, *inputs)
    return grid, low, high, prepared, span_a, span_b


def lift_inner(at, last, span, prepared, name):
    vmem = pl.BlockSpec(memory_space=pltpu.VMEM)
    smem = pl.BlockSpec(memory_space=pltpu.SMEM)
    return pl.pallas_call(
        functools.partial(middle_kernel, last),
        out_shape=shape(CX, CY + 2, CH, NZ),
        in_specs=[smem, smem] + [vmem] * 5,
        out_specs=vmem,
        scratch_shapes=[
            pltpu.VMEM((LARGE // SUB, 9 * CH, 3 * SUB), BF16),
            pltpu.VMEM((3, LARGE, NZ), F32),
        ],
        compiler_params=LIMIT,
        name=name,
    )(at, span, *prepared)


def ends_kernel(last, at, sides, middle, below, above, low_y, high_y):
    low = at[0] == 0
    top = at[0] == last
    for y, out in ((0, low_y), (CY + 1, high_y)):
        for x in range(CX):
            l = sides[x + 1, y] + middle[x, y]
            if x == 0:
                l = l + jnp.where(low, sides[0, y], below[y])
            if x == CX - 1:
                l = l + jnp.where(top, sides[CX + 1, y], above[y])
            out[x] = l


def z_modes(table, pair):
    lane = lax.broadcasted_iota(jnp.int32, (MODES, HALVES), 1)
    d = mm(table, pair, NT, HIGH)
    re, im = d[0:MODES], d[MODES:]
    return jnp.where(lane < CH, re, swap(im)), jnp.where(lane < CH, swap(re), im)


def latent_kernel(last, at, tabz, sides, middle, rest, below, above, low_y, high_y, left, right,
                  spec, own):
    low = at[0] == 0
    top = at[0] == last[0]
    first_pen = at[1] == 0
    last_pen = at[1] == last[1]
    table = tabz[...]
    for x in range(CX):
        for yp in range(CY // 2):
            i = x * CY + 2 * yp
            for j in range(2):
                y = 2 * yp + j + 1
                l = sides[x + 1, y] + middle[x, y] + rest[x, y]
                if x == 0:
                    l = l + jnp.where(low, sides[0, y], below[y])
                if x == CX - 1:
                    l = l + jnp.where(top, sides[CX + 1, y], above[y])
                if y == 1:
                    l = l + jnp.where(first_pen, low_y[x], left[x])
                if y == CY:
                    l = l + jnp.where(last_pen, high_y[x], right[x])
                own[i + j] = l
            u, v = z_modes(table, own[i:i + 2].reshape(2 * CH, NZ))
            spec[:, i, :] = u
            spec[:, i + 1, :] = v


def y_kernel(r, main, out):
    sgn = sign_row((MODES, HALVES))
    pens = r.shape[0]
    for i in range(2 * CX):
        rows = r[:, i * CY:(i + 1) * CY, :].reshape(pens * CY, HALVES)
        ab = mm(main[...], rows, NN, HIGH)
        out[:, i, :] = ab[:MODES] + swap(ab[MODES:]) * sgn


def x_kernel(r, fwd, inv, w, out, lhs, res):
    rows = r.shape[0] * r.shape[1]
    modes = 2 * MODES
    sgn = sign_row((modes, HALVES))
    ab = mm(fwd[...], r[...].reshape(rows, HALVES), NN, HIGH)
    x = ab[:modes] + swap(ab[modes:]) * sgn
    parts = [*pieces(x), *pieces(swap(x))]
    lhs[...] = jnp.zeros_like(lhs)
    for j, p in enumerate(parts):
        lhs[:, j, :] = p
    for k in range(2):
        for j in range(MODES):
            m = k * MODES + j
            res[m] = mm(lhs[m][:, 0:CH].astype(BF16), w[j, 0, k])
    re = res[:, 0, :] + res[:, 1, :] + res[:, 2, :]
    im = res[:, 3, :] + res[:, 4, :] + res[:, 5, :]
    mixed = re - swap(im) * sgn
    ab = mm(inv[...], mixed, NN, HIGH)
    a, b = ab[:rows], ab[rows:]
    y = a - swap(b) * sign_row((rows, HALVES))
    out[...] = y.reshape(out.shape)


def y_back_kernel(r, inv, out):
    rows = inv.shape[0] // 2
    sgn = sign_row((rows, HALVES))
    for i in range(2 * CX):
        ab = mm(inv[...], r[:, i, :], NN, HIGH)
        y = ab[:rows] - swap(ab[rows:]) * sgn
        out[:, i * CY:(i + 1) * CY, :] = y.reshape(rows // CY, CY, HALVES)


def final_kernel(zb, tab, own, skip, bias, out):
    lane = lax.broadcasted_iota(jnp.int32, (MODES, HALVES), 1)
    zero = jnp.zeros((CH, CH), F32)
    skip_t = jnp.transpose(skip[...])
    pair = jnp.concatenate(
        [jnp.concatenate([skip_t, zero], axis=1), jnp.concatenate([zero, skip_t], axis=1)], axis=0)
    col = jnp.concatenate([bias[...], bias[...]], axis=1)
    col = jnp.transpose(jnp.broadcast_to(col, (8, HALVES)))
    col = jnp.broadcast_to(col[:, 0:1], (HALVES, NZ))
    for x in range(CX):
        for yp in range(CY // 2):
            i = x * CY + 2 * yp
            u = zb[:, i, :]
            v = zb[:, i + 1, :]
            s = jnp.concatenate(
                [jnp.where(lane < CH, u, swap(v)), jnp.where(lane < CH, swap(u), v)], axis=0)
            spectral = mm(s, tab[...], TN, HIGH)
            lat = own[i:i + 2].reshape(2 * CH, NZ)
            total = spectral + mm(pair, lat, NN, HIGH) + col
            out[x, 2 * yp:2 * yp + 2] = gelu(total).astype(BF16).reshape(2, CH, NZ)


def call(kernel, shapes, args, scratch=(), smem=False, name=None):
    specs = [pl.BlockSpec(memory_space=pltpu.VMEM)] * len(args)
    if smem:
        specs[0] = pl.BlockSpec(memory_space=pltpu.SMEM)
    return pl.pallas_call(
        kernel,
        out_shape=shapes,
        in_specs=specs,
        scratch_shapes=list(scratch),
        compiler_params=LIMIT,
        name=name,
    )(*args)


def shape(*dims):
    return jax.ShapeDtypeStruct(dims, F32)


def exchange(x, axis):
    return lax.all_to_all(x, axis, split_axis=0, concat_axis=0, tiled=True)


def moved(x, axis, step):
    devices = range(lax.axis_size(axis))
    return lax.ppermute(x, axis, [(i - step, i) for i in devices if i - step in devices])


def per_device(features, positions, home_cells, neighbours, degrees, lift_input, kernel_first,
               kernel_bias, kernel_second, spectral_weights, skip_weights, skip_bias):
    bins = lax.axis_size("bin")
    pens = lax.axis_size("pen")
    at = jnp.stack([lax.axis_index("bin"), lax.axis_index("pen")]).astype(jnp.int32)
    last = (bins * CX - 1, pens * CY - 1)
    sides, low, high, prepared, span_a, span_b = lift_points(
        at, last, features.T, positions, home_cells, neighbours.T,
        degrees[None, :], lift_input, kernel_first, kernel_bias[None, :], kernel_second)
    below = moved(high, "bin", 1)
    above = moved(low, "bin", -1)
    middle = lift_inner(at, last, span_a, prepared, "lift_ends")
    half = shape(CX, CH, NZ)
    low_y, high_y = call(
        functools.partial(ends_kernel, bins - 1), [half, half],
        (at, sides, middle, below, above), smem=True, name="y_ends")
    left = moved(high_y, "pen", 1)
    right = moved(low_y, "pen", -1)
    rest = lift_inner(at, last, span_b, prepared, "lift_core")
    spec, own = call(
        functools.partial(latent_kernel, (bins - 1, pens - 1)),
        [shape(MODES, CX * CY, HALVES), shape(CX * CY, CH, NZ)],
        (at, jnp.asarray(z_forward_table()), sides, middle, rest, below, above, low_y, high_y,
         left, right), smem=True, name="latent_z")
    r = exchange(spec.reshape(pens, 2 * CX * CY, HALVES), "pen")
    r = call(y_kernel, shape(MODES, 2 * CX, HALVES), (r, jnp.asarray(y_forward_table(pens))),
             name="forward_y")
    r = exchange(r, "bin")
    fwd, inv = x_tables(bins)
    r = call(x_kernel, shape(MODES, 2 * CX, HALVES),
             (r, jnp.asarray(fwd), jnp.asarray(inv), spectral_weights),
             scratch=[pltpu.VMEM((2 * MODES, 8, HALVES), F32)] * 2, name="mix_x")
    r = exchange(r, "bin")
    r = call(y_back_kernel, shape(pens, 2 * CX * CY, HALVES),
             (r, jnp.asarray(y_inverse_table(pens))), name="inverse_y")
    r = exchange(r, "pen")
    out = call(
        final_kernel, jax.ShapeDtypeStruct((CX, CY, CH, NZ), BF16),
        (r.reshape(MODES, CX * CY, HALVES), jnp.asarray(z_inverse_table()), own,
         skip_weights, skip_bias[None, :]), name="finish")
    return out.transpose(0, 1, 3, 2)


def solution(mesh):
    in_specs = (
        P(("bin", "pen"), None),
        P(None, ("bin", "pen")),
        P(None, ("bin", "pen")),
        P(("bin", "pen"), None),
        P(("bin", "pen")),
        P(),
        P(),
        P(),
        P(),
        P(None, "bin", "pen", None, None),
        P(),
        P(),
    )
    out_specs = P("bin", "pen", None, None)
    return jax.shard_map(
        per_device, mesh=mesh, in_specs=in_specs, out_specs=out_specs, check_vma=False
    )
```

```python
import functools
import math

import jax
import jax.numpy as jnp
import numpy as np
from jax import lax
from jax.experimental import pallas as pl
from jax.experimental.pallas import tpu as pltpu
from jax.sharding import PartitionSpec as P

NZ = 192
CX = 4
CY = 8
PTS = 2048
CH = 64
MODES = 32
CHUNK = 256
SUB = 128
LARGE = 512
FIRST = 5
SECOND = 7
HALVES = 2 * CH

F32 = jnp.float32
BF16 = jnp.bfloat16
HIGH = lax.Precision.HIGH
LIMIT = pltpu.CompilerParams(vmem_limit_bytes=24 * 1024 * 1024)

NN = (((1,), (0,)), ((), ()))
NT = (((1,), (1,)), ((), ()))
TN = (((0,), (0,)), ((), ()))


def mm(a, b, dims=NN, precision=None):
    return lax.dot_general(a, b, dims, precision=precision, preferred_element_type=F32)


def gelu(x):
    inner = x * (0.7978845608028654 + 0.035677408136300125 * (x * x))
    half = 0.5 * x
    return half + half * jnp.tanh(inner)


def swap(x):
    return pltpu.roll(x, CH, 1)


def sign_row(shape):
    lane = lax.broadcasted_iota(jnp.int32, shape, 1)
    return jnp.where(lane < CH, 1.0, -1.0).astype(F32)


def tables(length, signed):
    mode = np.arange(MODES)
    if signed:
        mode = np.where(mode < MODES // 2, mode, mode - MODES)
    return mode


def angles(rows, length, signed):
    mode = tables(length, signed)
    phase = (np.asarray(rows)[:, None] * mode[None, :]) % length
    angle = phase * (2.0 * math.pi / length)
    scale = 1.0 / math.sqrt(length)
    return np.cos(angle) * scale, np.sin(angle) * scale


def z_forward_table():
    c, s = angles(np.arange(NZ), NZ, False)
    return np.concatenate([c.T, -s.T], axis=0).astype(np.float32)


def z_inverse_table():
    c, s = angles(np.arange(NZ), NZ, False)
    w = np.where(np.arange(MODES) == 0, 1.0, 2.0)[:, None]
    return np.concatenate([c.T * w, -s.T * w], axis=0).astype(np.float32)


def y_forward_table(pens):
    length = CY * pens
    c, s = angles(np.arange(length), length, True)
    return np.concatenate([c.T, s.T], axis=0).astype(np.float32)


def y_inverse_table(pens):
    length = CY * pens
    c, s = angles(np.arange(length), length, True)
    return np.concatenate([c, s], axis=0).astype(np.float32)


def x_tables(bins):
    length = CX * bins
    c, s = angles(np.arange(length), length, True)
    fwd = np.zeros((2, 2, MODES, bins, 2, CX))
    inv = np.zeros((2, bins, 2, CX, 2, MODES))
    for k in range(2):
        fwd[0, k, :, :, k, :] = c.T.reshape(MODES, bins, CX)
        fwd[1, k, :, :, k, :] = s.T.reshape(MODES, bins, CX)
        inv[0, :, k, :, k, :] = c.reshape(bins, CX, MODES)
        inv[1, :, k, :, k, :] = s.reshape(bins, CX, MODES)
    fwd = fwd.reshape(4 * MODES, bins * 2 * CX)
    inv = inv.reshape(2 * bins * 2 * CX, 2 * MODES)
    return fwd.astype(np.float32), inv.astype(np.float32)


def pack(cells):
    tail = cells[:, 128:NZ]
    half = CH // 2
    return jnp.concatenate(
        [cells[:, 0:128], jnp.concatenate([tail[0:half], tail[half:CH]], axis=1)], axis=0)


def unpack(rows):
    tail = rows[CH:]
    tail = jnp.concatenate([tail[:, 0:NZ - 128], tail[:, NZ - 128:]], axis=0)
    return jnp.concatenate([rows[0:CH], tail], axis=1)


def pieces(x):
    hi = x.astype(BF16).astype(F32)
    rest = x - hi
    mid = rest.astype(BF16).astype(F32)
    return hi, mid, rest - mid


PACKED = CH * NZ // 128
SIDE = 2 * CY
BOTH = SIDE + 4


def column_rank(hx, hy):
    side = jnp.where(hx == 0, 0, CY) + hy
    end = SIDE + (hx - 1) * 2 + jnp.where(hy == 0, 0, 1)
    core = BOTH + (hx - 1) * (CY - 2) + hy - 1
    inner = jnp.where((hy == 0) | (hy == CY - 1), end, core)
    return jnp.where((hx == 0) | (hx == CX - 1), side, inner)


def column_x(o):
    inner = jnp.where(o < BOTH, jnp.where(o < SIDE + 2, 1, 2), jnp.where(o < BOTH + CY - 2, 1, 2))
    return jnp.where(o < CY, 0, jnp.where(o < SIDE, CX - 1, inner))


def column_y(o):
    side = jnp.where(o < CY, o, o - CY)
    end = jnp.where((o == SIDE) | (o == SIDE + 2), 0, CY - 1)
    core = jnp.where(o < BOTH + CY - 2, o - BOTH, o - (BOTH + CY - 2)) + 1
    return jnp.where(o < SIDE, side, jnp.where(o < BOTH, end, core))


def add_chunk(last, at, base, size, plane0, data, rankb, taps, quad, lift_t, mess, keys, grid):
    lanes = lax.broadcasted_iota(jnp.int32, (PTS, 128), 1) + base
    perm = jnp.concatenate(
        [jnp.where(rankb[...] == lanes + j * 128, 1.0, 0.0).astype(BF16)
         for j in range(size // 128)], axis=1)
    t = mm(data[...], perm)
    hzs = t[73:74]
    cols = t[74:75]
    spans = [(jnp.min(cols[:, j * SUB:(j + 1) * SUB]).astype(jnp.int32),
              jnp.max(cols[:, j * SUB:(j + 1) * SUB]).astype(jnp.int32) + 1)
             for j in range(size // SUB)]
    key = 256.0 * cols
    key = jnp.concatenate(
        [key + jnp.maximum(hzs - 1.0, 0.0), key + hzs, key + jnp.minimum(hzs + 1.0, NZ - 1.0),
         jnp.zeros((5, size), F32)], axis=0)
    key = jnp.transpose(key)
    for dz in range(3):
        keys[dz, 0:size] = jnp.broadcast_to(key[:, dz:dz + 1], (size, NZ))

    values = mm(lift_t[...], t[0:64].astype(BF16))
    ox = t[64:65] + t[65:66] + t[66:67]
    oy = t[67:68] + t[68:69] + t[69:70]
    oz = t[70:71] + t[71:72] + t[72:73]
    coli = cols.astype(jnp.int32)
    gx = column_x(coli) + at[0] * CX
    gy = column_y(coli) + at[1] * CY
    k_x, k_y, k_z, k_b = (taps[j, :, 0:size] for j in range(4))

    def ends(g, end):
        return (jnp.where(g > 0, -1.0, 0.0), None, jnp.where(g < end, 1.0, 0.0))

    base_pre = k_x * ox + k_y * oy + k_z * oz + k_b
    ex = ends(gx, last[0])
    ey = ends(gy, last[1])
    ez = ends(hzs, NZ - 1.0)
    pend = []

    def flush():
        while len(pend) < 4:
            pend.append((None, jnp.zeros((CH, size), BF16)))
        kern = mm(quad[...], jnp.concatenate([h for _, h in pend], axis=0))
        for j, (where, _) in enumerate(pend):
            if where is None:
                continue
            dx, dy, dz = where
            k = dx * 9 + dy * 3 + dz
            m = kern[j * CH:(j + 1) * CH] * (values * t[80 + k:81 + k])
            hi = m.astype(BF16)
            r = (dx * 3 + dy) * CH
            for s in range(size // SUB):
                cut = slice(s * SUB, (s + 1) * SUB)
                mess[s, r:r + CH, dz * SUB:(dz + 1) * SUB] = hi[:, cut]
        pend.clear()

    for dx in range(3):
        pre_x = base_pre if ex[dx] is None else base_pre + ex[dx] * k_x
        for dy in range(3):
            pre_y = pre_x if ey[dy] is None else pre_x + ey[dy] * k_y
            for dz in range(3):
                pre = pre_y if ez[dz] is None else pre_y + ez[dz] * k_z
                pend.append(((dx, dy, dz), gelu(pre).astype(BF16)))
                if len(pend) == 4:
                    flush()
    flush()

    lane = lax.broadcasted_iota(jnp.int32, (SUB, NZ), 1).astype(F32)
    longest = spans[0][1] - spans[0][0]
    for begin, end in spans[1:]:
        longest = jnp.maximum(longest, end - begin)

    def column(j, _):
        results = []
        for s, (begin, end) in enumerate(spans):
            c = jnp.minimum(begin + j, end - 1)
            goal = lane + jnp.where(begin + j < end, 256.0 * c.astype(F32), -1.0e6)
            hot = jnp.concatenate(
                [jnp.where(keys[dz, s * SUB:(s + 1) * SUB] == goal, 1.0, 0.0).astype(BF16)
                 for dz in range(3)], axis=0)
            results.append((c, [mm(mess[s, q * 3 * CH:(q + 1) * 3 * CH], hot) for q in range(3)]))
        for c, acc in results:
            cx = column_x(c) - plane0
            cy = column_y(c)
            for dx in range(3):
                for dy in range(3):
                    grid[cx + dx, cy + dy] += acc[dx][dy * CH:(dy + 1) * CH]
        return 0

    lax.fori_loop(0, longest, column, 0)


def sides_kernel(last, at, feat_h, pos_h, home_h, nbr_h, deg_h, lift_h, first_h, bias_h, second_h,
                 grid, low, high, data, rankb, taps, quad, lift_t, span_a, span_b,
                 pos, home, nbr, deg, lift, first, bias, second, mess, keys, sems):
    pairs = [(home_h, home), (pos_h, pos), (nbr_h, nbr), (deg_h, deg),
             (feat_h, data.at[0:64]), (lift_h, lift), (first_h, first), (bias_h, bias),
             (second_h, second)]
    copies = [pltpu.make_async_copy(a, b, sems.at[i]) for i, (a, b) in enumerate(pairs)]
    for c in copies:
        c.start()
    grid[...] = jnp.zeros_like(grid)
    tri = jnp.where(
        lax.broadcasted_iota(jnp.int32, (CHUNK, CHUNK), 0)
        < lax.broadcasted_iota(jnp.int32, (CHUNK, CHUNK), 1), 1.0, 0.0).astype(BF16)
    for c in copies:
        c.wait()
    hx = home[0:1, :]
    hy = home[1:2, :]
    hz = home[2:3, :]
    col = column_rank(hx, hy)

    def blocks(limit, least):
        n = jnp.sum(jnp.where(col < limit, 1.0, 0.0)).astype(jnp.int32)
        return jnp.maximum((n + CHUNK - 1) // CHUNK, least)

    split = blocks(SIDE, FIRST)
    later = jnp.maximum(blocks(BOTH, SECOND), split)
    span_a[0] = split
    span_a[1] = later
    span_b[0] = later
    span_b[1] = PTS // CHUNK

    ids = lax.broadcasted_iota(jnp.int32, (CX * CY, PTS), 0)
    carry = jnp.sum(jnp.where(col < ids, 1.0, 0.0), axis=1, keepdims=True)
    for blk in range(PTS // CHUNK):
        part = slice(blk * CHUNK, (blk + 1) * CHUNK)
        hot = jnp.where(col[:, part] == ids[:, part], 1.0, 0.0)
        ahead = mm(hot.astype(BF16), tri) + carry
        rank = jnp.sum(hot * ahead, axis=0, keepdims=True)
        rank = jnp.transpose(jnp.broadcast_to(rank, (8, CHUNK)))
        rankb[part, :] = jnp.broadcast_to(rank[:, 0:1], (CHUNK, 128)).astype(jnp.int32)
        carry = carry + jnp.sum(hot, axis=1, keepdims=True)

    slot = lax.broadcasted_iota(jnp.int32, (16, PTS), 0)
    bits = jnp.sum(
        jnp.where(slot < deg[...], jnp.left_shift(1, nbr[...]), 0), axis=0, keepdims=True)
    code = lax.broadcasted_iota(jnp.int32, (32, PTS), 0)
    live = jnp.bitwise_and(jnp.right_shift(bits, code), 1).astype(F32)
    off_x = (hx + at[0] * CX).astype(F32) + 0.5 - pos[0:1, :]
    off_y = (hy + at[1] * CY).astype(F32) + 0.5 - pos[1:2, :]
    off_z = hz.astype(F32) + 0.5 - pos[2:3, :]
    rows = [*pieces(off_x), *pieces(off_y), *pieces(off_z), hz.astype(F32), col.astype(F32),
            jnp.zeros((5, PTS), F32)]
    data[64:80, :] = jnp.concatenate(rows, axis=0).astype(BF16)
    data[80:112, :] = live.astype(BF16)

    flat = jnp.concatenate([first[...], bias[...], jnp.zeros((4, CH), F32)], axis=0)
    flat = jnp.concatenate([flat, jnp.zeros((8, 128 - CH), F32)], axis=1)
    flat = jnp.transpose(flat)
    for j in range(4):
        taps[j] = jnp.broadcast_to(flat[0:CH, j:j + 1], (CH, LARGE))
    zero = jnp.zeros((CH, CH), F32)
    sec_t = jnp.transpose(second[...].astype(F32))
    quad[...] = jnp.concatenate(
        [jnp.concatenate([sec_t if i == j else zero for j in range(4)], axis=1)
         for i in range(4)], axis=0).astype(BF16)
    lift_t[...] = jnp.transpose(lift[...].astype(F32)).astype(BF16)

    def chunk(size, first, step, _):
        add_chunk(last, at, first + step * size, size, 0, data, rankb, taps, quad, lift_t, mess,
                  keys, grid)
        return 0

    large = split // 2
    lax.fori_loop(0, large, functools.partial(chunk, LARGE, 0), 0)
    lax.fori_loop(0, split - 2 * large, functools.partial(chunk, CHUNK, large * LARGE), 0)
    for y in range(CY + 2):
        low[y] = pack(grid[0, y])
        high[y] = pack(grid[CX + 1, y])


def middle_kernel(last, at, span, data, rankb, taps, quad, lift_t, grid, mess, keys):
    grid[...] = jnp.zeros_like(grid)

    def chunk(size, first, step, _):
        add_chunk(last, at, first + step * size, size, 1, data, rankb, taps, quad, lift_t, mess,
                  keys, grid)
        return 0

    split = span[0]
    odd = jnp.bitwise_and(span[1] - split, 1)
    large = (span[1] - split) // 2
    lax.fori_loop(0, odd, functools.partial(chunk, CHUNK, split * CHUNK), 0)
    lax.fori_loop(0, large, functools.partial(chunk, LARGE, (split + odd) * CHUNK), 0)


def lift_points(at, last, feat, pos, home, nbr, deg, lift, first, bias, second):
    vmem = pl.BlockSpec(memory_space=pltpu.VMEM)
    smem = pl.BlockSpec(memory_space=pltpu.SMEM)
    work = [
        pltpu.VMEM((LARGE // SUB, 9 * CH, 3 * SUB), BF16),
        pltpu.VMEM((3, LARGE, NZ), F32),
    ]
    inputs = tuple(
        pltpu.with_memory_space_constraint(x, pltpu.HBM)
        for x in (feat, pos, home, nbr, deg, lift, first, bias, second))
    grid, low, high, *prepared, span_a, span_b = pl.pallas_call(
        functools.partial(sides_kernel, last),
        out_shape=[
            shape(CX + 2, CY + 2, CH, NZ),
            shape(CY + 2, PACKED, 128),
            shape(CY + 2, PACKED, 128),
            jax.ShapeDtypeStruct((112, PTS), BF16),
            jax.ShapeDtypeStruct((PTS, 128), jnp.int32),
            shape(4, CH, LARGE),
            jax.ShapeDtypeStruct((4 * CH, 4 * CH), BF16),
            jax.ShapeDtypeStruct((CH, CH), BF16),
            jax.ShapeDtypeStruct((2,), jnp.int32),
            jax.ShapeDtypeStruct((2,), jnp.int32),
        ],
        in_specs=[smem] + [pl.BlockSpec(memory_space=pltpu.HBM)] * len(inputs),
        out_specs=[vmem] * 8 + [smem, smem],
        scratch_shapes=[pltpu.VMEM(x.shape, x.dtype) for x in inputs[1:]] + work
        + [pltpu.SemaphoreType.DMA((len(inputs),))],
        compiler_params=LIMIT,
        name="lift_sides",
    )(at, *inputs)
    return grid, low, high, prepared, span_a, span_b


def lift_inner(at, last, span, prepared, name):
    vmem = pl.BlockSpec(memory_space=pltpu.VMEM)
    smem = pl.BlockSpec(memory_space=pltpu.SMEM)
    return pl.pallas_call(
        functools.partial(middle_kernel, last),
        out_shape=shape(CX, CY + 2, CH, NZ),
        in_specs=[smem, smem] + [vmem] * 5,
        out_specs=vmem,
        scratch_shapes=[
            pltpu.VMEM((LARGE // SUB, 9 * CH, 3 * SUB), BF16),
            pltpu.VMEM((3, LARGE, NZ), F32),
        ],
        compiler_params=LIMIT,
        name=name,
    )(at, span, *prepared)


def ends_kernel(last, at, sides, middle, below, above, low_y, high_y):
    low = at[0] == 0
    top = at[0] == last
    for y, out in ((0, low_y), (CY + 1, high_y)):
        for x in range(CX):
            l = sides[x + 1, y] + middle[x, y]
            if x == 0:
                l = l + jnp.where(low, sides[0, y], unpack(below[y]))
            if x == CX - 1:
                l = l + jnp.where(top, sides[CX + 1, y], unpack(above[y]))
            out[x] = pack(l)


def z_modes(table, pair):
    lane = lax.broadcasted_iota(jnp.int32, (MODES, HALVES), 1)
    d = mm(table, pair, NT, HIGH)
    re, im = d[0:MODES], d[MODES:]
    return jnp.where(lane < CH, re, swap(im)), jnp.where(lane < CH, swap(re), im)


def latent_kernel(last, at, tabz, sides, middle, rest, below, above, low_y, high_y, left, right,
                  spec, own):
    low = at[0] == 0
    top = at[0] == last[0]
    first_pen = at[1] == 0
    last_pen = at[1] == last[1]
    table = tabz[...]
    for x in range(CX):
        for yp in range(CY // 2):
            i = x * CY + 2 * yp
            for j in range(2):
                y = 2 * yp + j + 1
                l = sides[x + 1, y] + middle[x, y] + rest[x, y]
                if x == 0:
                    l = l + jnp.where(low, sides[0, y], unpack(below[y]))
                if x == CX - 1:
                    l = l + jnp.where(top, sides[CX + 1, y], unpack(above[y]))
                if y == 1:
                    l = l + unpack(jnp.where(first_pen, low_y[x], left[x]))
                if y == CY:
                    l = l + unpack(jnp.where(last_pen, high_y[x], right[x]))
                own[i + j] = l
            u, v = z_modes(table, own[i:i + 2].reshape(2 * CH, NZ))
            spec[:, i, :] = u
            spec[:, i + 1, :] = v


def y_kernel(r, main, out):
    sgn = sign_row((MODES, HALVES))
    pens = r.shape[0]
    for i in range(2 * CX):
        rows = r[:, i * CY:(i + 1) * CY, :].reshape(pens * CY, HALVES)
        ab = mm(main[...], rows, NN, HIGH)
        out[:, i, :] = ab[:MODES] + swap(ab[MODES:]) * sgn


def x_kernel(r, fwd, inv, w, out, lhs, res):
    rows = r.shape[0] * r.shape[1]
    modes = 2 * MODES
    sgn = sign_row((modes, HALVES))
    ab = mm(fwd[...], r[...].reshape(rows, HALVES), NN, HIGH)
    x = ab[:modes] + swap(ab[modes:]) * sgn
    parts = [*pieces(x), *pieces(swap(x))]
    lhs[...] = jnp.zeros_like(lhs)
    for j, p in enumerate(parts):
        lhs[:, j, :] = p
    for k in range(2):
        for j in range(MODES):
            m = k * MODES + j
            res[m] = mm(lhs[m][:, 0:CH].astype(BF16), w[j, 0, k])
    re = res[:, 0, :] + res[:, 1, :] + res[:, 2, :]
    im = res[:, 3, :] + res[:, 4, :] + res[:, 5, :]
    mixed = re - swap(im) * sgn
    ab = mm(inv[...], mixed, NN, HIGH)
    a, b = ab[:rows], ab[rows:]
    y = a - swap(b) * sign_row((rows, HALVES))
    out[...] = y.reshape(out.shape)


def y_back_kernel(r, inv, out):
    rows = inv.shape[0] // 2
    sgn = sign_row((rows, HALVES))
    for i in range(2 * CX):
        ab = mm(inv[...], r[:, i, :], NN, HIGH)
        y = ab[:rows] - swap(ab[rows:]) * sgn
        out[:, i * CY:(i + 1) * CY, :] = y.reshape(rows // CY, CY, HALVES)


def final_kernel(zb, tab, own, skip, bias, out):
    lane = lax.broadcasted_iota(jnp.int32, (MODES, HALVES), 1)
    zero = jnp.zeros((CH, CH), F32)
    skip_t = jnp.transpose(skip[...])
    pair = jnp.concatenate(
        [jnp.concatenate([skip_t, zero], axis=1), jnp.concatenate([zero, skip_t], axis=1)], axis=0)
    col = jnp.concatenate([bias[...], bias[...]], axis=1)
    col = jnp.transpose(jnp.broadcast_to(col, (8, HALVES)))
    col = jnp.broadcast_to(col[:, 0:1], (HALVES, NZ))
    for x in range(CX):
        for yp in range(CY // 2):
            i = x * CY + 2 * yp
            u = zb[:, i, :]
            v = zb[:, i + 1, :]
            s = jnp.concatenate(
                [jnp.where(lane < CH, u, swap(v)), jnp.where(lane < CH, swap(u), v)], axis=0)
            spectral = mm(s, tab[...], TN, HIGH)
            lat = own[i:i + 2].reshape(2 * CH, NZ)
            total = spectral + mm(pair, lat, NN, HIGH) + col
            out[x, 2 * yp:2 * yp + 2] = gelu(total).astype(BF16).reshape(2, CH, NZ)


def call(kernel, shapes, args, scratch=(), smem=False, name=None):
    specs = [pl.BlockSpec(memory_space=pltpu.VMEM)] * len(args)
    if smem:
        specs[0] = pl.BlockSpec(memory_space=pltpu.SMEM)
    return pl.pallas_call(
        kernel,
        out_shape=shapes,
        in_specs=specs,
        scratch_shapes=list(scratch),
        compiler_params=LIMIT,
        name=name,
    )(*args)


def shape(*dims):
    return jax.ShapeDtypeStruct(dims, F32)


def exchange(x, axis):
    return lax.all_to_all(x, axis, split_axis=0, concat_axis=0, tiled=True)


def moved(x, axis, step):
    devices = range(lax.axis_size(axis))
    return lax.ppermute(x, axis, [(i - step, i) for i in devices if i - step in devices])


def per_device(features, positions, home_cells, neighbours, degrees, lift_input, kernel_first,
               kernel_bias, kernel_second, spectral_weights, skip_weights, skip_bias):
    bins = lax.axis_size("bin")
    pens = lax.axis_size("pen")
    at = jnp.stack([lax.axis_index("bin"), lax.axis_index("pen")]).astype(jnp.int32)
    last = (bins * CX - 1, pens * CY - 1)
    sides, low, high, prepared, span_a, span_b = lift_points(
        at, last, features.T, positions, home_cells, neighbours.T,
        degrees[None, :], lift_input, kernel_first, kernel_bias[None, :], kernel_second)
    below = moved(high, "bin", 1)
    above = moved(low, "bin", -1)
    middle = lift_inner(at, last, span_a, prepared, "lift_ends")
    half = shape(CX, PACKED, 128)
    low_y, high_y = call(
        functools.partial(ends_kernel, bins - 1), [half, half],
        (at, sides, middle, below, above), smem=True, name="y_ends")
    left = moved(high_y, "pen", 1)
    right = moved(low_y, "pen", -1)
    rest = lift_inner(at, last, span_b, prepared, "lift_core")
    spec, own = call(
        functools.partial(latent_kernel, (bins - 1, pens - 1)),
        [shape(MODES, CX * CY, HALVES), shape(CX * CY, CH, NZ)],
        (at, jnp.asarray(z_forward_table()), sides, middle, rest, below, above, low_y, high_y,
         left, right), smem=True, name="latent_z")
    r = exchange(spec.reshape(pens, 2 * CX * CY, HALVES), "pen")
    r = call(y_kernel, shape(MODES, 2 * CX, HALVES), (r, jnp.asarray(y_forward_table(pens))),
             name="forward_y")
    r = exchange(r, "bin")
    fwd, inv = x_tables(bins)
    r = call(x_kernel, shape(MODES, 2 * CX, HALVES),
             (r, jnp.asarray(fwd), jnp.asarray(inv), spectral_weights),
             scratch=[pltpu.VMEM((2 * MODES, 8, HALVES), F32)] * 2, name="mix_x")
    r = exchange(r, "bin")
    r = call(y_back_kernel, shape(pens, 2 * CX * CY, HALVES),
             (r, jnp.asarray(y_inverse_table(pens))), name="inverse_y")
    r = exchange(r, "pen")
    out = call(
        final_kernel, jax.ShapeDtypeStruct((CX, CY, CH, NZ), BF16),
        (r.reshape(MODES, CX * CY, HALVES), jnp.asarray(z_inverse_table()), own,
         skip_weights, skip_bias[None, :]), name="finish")
    return out.transpose(0, 1, 3, 2)


def solution(mesh):
    in_specs = (
        P(("bin", "pen"), None),
        P(None, ("bin", "pen")),
        P(None, ("bin", "pen")),
        P(("bin", "pen"), None),
        P(("bin", "pen")),
        P(),
        P(),
        P(),
        P(),
        P(None, "bin", "pen", None, None),
        P(),
        P(),
    )
    out_specs = P("bin", "pen", None, None)
    return jax.shard_map(
        per_device, mesh=mesh, in_specs=in_specs, out_specs=out_specs, check_vma=False
    )
```

```python
import functools
import math

import jax
import jax.numpy as jnp
import numpy as np
from jax import lax
from jax.experimental import pallas as pl
from jax.experimental.pallas import tpu as pltpu
from jax.sharding import PartitionSpec as P

NZ = 192
CX = 4
CY = 8
PTS = 2048
CH = 64
MODES = 32
CHUNK = 256
SUB = 128
LARGE = 512
FIRST = 5
SECOND = 7
HALVES = 2 * CH

F32 = jnp.float32
BF16 = jnp.bfloat16
HIGH = lax.Precision.HIGH
LIMIT = pltpu.CompilerParams(vmem_limit_bytes=24 * 1024 * 1024)

NN = (((1,), (0,)), ((), ()))
NT = (((1,), (1,)), ((), ()))
TN = (((0,), (0,)), ((), ()))


def mm(a, b, dims=NN, precision=None):
    return lax.dot_general(a, b, dims, precision=precision, preferred_element_type=F32)


def gelu(x):
    inner = x * (0.7978845608028654 + 0.035677408136300125 * (x * x))
    half = 0.5 * x
    return half + half * jnp.tanh(inner)


def twice_gelu(x):
    return x + x * jnp.tanh(x * (0.7978845608028654 + 0.035677408136300125 * (x * x)))


def swap(x):
    return pltpu.roll(x, CH, 1)


def sign_row(shape):
    lane = lax.broadcasted_iota(jnp.int32, shape, 1)
    return jnp.where(lane < CH, 1.0, -1.0).astype(F32)


def tables(length, signed):
    mode = np.arange(MODES)
    if signed:
        mode = np.where(mode < MODES // 2, mode, mode - MODES)
    return mode


def angles(rows, length, signed):
    mode = tables(length, signed)
    phase = (np.asarray(rows)[:, None] * mode[None, :]) % length
    angle = phase * (2.0 * math.pi / length)
    scale = 1.0 / math.sqrt(length)
    return np.cos(angle) * scale, np.sin(angle) * scale


def z_forward_table():
    c, s = angles(np.arange(NZ), NZ, False)
    return np.concatenate([c.T, -s.T], axis=0).astype(np.float32)


def z_inverse_table():
    c, s = angles(np.arange(NZ), NZ, False)
    w = np.where(np.arange(MODES) == 0, 1.0, 2.0)[:, None]
    return np.concatenate([c.T * w, -s.T * w], axis=0).astype(np.float32)


def y_forward_table(pens):
    length = CY * pens
    c, s = angles(np.arange(length), length, True)
    return np.concatenate([c.T, s.T], axis=0).astype(np.float32)


def y_inverse_table(pens):
    length = CY * pens
    c, s = angles(np.arange(length), length, True)
    return np.concatenate([c, s], axis=0).astype(np.float32)


def x_tables(bins):
    length = CX * bins
    c, s = angles(np.arange(length), length, True)
    fwd = np.zeros((2, 2, MODES, bins, 2, CX))
    inv = np.zeros((2, bins, 2, CX, 2, MODES))
    for k in range(2):
        fwd[0, k, :, :, k, :] = c.T.reshape(MODES, bins, CX)
        fwd[1, k, :, :, k, :] = s.T.reshape(MODES, bins, CX)
        inv[0, :, k, :, k, :] = c.reshape(bins, CX, MODES)
        inv[1, :, k, :, k, :] = s.reshape(bins, CX, MODES)
    fwd = fwd.reshape(4 * MODES, bins * 2 * CX)
    inv = inv.reshape(2 * bins * 2 * CX, 2 * MODES)
    return fwd.astype(np.float32), inv.astype(np.float32)


def pack(cells):
    tail = cells[:, 128:NZ]
    half = CH // 2
    return jnp.concatenate(
        [cells[:, 0:128], jnp.concatenate([tail[0:half], tail[half:CH]], axis=1)], axis=0)


def unpack(rows):
    tail = rows[CH:]
    tail = jnp.concatenate([tail[:, 0:NZ - 128], tail[:, NZ - 128:]], axis=0)
    return jnp.concatenate([rows[0:CH], tail], axis=1)


def pieces(x):
    hi = x.astype(BF16).astype(F32)
    rest = x - hi
    mid = rest.astype(BF16).astype(F32)
    return hi, mid, rest - mid


PACKED = CH * NZ // 128
SIDE = 2 * CY
BOTH = SIDE + 4


def column_rank(hx, hy):
    side = jnp.where(hx == 0, 0, CY) + hy
    end = SIDE + (hx - 1) * 2 + jnp.where(hy == 0, 0, 1)
    core = BOTH + (hx - 1) * (CY - 2) + hy - 1
    inner = jnp.where((hy == 0) | (hy == CY - 1), end, core)
    return jnp.where((hx == 0) | (hx == CX - 1), side, inner)


def column_x(o):
    inner = jnp.where(o < BOTH, jnp.where(o < SIDE + 2, 1, 2), jnp.where(o < BOTH + CY - 2, 1, 2))
    return jnp.where(o < CY, 0, jnp.where(o < SIDE, CX - 1, inner))


def column_y(o):
    side = jnp.where(o < CY, o, o - CY)
    end = jnp.where((o == SIDE) | (o == SIDE + 2), 0, CY - 1)
    core = jnp.where(o < BOTH + CY - 2, o - BOTH, o - (BOTH + CY - 2)) + 1
    return jnp.where(o < SIDE, side, jnp.where(o < BOTH, end, core))


def add_chunk(last, at, base, size, plane0, data, rankb, taps, quad, lift_t, mess, keys, grid):
    lanes = lax.broadcasted_iota(jnp.int32, (PTS, 128), 1) + base
    perm = jnp.concatenate(
        [jnp.where(rankb[...] == lanes + j * 128, 1.0, 0.0).astype(BF16)
         for j in range(size // 128)], axis=1)
    t = mm(data[...], perm)
    hzs = t[73:74]
    cols = t[74:75]
    spans = [(jnp.min(cols[:, j * SUB:(j + 1) * SUB]).astype(jnp.int32),
              jnp.max(cols[:, j * SUB:(j + 1) * SUB]).astype(jnp.int32) + 1)
             for j in range(size // SUB)]
    key = 256.0 * cols
    key = jnp.concatenate(
        [key + jnp.maximum(hzs - 1.0, 0.0), key + hzs, key + jnp.minimum(hzs + 1.0, NZ - 1.0),
         jnp.zeros((5, size), F32)], axis=0)
    key = jnp.transpose(key)
    for dz in range(3):
        keys[dz, 0:size] = jnp.broadcast_to(key[:, dz:dz + 1], (size, NZ))

    values = mm(lift_t[...], t[0:64].astype(BF16))
    ox = t[64:65] + t[65:66] + t[66:67]
    oy = t[67:68] + t[68:69] + t[69:70]
    oz = t[70:71] + t[71:72] + t[72:73]
    coli = cols.astype(jnp.int32)
    gx = column_x(coli) + at[0] * CX
    gy = column_y(coli) + at[1] * CY
    k_x, k_y, k_z, k_b = (taps[j, :, 0:size] for j in range(4))

    def ends(g, end):
        return (jnp.where(g > 0, -1.0, 0.0), None, jnp.where(g < end, 1.0, 0.0))

    base_pre = k_x * ox + k_y * oy + k_z * oz + k_b
    ex = ends(gx, last[0])
    ey = ends(gy, last[1])
    ez = ends(hzs, NZ - 1.0)
    pend = []

    def flush():
        while len(pend) < 4:
            pend.append((None, jnp.zeros((CH, size), BF16)))
        kern = mm(quad[...], jnp.concatenate([h for _, h in pend], axis=0))
        for j, (where, _) in enumerate(pend):
            if where is None:
                continue
            dx, dy, dz = where
            k = dx * 9 + dy * 3 + dz
            m = kern[j * CH:(j + 1) * CH] * (values * t[80 + k:81 + k])
            hi = m.astype(BF16)
            r = (dx * 3 + dy) * CH
            for s in range(size // SUB):
                cut = slice(s * SUB, (s + 1) * SUB)
                mess[s, r:r + CH, dz * SUB:(dz + 1) * SUB] = hi[:, cut]
        pend.clear()

    for dx in range(3):
        pre_x = base_pre if ex[dx] is None else base_pre + ex[dx] * k_x
        for dy in range(3):
            pre_y = pre_x if ey[dy] is None else pre_x + ey[dy] * k_y
            for dz in range(3):
                pre = pre_y if ez[dz] is None else pre_y + ez[dz] * k_z
                pend.append(((dx, dy, dz), twice_gelu(pre).astype(BF16)))
                if len(pend) == 4:
                    flush()
    flush()

    lane = lax.broadcasted_iota(jnp.int32, (SUB, NZ), 1).astype(F32)
    longest = spans[0][1] - spans[0][0]
    for begin, end in spans[1:]:
        longest = jnp.maximum(longest, end - begin)

    def column(j, _):
        results = []
        for s, (begin, end) in enumerate(spans):
            c = jnp.minimum(begin + j, end - 1)
            goal = lane + jnp.where(begin + j < end, 256.0 * c.astype(F32), -1.0e6)
            hot = jnp.concatenate(
                [jnp.where(keys[dz, s * SUB:(s + 1) * SUB] == goal, 1.0, 0.0).astype(BF16)
                 for dz in range(3)], axis=0)
            results.append((c, [mm(mess[s, q * 3 * CH:(q + 1) * 3 * CH], hot) for q in range(3)]))
        for c, acc in results:
            cx = column_x(c) - plane0
            cy = column_y(c)
            for dx in range(3):
                for dy in range(3):
                    grid[cx + dx, cy + dy] += acc[dx][dy * CH:(dy + 1) * CH]
        return 0

    lax.fori_loop(0, longest, column, 0)


def sides_kernel(last, at, feat_h, pos_h, home_h, nbr_h, deg_h, lift_h, first_h, bias_h, second_h,
                 grid, low, high, data, rankb, taps, quad, lift_t, span_a, span_b,
                 pos, home, nbr, deg, lift, first, bias, second, mess, keys, sems):
    pairs = [(home_h, home), (pos_h, pos), (nbr_h, nbr), (deg_h, deg),
             (feat_h, data.at[0:64]), (lift_h, lift), (first_h, first), (bias_h, bias),
             (second_h, second)]
    copies = [pltpu.make_async_copy(a, b, sems.at[i]) for i, (a, b) in enumerate(pairs)]
    for c in copies:
        c.start()
    grid[...] = jnp.zeros_like(grid)
    tri = jnp.where(
        lax.broadcasted_iota(jnp.int32, (CHUNK, CHUNK), 0)
        < lax.broadcasted_iota(jnp.int32, (CHUNK, CHUNK), 1), 1.0, 0.0).astype(BF16)
    copies[0].wait()
    hx = home[0:1, :]
    hy = home[1:2, :]
    hz = home[2:3, :]
    col = column_rank(hx, hy)

    def blocks(limit, least):
        n = jnp.sum(jnp.where(col < limit, 1.0, 0.0)).astype(jnp.int32)
        return jnp.maximum((n + CHUNK - 1) // CHUNK, least)

    split = blocks(SIDE, FIRST)
    later = jnp.maximum(blocks(BOTH, SECOND), split)
    span_a[0] = split
    span_a[1] = later
    span_b[0] = later
    span_b[1] = PTS // CHUNK

    ids = lax.broadcasted_iota(jnp.int32, (CX * CY, PTS), 0)
    carry = jnp.sum(jnp.where(col < ids, 1.0, 0.0), axis=1, keepdims=True)
    for blk in range(PTS // CHUNK):
        part = slice(blk * CHUNK, (blk + 1) * CHUNK)
        hot = jnp.where(col[:, part] == ids[:, part], 1.0, 0.0)
        ahead = mm(hot.astype(BF16), tri) + carry
        rank = jnp.sum(hot * ahead, axis=0, keepdims=True)
        rank = jnp.transpose(jnp.broadcast_to(rank, (8, CHUNK)))
        rankb[part, :] = jnp.broadcast_to(rank[:, 0:1], (CHUNK, 128)).astype(jnp.int32)
        carry = carry + jnp.sum(hot, axis=1, keepdims=True)

    for c in copies[1:]:
        c.wait()
    slot = lax.broadcasted_iota(jnp.int32, (16, PTS), 0)
    bits = jnp.sum(
        jnp.where(slot < deg[...], jnp.left_shift(1, nbr[...]), 0), axis=0, keepdims=True)
    code = lax.broadcasted_iota(jnp.int32, (32, PTS), 0)
    live = jnp.bitwise_and(jnp.right_shift(bits, code), 1).astype(F32)
    off_x = (hx + at[0] * CX).astype(F32) + 0.5 - pos[0:1, :]
    off_y = (hy + at[1] * CY).astype(F32) + 0.5 - pos[1:2, :]
    off_z = hz.astype(F32) + 0.5 - pos[2:3, :]
    rows = [*pieces(off_x), *pieces(off_y), *pieces(off_z), hz.astype(F32), col.astype(F32),
            jnp.zeros((5, PTS), F32)]
    data[64:80, :] = jnp.concatenate(rows, axis=0).astype(BF16)
    data[80:112, :] = live.astype(BF16)

    flat = jnp.concatenate([first[...], bias[...], jnp.zeros((4, CH), F32)], axis=0)
    flat = jnp.concatenate([flat, jnp.zeros((8, 128 - CH), F32)], axis=1)
    flat = jnp.transpose(flat)
    for j in range(4):
        taps[j] = jnp.broadcast_to(flat[0:CH, j:j + 1], (CH, LARGE))
    zero = jnp.zeros((CH, CH), F32)
    sec_t = jnp.transpose(0.5 * second[...].astype(F32))
    quad[...] = jnp.concatenate(
        [jnp.concatenate([sec_t if i == j else zero for j in range(4)], axis=1)
         for i in range(4)], axis=0).astype(BF16)
    lift_t[...] = jnp.transpose(lift[...].astype(F32)).astype(BF16)

    def chunk(size, first, step, _):
        add_chunk(last, at, first + step * size, size, 0, data, rankb, taps, quad, lift_t, mess,
                  keys, grid)
        return 0

    large = split // 2
    lax.fori_loop(0, large, functools.partial(chunk, LARGE, 0), 0)
    lax.fori_loop(0, split - 2 * large, functools.partial(chunk, CHUNK, large * LARGE), 0)
    for y in range(CY + 2):
        low[y] = pack(grid[0, y])
        high[y] = pack(grid[CX + 1, y])


def middle_kernel(last, at, span, data, rankb, taps, quad, lift_t, grid, mess, keys):
    grid[...] = jnp.zeros_like(grid)

    def chunk(size, first, step, _):
        add_chunk(last, at, first + step * size, size, 1, data, rankb, taps, quad, lift_t, mess,
                  keys, grid)
        return 0

    split = span[0]
    odd = jnp.bitwise_and(span[1] - split, 1)
    large = (span[1] - split) // 2
    lax.fori_loop(0, odd, functools.partial(chunk, CHUNK, split * CHUNK), 0)
    lax.fori_loop(0, large, functools.partial(chunk, LARGE, (split + odd) * CHUNK), 0)


def lift_points(at, last, feat, pos, home, nbr, deg, lift, first, bias, second):
    vmem = pl.BlockSpec(memory_space=pltpu.VMEM)
    smem = pl.BlockSpec(memory_space=pltpu.SMEM)
    work = [
        pltpu.VMEM((LARGE // SUB, 9 * CH, 3 * SUB), BF16),
        pltpu.VMEM((3, LARGE, NZ), F32),
    ]
    inputs = tuple(
        pltpu.with_memory_space_constraint(x, pltpu.HBM)
        for x in (feat, pos, home, nbr, deg, lift, first, bias, second))
    grid, low, high, *prepared, span_a, span_b = pl.pallas_call(
        functools.partial(sides_kernel, last),
        out_shape=[
            shape(CX + 2, CY + 2, CH, NZ),
            shape(CY + 2, PACKED, 128),
            shape(CY + 2, PACKED, 128),
            jax.ShapeDtypeStruct((112, PTS), BF16),
            jax.ShapeDtypeStruct((PTS, 128), jnp.int32),
            shape(4, CH, LARGE),
            jax.ShapeDtypeStruct((4 * CH, 4 * CH), BF16),
            jax.ShapeDtypeStruct((CH, CH), BF16),
            jax.ShapeDtypeStruct((2,), jnp.int32),
            jax.ShapeDtypeStruct((2,), jnp.int32),
        ],
        in_specs=[smem] + [pl.BlockSpec(memory_space=pltpu.HBM)] * len(inputs),
        out_specs=[vmem] * 8 + [smem, smem],
        scratch_shapes=[pltpu.VMEM(x.shape, x.dtype) for x in inputs[1:]] + work
        + [pltpu.SemaphoreType.DMA((len(inputs),))],
        compiler_params=LIMIT,
        name="lift_sides",
    )(at, *inputs)
    return grid, low, high, prepared, span_a, span_b


def lift_inner(at, last, span, prepared, name):
    vmem = pl.BlockSpec(memory_space=pltpu.VMEM)
    smem = pl.BlockSpec(memory_space=pltpu.SMEM)
    return pl.pallas_call(
        functools.partial(middle_kernel, last),
        out_shape=shape(CX, CY + 2, CH, NZ),
        in_specs=[smem, smem] + [vmem] * 5,
        out_specs=vmem,
        scratch_shapes=[
            pltpu.VMEM((LARGE // SUB, 9 * CH, 3 * SUB), BF16),
            pltpu.VMEM((3, LARGE, NZ), F32),
        ],
        compiler_params=LIMIT,
        name=name,
    )(at, span, *prepared)


def ends_kernel(last, at, sides, middle, below, above, low_y, high_y):
    low = at[0] == 0
    top = at[0] == last
    for y, out in ((0, low_y), (CY + 1, high_y)):
        for x in range(CX):
            l = sides[x + 1, y] + middle[x, y]
            if x == 0:
                l = l + jnp.where(low, sides[0, y], unpack(below[y]))
            if x == CX - 1:
                l = l + jnp.where(top, sides[CX + 1, y], unpack(above[y]))
            out[x] = pack(l)


def z_modes(table, pair):
    lane = lax.broadcasted_iota(jnp.int32, (MODES, HALVES), 1)
    d = mm(table, pair, NT, HIGH)
    re, im = d[0:MODES], d[MODES:]
    return jnp.where(lane < CH, re, swap(im)), jnp.where(lane < CH, swap(re), im)


def latent_kernel(last, at, tabz, sides, middle, rest, below, above, low_y, high_y, left, right,
                  spec, own):
    low = at[0] == 0
    top = at[0] == last[0]
    first_pen = at[1] == 0
    last_pen = at[1] == last[1]
    table = tabz[...]
    for x in range(CX):
        for yp in range(CY // 2):
            i = x * CY + 2 * yp
            for j in range(2):
                y = 2 * yp + j + 1
                l = sides[x + 1, y] + middle[x, y] + rest[x, y]
                if x == 0:
                    l = l + jnp.where(low, sides[0, y], unpack(below[y]))
                if x == CX - 1:
                    l = l + jnp.where(top, sides[CX + 1, y], unpack(above[y]))
                if y == 1:
                    l = l + unpack(jnp.where(first_pen, low_y[x], left[x]))
                if y == CY:
                    l = l + unpack(jnp.where(last_pen, high_y[x], right[x]))
                own[i + j] = l
            u, v = z_modes(table, own[i:i + 2].reshape(2 * CH, NZ))
            spec[:, i, :] = u
            spec[:, i + 1, :] = v


def y_kernel(r, main, out):
    sgn = sign_row((MODES, HALVES))
    pens = r.shape[0]
    for i in range(2 * CX):
        rows = r[:, i * CY:(i + 1) * CY, :].reshape(pens * CY, HALVES)
        ab = mm(main[...], rows, NN, HIGH)
        out[:, i, :] = ab[:MODES] + swap(ab[MODES:]) * sgn


def x_kernel(r, fwd, inv, w, out, lhs, res):
    rows = r.shape[0] * r.shape[1]
    modes = 2 * MODES
    sgn = sign_row((modes, HALVES))
    ab = mm(fwd[...], r[...].reshape(rows, HALVES), NN, HIGH)
    x = ab[:modes] + swap(ab[modes:]) * sgn
    parts = [*pieces(x), *pieces(swap(x))]
    lhs[...] = jnp.zeros_like(lhs)
    for j, p in enumerate(parts):
        lhs[:, j, :] = p
    for k in range(2):
        for j in range(MODES):
            m = k * MODES + j
            res[m] = mm(lhs[m][:, 0:CH].astype(BF16), w[j, 0, k])
    re = res[:, 0, :] + res[:, 1, :] + res[:, 2, :]
    im = res[:, 3, :] + res[:, 4, :] + res[:, 5, :]
    mixed = re - swap(im) * sgn
    ab = mm(inv[...], mixed, NN, HIGH)
    a, b = ab[:rows], ab[rows:]
    y = a - swap(b) * sign_row((rows, HALVES))
    out[...] = y.reshape(out.shape)


def y_back_kernel(r, inv, out):
    rows = inv.shape[0] // 2
    sgn = sign_row((rows, HALVES))
    for i in range(2 * CX):
        ab = mm(inv[...], r[:, i, :], NN, HIGH)
        y = ab[:rows] - swap(ab[rows:]) * sgn
        out[:, i * CY:(i + 1) * CY, :] = y.reshape(rows // CY, CY, HALVES)


def final_kernel(zb, tab, own, skip, bias, out, rows, sems):
    lane = lax.broadcasted_iota(jnp.int32, (MODES, HALVES), 1)
    zero = jnp.zeros((CH, CH), F32)
    skip_t = jnp.transpose(skip[...])
    pair = jnp.concatenate(
        [jnp.concatenate([skip_t, zero], axis=1), jnp.concatenate([zero, skip_t], axis=1)], axis=0)
    col = jnp.concatenate([bias[...], bias[...]], axis=1)
    col = jnp.transpose(jnp.broadcast_to(col, (8, HALVES)))
    col = jnp.broadcast_to(col[:, 0:1], (HALVES, NZ))
    copies = []
    for x in range(CX):
        for yp in range(CY // 2):
            i = x * CY + 2 * yp
            u = zb[:, i, :]
            v = zb[:, i + 1, :]
            s = jnp.concatenate(
                [jnp.where(lane < CH, u, swap(v)), jnp.where(lane < CH, swap(u), v)], axis=0)
            lat = own[i:i + 2].reshape(2 * CH, NZ)
            left = jnp.concatenate([jnp.transpose(s), pair], axis=1)
            total = mm(left, jnp.concatenate([tab[...], lat], axis=0), NN, HIGH) + col
            rows[x, 2 * yp:2 * yp + 2] = gelu(total).astype(BF16).reshape(2, CH, NZ)
        copies.append(pltpu.make_async_copy(rows.at[x], out.at[x], sems.at[x]))
        copies[-1].start()
    for c in copies:
        c.wait()


def finish(zb, own, skip, bias):
    cells = jax.ShapeDtypeStruct((CX, CY, CH, NZ), BF16)
    return pl.pallas_call(
        final_kernel,
        out_shape=cells,
        in_specs=[pl.BlockSpec(memory_space=pltpu.VMEM)] * 5,
        out_specs=pl.BlockSpec(memory_space=pltpu.HBM),
        scratch_shapes=[pltpu.VMEM(cells.shape, BF16), pltpu.SemaphoreType.DMA((CX,))],
        compiler_params=LIMIT,
        name="finish",
    )(zb, jnp.asarray(z_inverse_table()), own, skip, bias)


def call(kernel, shapes, args, scratch=(), smem=False, name=None):
    specs = [pl.BlockSpec(memory_space=pltpu.VMEM)] * len(args)
    if smem:
        specs[0] = pl.BlockSpec(memory_space=pltpu.SMEM)
    return pl.pallas_call(
        kernel,
        out_shape=shapes,
        in_specs=specs,
        scratch_shapes=list(scratch),
        compiler_params=LIMIT,
        name=name,
    )(*args)


def shape(*dims):
    return jax.ShapeDtypeStruct(dims, F32)


def exchange(x, axis):
    return lax.all_to_all(x, axis, split_axis=0, concat_axis=0, tiled=True)


def moved(x, axis, step):
    devices = range(lax.axis_size(axis))
    return lax.ppermute(x, axis, [(i - step, i) for i in devices if i - step in devices])


def per_device(features, positions, home_cells, neighbours, degrees, lift_input, kernel_first,
               kernel_bias, kernel_second, spectral_weights, skip_weights, skip_bias):
    bins = lax.axis_size("bin")
    pens = lax.axis_size("pen")
    at = jnp.stack([lax.axis_index("bin"), lax.axis_index("pen")]).astype(jnp.int32)
    last = (bins * CX - 1, pens * CY - 1)
    sides, low, high, prepared, span_a, span_b = lift_points(
        at, last, features.T, positions, home_cells, neighbours.T,
        degrees[None, :], lift_input, kernel_first, kernel_bias[None, :], kernel_second)
    below = moved(high, "bin", 1)
    above = moved(low, "bin", -1)
    middle = lift_inner(at, last, span_a, prepared, "lift_ends")
    half = shape(CX, PACKED, 128)
    low_y, high_y = call(
        functools.partial(ends_kernel, bins - 1), [half, half],
        (at, sides, middle, below, above), smem=True, name="y_ends")
    left = moved(high_y, "pen", 1)
    right = moved(low_y, "pen", -1)
    rest = lift_inner(at, last, span_b, prepared, "lift_core")
    spec, own = call(
        functools.partial(latent_kernel, (bins - 1, pens - 1)),
        [shape(MODES, CX * CY, HALVES), shape(CX * CY, CH, NZ)],
        (at, jnp.asarray(z_forward_table()), sides, middle, rest, below, above, low_y, high_y,
         left, right), smem=True, name="latent_z")
    r = exchange(spec.reshape(pens, 2 * CX * CY, HALVES), "pen")
    r = call(y_kernel, shape(MODES, 2 * CX, HALVES), (r, jnp.asarray(y_forward_table(pens))),
             name="forward_y")
    r = exchange(r, "bin")
    fwd, inv = x_tables(bins)
    r = call(x_kernel, shape(MODES, 2 * CX, HALVES),
             (r, jnp.asarray(fwd), jnp.asarray(inv), spectral_weights),
             scratch=[pltpu.VMEM((2 * MODES, 8, HALVES), F32)] * 2, name="mix_x")
    r = exchange(r, "bin")
    r = call(y_back_kernel, shape(pens, 2 * CX * CY, HALVES),
             (r, jnp.asarray(y_inverse_table(pens))), name="inverse_y")
    r = exchange(r, "pen")
    out = finish(r.reshape(MODES, CX * CY, HALVES), own, skip_weights, skip_bias[None, :])
    return out.transpose(0, 1, 3, 2)


def solution(mesh):
    in_specs = (
        P(("bin", "pen"), None),
        P(None, ("bin", "pen")),
        P(None, ("bin", "pen")),
        P(("bin", "pen"), None),
        P(("bin", "pen")),
        P(),
        P(),
        P(),
        P(),
        P(None, "bin", "pen", None, None),
        P(),
        P(),
    )
    out_specs = P("bin", "pen", None, None)
    return jax.shard_map(
        per_device, mesh=mesh, in_specs=in_specs, out_specs=out_specs, check_vma=False
    )
```

```python
import functools
import math

import jax
import jax.numpy as jnp
import numpy as np
from jax import lax
from jax.experimental import pallas as pl
from jax.experimental.pallas import tpu as pltpu
from jax.sharding import PartitionSpec as P

NZ = 192
CX = 4
CY = 8
PTS = 2048
CH = 64
MODES = 32
CHUNK = 256
SUB = 128
LARGE = 512
FIRST = 5
SECOND = 7
HALVES = 2 * CH

F32 = jnp.float32
BF16 = jnp.bfloat16
HIGH = lax.Precision.HIGH
LIMIT = pltpu.CompilerParams(vmem_limit_bytes=24 * 1024 * 1024)

NN = (((1,), (0,)), ((), ()))
NT = (((1,), (1,)), ((), ()))
TN = (((0,), (0,)), ((), ()))


def mm(a, b, dims=NN, precision=None):
    return lax.dot_general(a, b, dims, precision=precision, preferred_element_type=F32)


def gelu(x):
    inner = x * (0.7978845608028654 + 0.035677408136300125 * (x * x))
    half = 0.5 * x
    return half + half * jnp.tanh(inner)


def twice_gelu(x):
    return x + x * jnp.tanh(x * (0.7978845608028654 + 0.035677408136300125 * (x * x)))


def swap(x):
    return pltpu.roll(x, CH, 1)


def sign_row(shape):
    lane = lax.broadcasted_iota(jnp.int32, shape, 1)
    return jnp.where(lane < CH, 1.0, -1.0).astype(F32)


def tables(length, signed):
    mode = np.arange(MODES)
    if signed:
        mode = np.where(mode < MODES // 2, mode, mode - MODES)
    return mode


def angles(rows, length, signed):
    mode = tables(length, signed)
    phase = (np.asarray(rows)[:, None] * mode[None, :]) % length
    angle = phase * (2.0 * math.pi / length)
    scale = 1.0 / math.sqrt(length)
    return np.cos(angle) * scale, np.sin(angle) * scale


def z_forward_table():
    c, s = angles(np.arange(NZ), NZ, False)
    return np.concatenate([c.T, -s.T], axis=0).astype(np.float32)


def z_inverse_table():
    c, s = angles(np.arange(NZ), NZ, False)
    w = np.where(np.arange(MODES) == 0, 1.0, 2.0)[:, None]
    return np.concatenate([c.T * w, -s.T * w], axis=0).astype(np.float32)


def y_forward_table(pens):
    length = CY * pens
    c, s = angles(np.arange(length), length, True)
    return np.concatenate([c.T, s.T], axis=0).astype(np.float32)


def y_inverse_table(pens):
    length = CY * pens
    c, s = angles(np.arange(length), length, True)
    return np.concatenate([c, s], axis=0).astype(np.float32)


def x_tables(bins):
    length = CX * bins
    c, s = angles(np.arange(length), length, True)
    fwd = np.zeros((2, 2, MODES, bins, 2, CX))
    inv = np.zeros((2, bins, 2, CX, 2, MODES))
    for k in range(2):
        fwd[0, k, :, :, k, :] = c.T.reshape(MODES, bins, CX)
        fwd[1, k, :, :, k, :] = s.T.reshape(MODES, bins, CX)
        inv[0, :, k, :, k, :] = c.reshape(bins, CX, MODES)
        inv[1, :, k, :, k, :] = s.reshape(bins, CX, MODES)
    fwd = fwd.reshape(4 * MODES, bins * 2 * CX)
    inv = inv.reshape(2 * bins * 2 * CX, 2 * MODES)
    return fwd.astype(np.float32), inv.astype(np.float32)


def pack(cells):
    tail = cells[:, 128:NZ]
    half = CH // 2
    return jnp.concatenate(
        [cells[:, 0:128], jnp.concatenate([tail[0:half], tail[half:CH]], axis=1)], axis=0)


def unpack(rows):
    tail = rows[CH:]
    tail = jnp.concatenate([tail[:, 0:NZ - 128], tail[:, NZ - 128:]], axis=0)
    return jnp.concatenate([rows[0:CH], tail], axis=1)


def pieces(x):
    hi = x.astype(BF16).astype(F32)
    rest = x - hi
    mid = rest.astype(BF16).astype(F32)
    return hi, mid, rest - mid


PACKED = CH * NZ // 128
SIDE = 2 * CY
BOTH = SIDE + 4


def column_rank(hx, hy):
    side = jnp.where(hx == 0, 0, CY) + hy
    end = SIDE + (hx - 1) * 2 + jnp.where(hy == 0, 0, 1)
    core = BOTH + (hx - 1) * (CY - 2) + hy - 1
    inner = jnp.where((hy == 0) | (hy == CY - 1), end, core)
    return jnp.where((hx == 0) | (hx == CX - 1), side, inner)


def column_x(o):
    inner = jnp.where(o < BOTH, jnp.where(o < SIDE + 2, 1, 2), jnp.where(o < BOTH + CY - 2, 1, 2))
    return jnp.where(o < CY, 0, jnp.where(o < SIDE, CX - 1, inner))


def column_y(o):
    side = jnp.where(o < CY, o, o - CY)
    end = jnp.where((o == SIDE) | (o == SIDE + 2), 0, CY - 1)
    core = jnp.where(o < BOTH + CY - 2, o - BOTH, o - (BOTH + CY - 2)) + 1
    return jnp.where(o < SIDE, side, jnp.where(o < BOTH, end, core))


def add_chunk(last, at, base, size, plane0, data, rankb, taps, quad, lift_t, mess, keys, grid):
    lanes = lax.broadcasted_iota(jnp.int32, (PTS, 128), 1) + base
    perm = jnp.concatenate(
        [jnp.where(rankb[...] == lanes + j * 128, 1.0, 0.0).astype(BF16)
         for j in range(size // 128)], axis=1)
    t = mm(data[...], perm)
    hzs = t[73:74]
    cols = t[74:75]
    spans = [(jnp.min(cols[:, j * SUB:(j + 1) * SUB]).astype(jnp.int32),
              jnp.max(cols[:, j * SUB:(j + 1) * SUB]).astype(jnp.int32) + 1)
             for j in range(size // SUB)]
    key = 256.0 * cols
    key = jnp.concatenate(
        [key + jnp.maximum(hzs - 1.0, 0.0), key + hzs, key + jnp.minimum(hzs + 1.0, NZ - 1.0),
         jnp.zeros((5, size), F32)], axis=0)
    key = jnp.transpose(key)
    for dz in range(3):
        keys[dz, 0:size] = jnp.broadcast_to(key[:, dz:dz + 1], (size, NZ))

    values = mm(lift_t[...], t[0:64].astype(BF16))
    ox = t[64:65] + t[65:66] + t[66:67]
    oy = t[67:68] + t[68:69] + t[69:70]
    oz = t[70:71] + t[71:72] + t[72:73]
    coli = cols.astype(jnp.int32)
    gx = column_x(coli) + at[0] * CX
    gy = column_y(coli) + at[1] * CY
    k_x, k_y, k_z, k_b = (taps[j, :, 0:size] for j in range(4))

    def ends(g, end):
        return (jnp.where(g > 0, -1.0, 0.0), None, jnp.where(g < end, 1.0, 0.0))

    base_pre = k_x * ox + k_y * oy + k_z * oz + k_b
    ex = ends(gx, last[0])
    ey = ends(gy, last[1])
    ez = ends(hzs, NZ - 1.0)
    pend = []

    def flush():
        while len(pend) < 4:
            pend.append((None, jnp.zeros((CH, size), BF16)))
        kern = mm(quad[...], jnp.concatenate([h for _, h in pend], axis=0))
        for j, (where, _) in enumerate(pend):
            if where is None:
                continue
            dx, dy, dz = where
            k = dx * 9 + dy * 3 + dz
            m = kern[j * CH:(j + 1) * CH] * (values * t[80 + k:81 + k])
            hi = m.astype(BF16)
            r = (dx * 3 + dy) * CH
            for s in range(size // SUB):
                cut = slice(s * SUB, (s + 1) * SUB)
                mess[s, r:r + CH, dz * SUB:(dz + 1) * SUB] = hi[:, cut]
        pend.clear()

    for dx in range(3):
        pre_x = base_pre if ex[dx] is None else base_pre + ex[dx] * k_x
        for dy in range(3):
            pre_y = pre_x if ey[dy] is None else pre_x + ey[dy] * k_y
            for dz in range(3):
                pre = pre_y if ez[dz] is None else pre_y + ez[dz] * k_z
                pend.append(((dx, dy, dz), twice_gelu(pre).astype(BF16)))
                if len(pend) == 4:
                    flush()
    flush()

    lane = lax.broadcasted_iota(jnp.int32, (SUB, NZ), 1).astype(F32)
    longest = spans[0][1] - spans[0][0]
    for begin, end in spans[1:]:
        longest = jnp.maximum(longest, end - begin)

    def column(j, _):
        results = []
        for s, (begin, end) in enumerate(spans):
            c = jnp.minimum(begin + j, end - 1)
            goal = lane + jnp.where(begin + j < end, 256.0 * c.astype(F32), -1.0e6)
            hot = jnp.concatenate(
                [jnp.where(keys[dz, s * SUB:(s + 1) * SUB] == goal, 1.0, 0.0).astype(BF16)
                 for dz in range(3)], axis=0)
            results.append((c, [mm(mess[s, q * 3 * CH:(q + 1) * 3 * CH], hot) for q in range(3)]))
        for c, acc in results:
            cx = column_x(c) - plane0
            cy = column_y(c)
            for dx in range(3):
                for dy in range(3):
                    grid[cx + dx, cy + dy] += acc[dx][dy * CH:(dy + 1) * CH]
        return 0

    lax.fori_loop(0, longest, column, 0)


def sides_kernel(last, at, feat_h, pos_h, home_h, nbr_h, deg_h, lift_h, first_h, bias_h, second_h,
                 grid, low, high, data, rankb, taps, quad, lift_t, span_a, span_b,
                 pos, home, nbr, deg, lift, first, bias, second, mess, keys, sems):
    pairs = [(home_h, home), (pos_h, pos), (nbr_h, nbr), (deg_h, deg),
             (feat_h, data.at[0:64]), (lift_h, lift), (first_h, first), (bias_h, bias),
             (second_h, second)]
    copies = [pltpu.make_async_copy(a, b, sems.at[i]) for i, (a, b) in enumerate(pairs)]
    for c in copies:
        c.start()
    grid[...] = jnp.zeros_like(grid)
    tri = jnp.where(
        lax.broadcasted_iota(jnp.int32, (CHUNK, CHUNK), 0)
        < lax.broadcasted_iota(jnp.int32, (CHUNK, CHUNK), 1), 1.0, 0.0).astype(BF16)
    copies[0].wait()
    hx = home[0:1, :]
    hy = home[1:2, :]
    hz = home[2:3, :]
    col = column_rank(hx, hy)

    def blocks(limit, least):
        n = jnp.sum(jnp.where(col < limit, 1.0, 0.0)).astype(jnp.int32)
        return jnp.maximum((n + CHUNK - 1) // CHUNK, least)

    split = blocks(SIDE, FIRST)
    later = jnp.maximum(blocks(BOTH, SECOND), split)
    span_a[0] = split
    span_a[1] = later
    span_b[0] = later
    span_b[1] = PTS // CHUNK

    ids = lax.broadcasted_iota(jnp.int32, (CX * CY, PTS), 0)
    carry = jnp.sum(jnp.where(col < ids, 1.0, 0.0), axis=1, keepdims=True)
    for blk in range(PTS // CHUNK):
        part = slice(blk * CHUNK, (blk + 1) * CHUNK)
        hot = jnp.where(col[:, part] == ids[:, part], 1.0, 0.0)
        ahead = mm(hot.astype(BF16), tri) + carry
        rank = jnp.sum(hot * ahead, axis=0, keepdims=True)
        rank = jnp.transpose(jnp.broadcast_to(rank, (8, CHUNK)))
        rankb[part, :] = jnp.broadcast_to(rank[:, 0:1], (CHUNK, 128)).astype(jnp.int32)
        carry = carry + jnp.sum(hot, axis=1, keepdims=True)

    for c in copies[1:]:
        c.wait()
    slot = lax.broadcasted_iota(jnp.int32, (16, PTS), 0)
    bits = jnp.sum(
        jnp.where(slot < deg[...], jnp.left_shift(1, nbr[...]), 0), axis=0, keepdims=True)
    code = lax.broadcasted_iota(jnp.int32, (32, PTS), 0)
    live = jnp.bitwise_and(jnp.right_shift(bits, code), 1).astype(F32)
    off_x = (hx + at[0] * CX).astype(F32) + 0.5 - pos[0:1, :]
    off_y = (hy + at[1] * CY).astype(F32) + 0.5 - pos[1:2, :]
    off_z = hz.astype(F32) + 0.5 - pos[2:3, :]
    rows = [*pieces(off_x), *pieces(off_y), *pieces(off_z), hz.astype(F32), col.astype(F32),
            jnp.zeros((5, PTS), F32)]
    data[64:80, :] = jnp.concatenate(rows, axis=0).astype(BF16)
    data[80:112, :] = live.astype(BF16)

    flat = jnp.concatenate([first[...], bias[...], jnp.zeros((4, CH), F32)], axis=0)
    flat = jnp.concatenate([flat, jnp.zeros((8, 128 - CH), F32)], axis=1)
    flat = jnp.transpose(flat)
    for j in range(4):
        taps[j] = jnp.broadcast_to(flat[0:CH, j:j + 1], (CH, LARGE))
    zero = jnp.zeros((CH, CH), F32)
    sec_t = jnp.transpose(0.5 * second[...].astype(F32))
    quad[...] = jnp.concatenate(
        [jnp.concatenate([sec_t if i == j else zero for j in range(4)], axis=1)
         for i in range(4)], axis=0).astype(BF16)
    lift_t[...] = jnp.transpose(lift[...].astype(F32)).astype(BF16)

    def chunk(size, first, step, _):
        add_chunk(last, at, first + step * size, size, 0, data, rankb, taps, quad, lift_t, mess,
                  keys, grid)
        return 0

    large = split // 2
    lax.fori_loop(0, large, functools.partial(chunk, LARGE, 0), 0)
    lax.fori_loop(0, split - 2 * large, functools.partial(chunk, CHUNK, large * LARGE), 0)
    for y in range(CY + 2):
        low[y] = pack(grid[0, y])
        high[y] = pack(grid[CX + 1, y])


def middle_kernel(last, at, span, data, rankb, taps, quad, lift_t, *refs):
    *halo, grid, mess, keys = refs
    if halo:
        sides, middle, below, above = halo
        low = at[0] == 0
        top = at[0] * CX + CX - 1 == last[0]
        for x in range(CX):
            for y in range(1, CY + 1):
                l = sides[x + 1, y] + middle[x, y]
                if x == 0:
                    l = l + jnp.where(low, sides[0, y], unpack(below[y]))
                if x == CX - 1:
                    l = l + jnp.where(top, sides[CX + 1, y], unpack(above[y]))
                grid[x, y] = l
    else:
        grid[...] = jnp.zeros_like(grid)

    def chunk(size, first, step, _):
        add_chunk(last, at, first + step * size, size, 1, data, rankb, taps, quad, lift_t, mess,
                  keys, grid)
        return 0

    split = span[0]
    odd = jnp.bitwise_and(span[1] - split, 1)
    large = (span[1] - split) // 2
    lax.fori_loop(0, odd, functools.partial(chunk, CHUNK, split * CHUNK), 0)
    lax.fori_loop(0, large, functools.partial(chunk, LARGE, (split + odd) * CHUNK), 0)


def lift_points(at, last, feat, pos, home, nbr, deg, lift, first, bias, second):
    vmem = pl.BlockSpec(memory_space=pltpu.VMEM)
    smem = pl.BlockSpec(memory_space=pltpu.SMEM)
    work = [
        pltpu.VMEM((LARGE // SUB, 9 * CH, 3 * SUB), BF16),
        pltpu.VMEM((3, LARGE, NZ), F32),
    ]
    inputs = tuple(
        pltpu.with_memory_space_constraint(x, pltpu.HBM)
        for x in (feat, pos, home, nbr, deg, lift, first, bias, second))
    grid, low, high, *prepared, span_a, span_b = pl.pallas_call(
        functools.partial(sides_kernel, last),
        out_shape=[
            shape(CX + 2, CY + 2, CH, NZ),
            shape(CY + 2, PACKED, 128),
            shape(CY + 2, PACKED, 128),
            jax.ShapeDtypeStruct((112, PTS), BF16),
            jax.ShapeDtypeStruct((PTS, 128), jnp.int32),
            shape(4, CH, LARGE),
            jax.ShapeDtypeStruct((4 * CH, 4 * CH), BF16),
            jax.ShapeDtypeStruct((CH, CH), BF16),
            jax.ShapeDtypeStruct((2,), jnp.int32),
            jax.ShapeDtypeStruct((2,), jnp.int32),
        ],
        in_specs=[smem] + [pl.BlockSpec(memory_space=pltpu.HBM)] * len(inputs),
        out_specs=[vmem] * 8 + [smem, smem],
        scratch_shapes=[pltpu.VMEM(x.shape, x.dtype) for x in inputs[1:]] + work
        + [pltpu.SemaphoreType.DMA((len(inputs),))],
        compiler_params=LIMIT,
        name="lift_sides",
    )(at, *inputs)
    return grid, low, high, prepared, span_a, span_b


def lift_inner(at, last, span, prepared, name, halo=()):
    vmem = pl.BlockSpec(memory_space=pltpu.VMEM)
    smem = pl.BlockSpec(memory_space=pltpu.SMEM)
    return pl.pallas_call(
        functools.partial(middle_kernel, last),
        out_shape=shape(CX, CY + 2, CH, NZ),
        in_specs=[smem, smem] + [vmem] * (5 + len(halo)),
        out_specs=vmem,
        scratch_shapes=[
            pltpu.VMEM((LARGE // SUB, 9 * CH, 3 * SUB), BF16),
            pltpu.VMEM((3, LARGE, NZ), F32),
        ],
        compiler_params=LIMIT,
        name=name,
    )(at, span, *prepared, *halo)


def ends_kernel(last, at, sides, middle, below, above, low_y, high_y):
    low = at[0] == 0
    top = at[0] == last
    for y, out in ((0, low_y), (CY + 1, high_y)):
        for x in range(CX):
            l = sides[x + 1, y] + middle[x, y]
            if x == 0:
                l = l + jnp.where(low, sides[0, y], unpack(below[y]))
            if x == CX - 1:
                l = l + jnp.where(top, sides[CX + 1, y], unpack(above[y]))
            out[x] = pack(l)


def z_modes(table, pair):
    lane = lax.broadcasted_iota(jnp.int32, (MODES, HALVES), 1)
    d = mm(table, pair, NT, HIGH)
    re, im = d[0:MODES], d[MODES:]
    return jnp.where(lane < CH, re, swap(im)), jnp.where(lane < CH, swap(re), im)


def latent_kernel(last, at, tabz, rest, low_y, high_y, left, right, spec, own):
    first_pen = at[1] == 0
    last_pen = at[1] == last
    table = tabz[...]
    for x in range(CX):
        for yp in range(CY // 2):
            i = x * CY + 2 * yp
            for j in range(2):
                y = 2 * yp + j + 1
                l = rest[x, y]
                if y == 1:
                    l = l + unpack(jnp.where(first_pen, low_y[x], left[x]))
                if y == CY:
                    l = l + unpack(jnp.where(last_pen, high_y[x], right[x]))
                own[i + j] = l
            u, v = z_modes(table, own[i:i + 2].reshape(2 * CH, NZ))
            spec[:, i, :] = u
            spec[:, i + 1, :] = v


def y_kernel(r, main, out):
    sgn = sign_row((MODES, HALVES))
    pens = r.shape[0]
    for i in range(2 * CX):
        rows = r[:, i * CY:(i + 1) * CY, :].reshape(pens * CY, HALVES)
        ab = mm(main[...], rows, NN, HIGH)
        out[:, i, :] = ab[:MODES] + swap(ab[MODES:]) * sgn


def x_kernel(r, fwd, inv, w, out, lhs, res):
    rows = r.shape[0] * r.shape[1]
    modes = 2 * MODES
    sgn = sign_row((modes, HALVES))
    ab = mm(fwd[...], r[...].reshape(rows, HALVES), NN, HIGH)
    x = ab[:modes] + swap(ab[modes:]) * sgn
    parts = [*pieces(x), *pieces(swap(x))]
    lhs[...] = jnp.zeros_like(lhs)
    for j, p in enumerate(parts):
        lhs[:, j, :] = p
    for k in range(2):
        for j in range(MODES):
            m = k * MODES + j
            res[m] = mm(lhs[m][:, 0:CH].astype(BF16), w[j, 0, k])
    re = res[:, 0, :] + res[:, 1, :] + res[:, 2, :]
    im = res[:, 3, :] + res[:, 4, :] + res[:, 5, :]
    mixed = re - swap(im) * sgn
    ab = mm(inv[...], mixed, NN, HIGH)
    a, b = ab[:rows], ab[rows:]
    y = a - swap(b) * sign_row((rows, HALVES))
    out[...] = y.reshape(out.shape)


def y_back_kernel(r, inv, out):
    rows = inv.shape[0] // 2
    sgn = sign_row((rows, HALVES))
    for i in range(2 * CX):
        ab = mm(inv[...], r[:, i, :], NN, HIGH)
        y = ab[:rows] - swap(ab[rows:]) * sgn
        out[:, i * CY:(i + 1) * CY, :] = y.reshape(rows // CY, CY, HALVES)


def final_kernel(zb, tab, own, skip, bias, out, rows, sems):
    lane = lax.broadcasted_iota(jnp.int32, (MODES, HALVES), 1)
    zero = jnp.zeros((CH, CH), F32)
    skip_t = jnp.transpose(skip[...])
    pair = jnp.concatenate(
        [jnp.concatenate([skip_t, zero], axis=1), jnp.concatenate([zero, skip_t], axis=1)], axis=0)
    col = jnp.concatenate([bias[...], bias[...]], axis=1)
    col = jnp.transpose(jnp.broadcast_to(col, (8, HALVES)))
    col = jnp.broadcast_to(col[:, 0:1], (HALVES, NZ))
    copies = []
    for x in range(CX):
        for yp in range(CY // 2):
            i = x * CY + 2 * yp
            u = zb[:, i, :]
            v = zb[:, i + 1, :]
            s = jnp.concatenate(
                [jnp.where(lane < CH, u, swap(v)), jnp.where(lane < CH, swap(u), v)], axis=0)
            lat = own[i:i + 2].reshape(2 * CH, NZ)
            left = jnp.concatenate([jnp.transpose(s), pair], axis=1)
            total = mm(left, jnp.concatenate([tab[...], lat], axis=0), NN, HIGH) + col
            rows[x, 2 * yp:2 * yp + 2] = gelu(total).astype(BF16).reshape(2, CH, NZ)
        copies.append(pltpu.make_async_copy(rows.at[x], out.at[x], sems.at[x]))
        copies[-1].start()
    for c in copies:
        c.wait()


def finish(zb, own, skip, bias):
    cells = jax.ShapeDtypeStruct((CX, CY, CH, NZ), BF16)
    return pl.pallas_call(
        final_kernel,
        out_shape=cells,
        in_specs=[pl.BlockSpec(memory_space=pltpu.VMEM)] * 5,
        out_specs=pl.BlockSpec(memory_space=pltpu.HBM),
        scratch_shapes=[pltpu.VMEM(cells.shape, BF16), pltpu.SemaphoreType.DMA((CX,))],
        compiler_params=LIMIT,
        name="finish",
    )(zb, jnp.asarray(z_inverse_table()), own, skip, bias)


def call(kernel, shapes, args, scratch=(), smem=False, name=None):
    specs = [pl.BlockSpec(memory_space=pltpu.VMEM)] * len(args)
    if smem:
        specs[0] = pl.BlockSpec(memory_space=pltpu.SMEM)
    return pl.pallas_call(
        kernel,
        out_shape=shapes,
        in_specs=specs,
        scratch_shapes=list(scratch),
        compiler_params=LIMIT,
        name=name,
    )(*args)


def shape(*dims):
    return jax.ShapeDtypeStruct(dims, F32)


def exchange(x, axis):
    return lax.all_to_all(x, axis, split_axis=0, concat_axis=0, tiled=True)


def moved(x, axis, step):
    devices = range(lax.axis_size(axis))
    return lax.ppermute(x, axis, [(i - step, i) for i in devices if i - step in devices])


def per_device(features, positions, home_cells, neighbours, degrees, lift_input, kernel_first,
               kernel_bias, kernel_second, spectral_weights, skip_weights, skip_bias):
    bins = lax.axis_size("bin")
    pens = lax.axis_size("pen")
    at = jnp.stack([lax.axis_index("bin"), lax.axis_index("pen")]).astype(jnp.int32)
    last = (bins * CX - 1, pens * CY - 1)
    sides, low, high, prepared, span_a, span_b = lift_points(
        at, last, features.T, positions, home_cells, neighbours.T,
        degrees[None, :], lift_input, kernel_first, kernel_bias[None, :], kernel_second)
    below = moved(high, "bin", 1)
    above = moved(low, "bin", -1)
    middle = lift_inner(at, last, span_a, prepared, "lift_ends")
    half = shape(CX, PACKED, 128)
    low_y, high_y = call(
        functools.partial(ends_kernel, bins - 1), [half, half],
        (at, sides, middle, below, above), smem=True, name="y_ends")
    left = moved(high_y, "pen", 1)
    right = moved(low_y, "pen", -1)
    rest = lift_inner(at, last, span_b, prepared, "lift_core", (sides, middle, below, above))
    spec, own = call(
        functools.partial(latent_kernel, pens - 1),
        [shape(MODES, CX * CY, HALVES), shape(CX * CY, CH, NZ)],
        (at, jnp.asarray(z_forward_table()), rest, low_y, high_y, left, right),
        smem=True, name="latent_z")
    r = exchange(spec.reshape(pens, 2 * CX * CY, HALVES), "pen")
    r = call(y_kernel, shape(MODES, 2 * CX, HALVES), (r, jnp.asarray(y_forward_table(pens))),
             name="forward_y")
    r = exchange(r, "bin")
    fwd, inv = x_tables(bins)
    r = call(x_kernel, shape(MODES, 2 * CX, HALVES),
             (r, jnp.asarray(fwd), jnp.asarray(inv), spectral_weights),
             scratch=[pltpu.VMEM((2 * MODES, 8, HALVES), F32)] * 2, name="mix_x")
    r = exchange(r, "bin")
    r = call(y_back_kernel, shape(pens, 2 * CX * CY, HALVES),
             (r, jnp.asarray(y_inverse_table(pens))), name="inverse_y")
    r = exchange(r, "pen")
    out = finish(r.reshape(MODES, CX * CY, HALVES), own, skip_weights, skip_bias[None, :])
    return out.transpose(0, 1, 3, 2)


def solution(mesh):
    in_specs = (
        P(("bin", "pen"), None),
        P(None, ("bin", "pen")),
        P(None, ("bin", "pen")),
        P(("bin", "pen"), None),
        P(("bin", "pen")),
        P(),
        P(),
        P(),
        P(),
        P(None, "bin", "pen", None, None),
        P(),
        P(),
    )
    out_specs = P("bin", "pen", None, None)
    return jax.shard_map(
        per_device, mesh=mesh, in_specs=in_specs, out_specs=out_specs, check_vma=False
    )
```

```python
import functools
import math

import jax
import jax.numpy as jnp
import numpy as np
from jax import lax
from jax.experimental import pallas as pl
from jax.experimental.pallas import tpu as pltpu
from jax.sharding import PartitionSpec as P

NZ = 192
CX = 4
CY = 8
PTS = 2048
CH = 64
MODES = 32
CHUNK = 256
SUB = 128
LARGE = 512
FIRST = 5
SECOND = 7
HALVES = 2 * CH

F32 = jnp.float32
BF16 = jnp.bfloat16
HIGH = lax.Precision.HIGH
LIMIT = pltpu.CompilerParams(vmem_limit_bytes=24 * 1024 * 1024)

NN = (((1,), (0,)), ((), ()))
NT = (((1,), (1,)), ((), ()))
TN = (((0,), (0,)), ((), ()))


def mm(a, b, dims=NN, precision=None):
    return lax.dot_general(a, b, dims, precision=precision, preferred_element_type=F32)


def gelu(x):
    inner = x * (0.7978845608028654 + 0.035677408136300125 * (x * x))
    half = 0.5 * x
    return half + half * jnp.tanh(inner)


def twice_gelu(x):
    return x + x * jnp.tanh(x * (0.7978845608028654 + 0.035677408136300125 * (x * x)))


def swap(x):
    return pltpu.roll(x, CH, 1)


def sign_row(shape):
    lane = lax.broadcasted_iota(jnp.int32, shape, 1)
    return jnp.where(lane < CH, 1.0, -1.0).astype(F32)


def tables(length, signed):
    mode = np.arange(MODES)
    if signed:
        mode = np.where(mode < MODES // 2, mode, mode - MODES)
    return mode


def angles(rows, length, signed):
    mode = tables(length, signed)
    phase = (np.asarray(rows)[:, None] * mode[None, :]) % length
    angle = phase * (2.0 * math.pi / length)
    scale = 1.0 / math.sqrt(length)
    return np.cos(angle) * scale, np.sin(angle) * scale


def z_forward_table():
    c, s = angles(np.arange(NZ), NZ, False)
    return np.concatenate([c.T, -s.T], axis=0).astype(np.float32)


def z_inverse_table():
    c, s = angles(np.arange(NZ), NZ, False)
    w = np.where(np.arange(MODES) == 0, 1.0, 2.0)[:, None]
    return np.concatenate([c.T * w, -s.T * w], axis=0).astype(np.float32)


def y_forward_table(pens):
    length = CY * pens
    c, s = angles(np.arange(length), length, True)
    return np.concatenate([c.T, s.T], axis=0).astype(np.float32)


def y_inverse_table(pens):
    length = CY * pens
    c, s = angles(np.arange(length), length, True)
    return np.concatenate([c, s], axis=0).astype(np.float32)


def x_tables(bins):
    length = CX * bins
    c, s = angles(np.arange(length), length, True)
    fwd = np.zeros((2, 2, MODES, bins, 2, CX))
    inv = np.zeros((2, bins, 2, CX, 2, MODES))
    for k in range(2):
        fwd[0, k, :, :, k, :] = c.T.reshape(MODES, bins, CX)
        fwd[1, k, :, :, k, :] = s.T.reshape(MODES, bins, CX)
        inv[0, :, k, :, k, :] = c.reshape(bins, CX, MODES)
        inv[1, :, k, :, k, :] = s.reshape(bins, CX, MODES)
    fwd = fwd.reshape(4 * MODES, bins * 2 * CX)
    inv = inv.reshape(2 * bins * 2 * CX, 2 * MODES)
    return fwd.astype(np.float32), inv.astype(np.float32)


def pack(cells):
    tail = cells[:, 128:NZ]
    half = CH // 2
    return jnp.concatenate(
        [cells[:, 0:128], jnp.concatenate([tail[0:half], tail[half:CH]], axis=1)], axis=0)


def unpack(rows):
    tail = rows[CH:]
    tail = jnp.concatenate([tail[:, 0:NZ - 128], tail[:, NZ - 128:]], axis=0)
    return jnp.concatenate([rows[0:CH], tail], axis=1)


def pieces(x):
    hi = x.astype(BF16).astype(F32)
    rest = x - hi
    mid = rest.astype(BF16).astype(F32)
    return hi, mid, rest - mid


PACKED = CH * NZ // 128
SIDE = 2 * CY
BOTH = SIDE + 4


def column_rank(hx, hy):
    side = jnp.where(hx == 0, 0, CY) + hy
    end = SIDE + (hx - 1) * 2 + jnp.where(hy == 0, 0, 1)
    core = BOTH + (hx - 1) * (CY - 2) + hy - 1
    inner = jnp.where((hy == 0) | (hy == CY - 1), end, core)
    return jnp.where((hx == 0) | (hx == CX - 1), side, inner)


def column_x(o):
    inner = jnp.where(o < BOTH, jnp.where(o < SIDE + 2, 1, 2), jnp.where(o < BOTH + CY - 2, 1, 2))
    return jnp.where(o < CY, 0, jnp.where(o < SIDE, CX - 1, inner))


def column_y(o):
    side = jnp.where(o < CY, o, o - CY)
    end = jnp.where((o == SIDE) | (o == SIDE + 2), 0, CY - 1)
    core = jnp.where(o < BOTH + CY - 2, o - BOTH, o - (BOTH + CY - 2)) + 1
    return jnp.where(o < SIDE, side, jnp.where(o < BOTH, end, core))


def add_chunk(last, at, base, size, plane0, data, rankb, taps, quad, lift_t, mess, keys, grid):
    lanes = lax.broadcasted_iota(jnp.int32, (PTS, 128), 1) + base
    perm = jnp.concatenate(
        [jnp.where(rankb[...] == lanes + j * 128, 1.0, 0.0).astype(BF16)
         for j in range(size // 128)], axis=1)
    t = mm(data[...], perm)
    hzs = t[73:74]
    cols = t[74:75]
    spans = [(jnp.min(cols[:, j * SUB:(j + 1) * SUB]).astype(jnp.int32),
              jnp.max(cols[:, j * SUB:(j + 1) * SUB]).astype(jnp.int32) + 1)
             for j in range(size // SUB)]
    key = 256.0 * cols
    key = jnp.concatenate(
        [key + jnp.maximum(hzs - 1.0, 0.0), key + hzs, key + jnp.minimum(hzs + 1.0, NZ - 1.0),
         jnp.zeros((5, size), F32)], axis=0)
    key = jnp.transpose(key)
    for dz in range(3):
        keys[dz, 0:size] = jnp.broadcast_to(key[:, dz:dz + 1], (size, NZ))

    values = mm(lift_t[...], t[0:64].astype(BF16))
    ox = t[64:65] + t[65:66] + t[66:67]
    oy = t[67:68] + t[68:69] + t[69:70]
    oz = t[70:71] + t[71:72] + t[72:73]
    coli = cols.astype(jnp.int32)
    gx = column_x(coli) + at[0] * CX
    gy = column_y(coli) + at[1] * CY
    k_x, k_y, k_z, k_b = (taps[j, :, 0:size] for j in range(4))

    def ends(g, end):
        return (jnp.where(g > 0, -1.0, 0.0), None, jnp.where(g < end, 1.0, 0.0))

    base_pre = k_x * ox + k_y * oy + k_z * oz + k_b
    ex = ends(gx, last[0])
    ey = ends(gy, last[1])
    ez = ends(hzs, NZ - 1.0)
    pend = []

    def flush():
        while len(pend) < 4:
            pend.append((None, jnp.zeros((CH, size), BF16)))
        kern = mm(quad[...], jnp.concatenate([h for _, h in pend], axis=0))
        for j, (where, _) in enumerate(pend):
            if where is None:
                continue
            dx, dy, dz = where
            k = dx * 9 + dy * 3 + dz
            m = kern[j * CH:(j + 1) * CH] * (values * t[80 + k:81 + k])
            hi = m.astype(BF16)
            r = (dx * 3 + dy) * CH
            for s in range(size // SUB):
                cut = slice(s * SUB, (s + 1) * SUB)
                mess[s, r:r + CH, dz * SUB:(dz + 1) * SUB] = hi[:, cut]
        pend.clear()

    for dx in range(3):
        pre_x = base_pre if ex[dx] is None else base_pre + ex[dx] * k_x
        for dy in range(3):
            pre_y = pre_x if ey[dy] is None else pre_x + ey[dy] * k_y
            for dz in range(3):
                pre = pre_y if ez[dz] is None else pre_y + ez[dz] * k_z
                pend.append(((dx, dy, dz), twice_gelu(pre).astype(BF16)))
                if len(pend) == 4:
                    flush()
    flush()

    lane = lax.broadcasted_iota(jnp.int32, (SUB, NZ), 1).astype(F32)
    longest = spans[0][1] - spans[0][0]
    for begin, end in spans[1:]:
        longest = jnp.maximum(longest, end - begin)

    def column(j, _):
        results = []
        for s, (begin, end) in enumerate(spans):
            c = jnp.minimum(begin + j, end - 1)
            goal = lane + jnp.where(begin + j < end, 256.0 * c.astype(F32), -1.0e6)
            hot = jnp.concatenate(
                [jnp.where(keys[dz, s * SUB:(s + 1) * SUB] == goal, 1.0, 0.0).astype(BF16)
                 for dz in range(3)], axis=0)
            results.append((c, [mm(mess[s, q * 3 * CH:(q + 1) * 3 * CH], hot) for q in range(3)]))
        for c, acc in results:
            cx = column_x(c) - plane0
            cy = column_y(c)
            for dx in range(3):
                for dy in range(3):
                    grid[cx + dx, cy + dy] += acc[dx][dy * CH:(dy + 1) * CH]
        return 0

    lax.fori_loop(0, longest, column, 0)


def sides_kernel(last, at, feat_h, pos_h, home_h, nbr_h, deg_h, lift_h, first_h, bias_h, second_h,
                 grid, low, high, data, rankb, taps, quad, lift_t, span_a, span_b,
                 pos, home, nbr, deg, lift, first, bias, second, mess, keys, sems):
    pairs = [(home_h, home), (pos_h, pos), (nbr_h, nbr), (deg_h, deg),
             (feat_h, data.at[0:64]), (lift_h, lift), (first_h, first), (bias_h, bias),
             (second_h, second)]
    copies = [pltpu.make_async_copy(a, b, sems.at[i]) for i, (a, b) in enumerate(pairs)]
    for c in copies:
        c.start()
    grid[...] = jnp.zeros_like(grid)
    tri = jnp.where(
        lax.broadcasted_iota(jnp.int32, (CHUNK, CHUNK), 0)
        < lax.broadcasted_iota(jnp.int32, (CHUNK, CHUNK), 1), 1.0, 0.0).astype(BF16)
    copies[0].wait()
    hx = home[0:1, :]
    hy = home[1:2, :]
    hz = home[2:3, :]
    col = column_rank(hx, hy)

    def blocks(limit, least):
        n = jnp.sum(jnp.where(col < limit, 1.0, 0.0)).astype(jnp.int32)
        return jnp.maximum((n + CHUNK - 1) // CHUNK, least)

    split = blocks(SIDE, FIRST)
    later = jnp.maximum(blocks(BOTH, SECOND), split)
    span_a[0] = split
    span_a[1] = later
    span_b[0] = later
    span_b[1] = PTS // CHUNK

    ids = lax.broadcasted_iota(jnp.int32, (CX * CY, PTS), 0)
    carry = jnp.sum(jnp.where(col < ids, 1.0, 0.0), axis=1, keepdims=True)
    for blk in range(PTS // CHUNK):
        part = slice(blk * CHUNK, (blk + 1) * CHUNK)
        hot = jnp.where(col[:, part] == ids[:, part], 1.0, 0.0)
        ahead = mm(hot.astype(BF16), tri) + carry
        rank = jnp.sum(hot * ahead, axis=0, keepdims=True)
        rank = jnp.transpose(jnp.broadcast_to(rank, (8, CHUNK)))
        rankb[part, :] = jnp.broadcast_to(rank[:, 0:1], (CHUNK, 128)).astype(jnp.int32)
        carry = carry + jnp.sum(hot, axis=1, keepdims=True)

    for c in copies[1:]:
        c.wait()
    slot = lax.broadcasted_iota(jnp.int32, (16, PTS), 0)
    bits = jnp.sum(
        jnp.where(slot < deg[...], jnp.left_shift(1, nbr[...]), 0), axis=0, keepdims=True)
    code = lax.broadcasted_iota(jnp.int32, (32, PTS), 0)
    live = jnp.bitwise_and(jnp.right_shift(bits, code), 1).astype(F32)
    off_x = (hx + at[0] * CX).astype(F32) + 0.5 - pos[0:1, :]
    off_y = (hy + at[1] * CY).astype(F32) + 0.5 - pos[1:2, :]
    off_z = hz.astype(F32) + 0.5 - pos[2:3, :]
    rows = [*pieces(off_x), *pieces(off_y), *pieces(off_z), hz.astype(F32), col.astype(F32),
            jnp.zeros((5, PTS), F32)]
    data[64:80, :] = jnp.concatenate(rows, axis=0).astype(BF16)
    data[80:112, :] = live.astype(BF16)

    flat = jnp.concatenate([first[...], bias[...], jnp.zeros((4, CH), F32)], axis=0)
    flat = jnp.concatenate([flat, jnp.zeros((8, 128 - CH), F32)], axis=1)
    flat = jnp.transpose(flat)
    for j in range(4):
        taps[j] = jnp.broadcast_to(flat[0:CH, j:j + 1], (CH, LARGE))
    zero = jnp.zeros((CH, CH), F32)
    sec_t = jnp.transpose(0.5 * second[...].astype(F32))
    quad[...] = jnp.concatenate(
        [jnp.concatenate([sec_t if i == j else zero for j in range(4)], axis=1)
         for i in range(4)], axis=0).astype(BF16)
    lift_t[...] = jnp.transpose(lift[...].astype(F32)).astype(BF16)

    def chunk(size, first, step, _):
        add_chunk(last, at, first + step * size, size, 0, data, rankb, taps, quad, lift_t, mess,
                  keys, grid)
        return 0

    large = split // 2
    lax.fori_loop(0, large, functools.partial(chunk, LARGE, 0), 0)
    lax.fori_loop(0, split - 2 * large, functools.partial(chunk, CHUNK, large * LARGE), 0)
    for y in range(CY + 2):
        low[y] = pack(grid[0, y])
        high[y] = pack(grid[CX + 1, y])


def middle_kernel(last, at, span, data, rankb, taps, quad, lift_t, *refs):
    *halo, grid, mess, keys = refs
    if halo:
        sides, middle, below, above = halo
        low = at[0] == 0
        top = at[0] * CX + CX - 1 == last[0]
        for x in range(CX):
            for y in range(1, CY + 1):
                l = sides[x + 1, y] + middle[x, y]
                if x == 0:
                    l = l + jnp.where(low, sides[0, y], unpack(below[y]))
                if x == CX - 1:
                    l = l + jnp.where(top, sides[CX + 1, y], unpack(above[y]))
                grid[x, y] = l
    else:
        grid[...] = jnp.zeros_like(grid)

    def chunk(size, first, step, _):
        add_chunk(last, at, first + step * size, size, 1, data, rankb, taps, quad, lift_t, mess,
                  keys, grid)
        return 0

    split = span[0]
    odd = jnp.bitwise_and(span[1] - split, 1)
    large = (span[1] - split) // 2
    lax.fori_loop(0, odd, functools.partial(chunk, CHUNK, split * CHUNK), 0)
    lax.fori_loop(0, large, functools.partial(chunk, LARGE, (split + odd) * CHUNK), 0)


def lift_points(at, last, feat, pos, home, nbr, deg, lift, first, bias, second):
    vmem = pl.BlockSpec(memory_space=pltpu.VMEM)
    smem = pl.BlockSpec(memory_space=pltpu.SMEM)
    work = [
        pltpu.VMEM((LARGE // SUB, 9 * CH, 3 * SUB), BF16),
        pltpu.VMEM((3, LARGE, NZ), F32),
    ]
    inputs = tuple(
        pltpu.with_memory_space_constraint(x, pltpu.HBM)
        for x in (feat, pos, home, nbr, deg, lift, first, bias, second))
    grid, low, high, *prepared, span_a, span_b = pl.pallas_call(
        functools.partial(sides_kernel, last),
        out_shape=[
            shape(CX + 2, CY + 2, CH, NZ),
            shape(CY + 2, PACKED, 128),
            shape(CY + 2, PACKED, 128),
            jax.ShapeDtypeStruct((112, PTS), BF16),
            jax.ShapeDtypeStruct((PTS, 128), jnp.int32),
            shape(4, CH, LARGE),
            jax.ShapeDtypeStruct((4 * CH, 4 * CH), BF16),
            jax.ShapeDtypeStruct((CH, CH), BF16),
            jax.ShapeDtypeStruct((2,), jnp.int32),
            jax.ShapeDtypeStruct((2,), jnp.int32),
        ],
        in_specs=[smem] + [pl.BlockSpec(memory_space=pltpu.HBM)] * len(inputs),
        out_specs=[vmem] * 8 + [smem, smem],
        scratch_shapes=[pltpu.VMEM(x.shape, x.dtype) for x in inputs[1:]] + work
        + [pltpu.SemaphoreType.DMA((len(inputs),))],
        compiler_params=LIMIT,
        name="lift_sides",
    )(at, *inputs)
    return grid, low, high, prepared, span_a, span_b


def lift_inner(at, last, span, prepared, name, halo=()):
    vmem = pl.BlockSpec(memory_space=pltpu.VMEM)
    smem = pl.BlockSpec(memory_space=pltpu.SMEM)
    return pl.pallas_call(
        functools.partial(middle_kernel, last),
        out_shape=shape(CX, CY + 2, CH, NZ),
        in_specs=[smem, smem] + [vmem] * (5 + len(halo)),
        out_specs=vmem,
        scratch_shapes=[
            pltpu.VMEM((LARGE // SUB, 9 * CH, 3 * SUB), BF16),
            pltpu.VMEM((3, LARGE, NZ), F32),
        ],
        compiler_params=LIMIT,
        name=name,
    )(at, span, *prepared, *halo)


def ends_kernel(last, at, sides, middle, below, above, low_y, high_y):
    low = at[0] == 0
    top = at[0] == last
    for y, out in ((0, low_y), (CY + 1, high_y)):
        for x in range(CX):
            l = sides[x + 1, y] + middle[x, y]
            if x == 0:
                l = l + jnp.where(low, sides[0, y], unpack(below[y]))
            if x == CX - 1:
                l = l + jnp.where(top, sides[CX + 1, y], unpack(above[y]))
            out[x] = pack(l)


def z_modes(d):
    lane = lax.broadcasted_iota(jnp.int32, (MODES, HALVES), 1)
    re, im = d[0:MODES], d[MODES:]
    return jnp.where(lane < CH, re, swap(im)), jnp.where(lane < CH, swap(re), im)


def latent_kernel(last, at, tabz, rest, low_y, high_y, left, right, spec, own):
    first_pen = at[1] == 0
    last_pen = at[1] == last
    table = tabz[...]
    for x in range(CX):
        for yq in range(CY // 4):
            i = x * CY + 4 * yq
            for j in range(4):
                y = 4 * yq + j + 1
                l = rest[x, y]
                if y == 1:
                    l = l + unpack(jnp.where(first_pen, low_y[x], left[x]))
                if y == CY:
                    l = l + unpack(jnp.where(last_pen, high_y[x], right[x]))
                own[i + j] = l
            d = mm(table, own[i:i + 4].reshape(4 * CH, NZ), NT, HIGH)
            for j in (0, 2):
                u, v = z_modes(d[:, j * CH:(j + 2) * CH])
                spec[:, i + j, :] = u
                spec[:, i + j + 1, :] = v


def y_kernel(r, main, out):
    sgn = sign_row((MODES, HALVES))
    pens = r.shape[0]
    for i in range(2 * CX):
        rows = r[:, i * CY:(i + 1) * CY, :].reshape(pens * CY, HALVES)
        ab = mm(main[...], rows, NN, HIGH)
        out[:, i, :] = ab[:MODES] + swap(ab[MODES:]) * sgn


def x_kernel(r, fwd, inv, w, out, lhs, res):
    rows = r.shape[0] * r.shape[1]
    modes = 2 * MODES
    sgn = sign_row((modes, HALVES))
    ab = mm(fwd[...], r[...].reshape(rows, HALVES), NN, HIGH)
    x = ab[:modes] + swap(ab[modes:]) * sgn
    parts = [*pieces(x), *pieces(swap(x))]
    lhs[...] = jnp.zeros_like(lhs)
    for j, p in enumerate(parts):
        lhs[:, j, :] = p
    for k in range(2):
        for j in range(MODES):
            m = k * MODES + j
            res[m] = mm(lhs[m][:, 0:CH].astype(BF16), w[j, 0, k])
    re = res[:, 0, :] + res[:, 1, :] + res[:, 2, :]
    im = res[:, 3, :] + res[:, 4, :] + res[:, 5, :]
    mixed = re - swap(im) * sgn
    ab = mm(inv[...], mixed, NN, HIGH)
    a, b = ab[:rows], ab[rows:]
    y = a - swap(b) * sign_row((rows, HALVES))
    out[...] = y.reshape(out.shape)


def y_back_kernel(r, inv, out):
    rows = inv.shape[0] // 2
    sgn = sign_row((rows, HALVES))
    for i in range(2 * CX):
        ab = mm(inv[...], r[:, i, :], NN, HIGH)
        y = ab[:rows] - swap(ab[rows:]) * sgn
        out[:, i * CY:(i + 1) * CY, :] = y.reshape(rows // CY, CY, HALVES)


def final_kernel(zb, tab, own, skip, bias, out, rows, sems):
    lane = lax.broadcasted_iota(jnp.int32, (MODES, HALVES), 1)
    zero = jnp.zeros((CH, CH), F32)
    skip_t = jnp.transpose(skip[...])
    pair = jnp.concatenate(
        [jnp.concatenate([skip_t, zero], axis=1), jnp.concatenate([zero, skip_t], axis=1)], axis=0)
    col = jnp.concatenate([bias[...], bias[...]], axis=1)
    col = jnp.transpose(jnp.broadcast_to(col, (8, HALVES)))
    col = jnp.broadcast_to(col[:, 0:1], (HALVES, NZ))
    copies = []
    for x in range(CX):
        for yp in range(CY // 2):
            i = x * CY + 2 * yp
            u = zb[:, i, :]
            v = zb[:, i + 1, :]
            s = jnp.concatenate(
                [jnp.where(lane < CH, u, swap(v)), jnp.where(lane < CH, swap(u), v)], axis=0)
            lat = own[i:i + 2].reshape(2 * CH, NZ)
            left = jnp.concatenate([jnp.transpose(s), pair], axis=1)
            total = mm(left, jnp.concatenate([tab[...], lat], axis=0), NN, HIGH) + col
            rows[x, 2 * yp:2 * yp + 2] = gelu(total).astype(BF16).reshape(2, CH, NZ)
        copies.append(pltpu.make_async_copy(rows.at[x], out.at[x], sems.at[x]))
        copies[-1].start()
    for c in copies:
        c.wait()


def finish(zb, own, skip, bias):
    cells = jax.ShapeDtypeStruct((CX, CY, CH, NZ), BF16)
    return pl.pallas_call(
        final_kernel,
        out_shape=cells,
        in_specs=[pl.BlockSpec(memory_space=pltpu.VMEM)] * 5,
        out_specs=pl.BlockSpec(memory_space=pltpu.HBM),
        scratch_shapes=[pltpu.VMEM(cells.shape, BF16), pltpu.SemaphoreType.DMA((CX,))],
        compiler_params=LIMIT,
        name="finish",
    )(zb, jnp.asarray(z_inverse_table()), own, skip, bias)


def call(kernel, shapes, args, scratch=(), smem=False, name=None):
    specs = [pl.BlockSpec(memory_space=pltpu.VMEM)] * len(args)
    if smem:
        specs[0] = pl.BlockSpec(memory_space=pltpu.SMEM)
    return pl.pallas_call(
        kernel,
        out_shape=shapes,
        in_specs=specs,
        scratch_shapes=list(scratch),
        compiler_params=LIMIT,
        name=name,
    )(*args)


def shape(*dims):
    return jax.ShapeDtypeStruct(dims, F32)


def exchange(x, axis):
    return lax.all_to_all(x, axis, split_axis=0, concat_axis=0, tiled=True)


def moved(x, axis, step):
    devices = range(lax.axis_size(axis))
    return lax.ppermute(x, axis, [(i - step, i) for i in devices if i - step in devices])


def per_device(features, positions, home_cells, neighbours, degrees, lift_input, kernel_first,
               kernel_bias, kernel_second, spectral_weights, skip_weights, skip_bias):
    bins = lax.axis_size("bin")
    pens = lax.axis_size("pen")
    at = jnp.stack([lax.axis_index("bin"), lax.axis_index("pen")]).astype(jnp.int32)
    last = (bins * CX - 1, pens * CY - 1)
    sides, low, high, prepared, span_a, span_b = lift_points(
        at, last, features.T, positions, home_cells, neighbours.T,
        degrees[None, :], lift_input, kernel_first, kernel_bias[None, :], kernel_second)
    below = moved(high, "bin", 1)
    above = moved(low, "bin", -1)
    middle = lift_inner(at, last, span_a, prepared, "lift_ends")
    half = shape(CX, PACKED, 128)
    low_y, high_y = call(
        functools.partial(ends_kernel, bins - 1), [half, half],
        (at, sides, middle, below, above), smem=True, name="y_ends")
    left = moved(high_y, "pen", 1)
    right = moved(low_y, "pen", -1)
    rest = lift_inner(at, last, span_b, prepared, "lift_core", (sides, middle, below, above))
    spec, own = call(
        functools.partial(latent_kernel, pens - 1),
        [shape(MODES, CX * CY, HALVES), shape(CX * CY, CH, NZ)],
        (at, jnp.asarray(z_forward_table()), rest, low_y, high_y, left, right),
        smem=True, name="latent_z")
    r = exchange(spec.reshape(pens, 2 * CX * CY, HALVES), "pen")
    r = call(y_kernel, shape(MODES, 2 * CX, HALVES), (r, jnp.asarray(y_forward_table(pens))),
             name="forward_y")
    r = exchange(r, "bin")
    fwd, inv = x_tables(bins)
    r = call(x_kernel, shape(MODES, 2 * CX, HALVES),
             (r, jnp.asarray(fwd), jnp.asarray(inv), spectral_weights),
             scratch=[pltpu.VMEM((2 * MODES, 8, HALVES), F32)] * 2, name="mix_x")
    r = exchange(r, "bin")
    r = call(y_back_kernel, shape(pens, 2 * CX * CY, HALVES),
             (r, jnp.asarray(y_inverse_table(pens))), name="inverse_y")
    r = exchange(r, "pen")
    out = finish(r.reshape(MODES, CX * CY, HALVES), own, skip_weights, skip_bias[None, :])
    return out.transpose(0, 1, 3, 2)


def solution(mesh):
    in_specs = (
        P(("bin", "pen"), None),
        P(None, ("bin", "pen")),
        P(None, ("bin", "pen")),
        P(("bin", "pen"), None),
        P(("bin", "pen")),
        P(),
        P(),
        P(),
        P(),
        P(None, "bin", "pen", None, None),
        P(),
        P(),
    )
    out_specs = P("bin", "pen", None, None)
    return jax.shard_map(
        per_device, mesh=mesh, in_specs=in_specs, out_specs=out_specs, check_vma=False
    )
```
